32 devices in a mesh: rep: 4 (over y, x), fsdp: 8 (over z, core).
Axes of the slice: x: 2, y: 2, z: 4, core: 2. Of those that a mesh axis runs over, the one named last changes fastest.
Arguments:
- block_input: bfloat16 [32768, 768], P(('rep', 'fsdp')), may hold values from -6 to 6
- cotangent: bfloat16 [32768, 768], P(('rep', 'fsdp')), may hold values from -6 to 6
- lengths: int32 [32], P(('rep', 'fsdp')), may hold values from 128 to 1024, as said below
- first_gain: bfloat16 [768], P('fsdp'), may hold values from 0.5 to 1.5
- first_shift: bfloat16 [768], P('fsdp'), may hold values from -1.75 to 1.75
- second_gain: bfloat16 [768], P('fsdp'), may hold values from 0.5 to 1.5
- second_shift: bfloat16 [768], P('fsdp'), may hold values from -1.75 to 1.75
- triple_weight: bfloat16 [768, 2304], P('fsdp'), may hold values from -0.21875 to 0.21875
- triple_bias: bfloat16 [2304], P('fsdp'), may hold values from -3 to 3
- output_weight: bfloat16 [768, 768], P('fsdp'), may hold values from -1.75 to 1.75
- output_bias: bfloat16 [768], P('fsdp'), may hold values from -1.75 to 1.75
- upward_weight: bfloat16 [768, 3072], P('fsdp'), may hold values from -0.21875 to 0.21875
- upward_bias: bfloat16 [3072], P('fsdp'), may hold values from -3 to 3
- downward_weight: bfloat16 [3072, 768], P('fsdp'), may hold values from -0.109375 to 0.109375
- downward_bias: bfloat16 [768], P('fsdp'), may hold values from -1.75 to 1.75
Outputs:
- block_output: bfloat16 [32768, 768], P(('rep', 'fsdp'))
- input_grad: bfloat16 [32768, 768], P(('rep', 'fsdp'))
- first_gain_grad: float32 [768], P('fsdp')
- first_shift_grad: float32 [768], P('fsdp')
- second_gain_grad: float32 [768], P('fsdp')
- second_shift_grad: float32 [768], P('fsdp')
- triple_weight_grad: float32 [768, 2304], P('fsdp')
- triple_bias_grad: float32 [2304], P('fsdp')
- output_weight_grad: float32 [768, 768], P('fsdp')
- output_bias_grad: float32 [768], P('fsdp')
- upward_weight_grad: float32 [768, 3072], P('fsdp')
- upward_bias_grad: float32 [3072], P('fsdp')
- downward_weight_grad: float32 [3072, 768], P('fsdp')
- downward_bias_grad: float32 [768], P('fsdp')
- example_norms: float32 [32], replicated
The draws below stay inside these ranges and needn't reach their ends.
Inputs may be any that keep to these rules, and one draw needn't show every extreme that they name: `lengths`: A sequence's real tokens fill the front of its 1024 rows; in every draw one sequence has exactly 1024 real tokens and one exactly 128.
All inputs are finite; a program needn't handle non-finite values.
Results may differ from the reference program's by a relative error of at most 0.012.
Values may be sent and summed in bfloat16 or wider, within the bound.
No kernel may reach another device: no remote copies, remote signals or barrier semaphores. Data moves between devices by JAX's collectives and lax.ppermute only.
A program may use at most 192 MiB of HBM per device.

```python
import math
from functools import reduce
import jax
import jax.numpy as jnp
from jax import lax

D = 768
HEADS = 12
HEAD_DIM = 64
ROT = 16
FF = 3072
LEN = 1024
SEQS = 32
TOKENS = 32768


def draw_lengths(key, part):
    first, second = jax.random.split(key)
    spread = jax.random.randint(first, (SEQS,), 0, 64)
    shortest = LEN // 8
    drawn = shortest + spread * (spread + 126) * (LEN - shortest) // (63 * 189)
    order = jax.random.permutation(second, SEQS)
    drawn = drawn.at[order[0]].set(LEN).at[order[1]].set(shortest)
    return drawn.astype(jnp.int32)


def block_levels(stream_key, extent, shards, low, largest):
    loudness, own = 1.0, jax.random.fold_in(stream_key, 6)
    for axis_at, parts in shards:
        heights = jnp.exp(jax.random.uniform(jax.random.fold_in(own, axis_at), (parts,), jnp.float32, low / len(shards), largest / len(shards)))
        loudness = loudness * jnp.repeat(heights, extent[axis_at] // parts).reshape([-1 if axis == axis_at else 1 for axis in range(len(extent))])
    return loudness


def normal_values(own_key, dims, scale, limit, cuts=(), kind=jnp.bfloat16):
    entries = jax.random.normal(own_key, dims, jnp.float32) * scale
    if len(cuts) > 0:
        entries = block_levels(own_key, dims, cuts, -0.22, 0.18) * entries
    return jnp.clip(entries, min=-limit, max=limit).astype(kind)


def setup_inputs(seed: int = 0) -> dict:
    streams_of = jax.random.split(jax.random.key(seed), 16)
    block_input = normal_values(streams_of[0], (TOKENS, D), 1.0, 6.0, ((0, 32),))
    cotangent = normal_values(streams_of[1], (TOKENS, D), 1.0, 6.0, ((0, 32),))
    lengths = draw_lengths(jax.random.fold_in(streams_of[15], 71), 0)
    first_gain = jnp.clip(1.0 + 0.1 * jax.random.normal(streams_of[3], (D,), jnp.float32), 0.5, 1.5).astype(jnp.bfloat16)
    first_shift = normal_values(streams_of[4], (D,), 0.3, 1.75, ((0, 8),))
    second_gain = jnp.clip(1.0 + 0.1 * jax.random.normal(streams_of[5], (D,), jnp.float32), 0.5, 1.5).astype(jnp.bfloat16)
    second_shift = normal_values(streams_of[6], (D,), 0.3, 1.75, ((0, 8),))
    triple_weight = normal_values(streams_of[7], (D, 3 * D), D ** -0.5, 0.21875, ((0, 8),))
    triple_bias = normal_values(streams_of[8], (3 * D,), 0.5, 3.0, ((0, 8),))
    output_weight = normal_values(streams_of[9], (D, D), (D // 64) ** -0.5, 1.75, ((0, 8),))
    output_bias = normal_values(streams_of[10], (D,), 0.3, 1.75, ((0, 8),))
    upward_weight = normal_values(streams_of[11], (D, FF), D ** -0.5, 0.21875, ((0, 8),))
    upward_bias = normal_values(streams_of[12], (FF,), 0.5, 3.0, ((0, 8),))
    downward_weight = normal_values(streams_of[13], (FF, D), FF ** -0.5, 0.109375, ((0, 8),))
    downward_bias = normal_values(streams_of[14], (D,), 0.3, 1.75, ((0, 8),))
    return dict(block_input=block_input, cotangent=cotangent, lengths=lengths, first_gain=first_gain, first_shift=first_shift, second_gain=second_gain, second_shift=second_shift, triple_weight=triple_weight, triple_bias=triple_bias, output_weight=output_weight, output_bias=output_bias, upward_weight=upward_weight, upward_bias=upward_bias, downward_weight=downward_weight, downward_bias=downward_bias)


@jax.custom_vjp
def low(v):
    return lax.optimization_barrier(v.astype(jnp.bfloat16)).astype(jnp.float32)

@jax.custom_vjp
def low_back(v):
    return v

def low_keep(v):
    return (low(v), None)

def low_pass(kept, grad):
    return (grad,)

def back_keep(v):
    return (v, None)

def back_low(kept, grad):
    return (low(grad),)
low.defvjp(low_keep, low_pass)
low_back.defvjp(back_keep, back_low)
epsilon = 1e-05
masked_score = -1e+30
highest = lax.Precision.HIGHEST

def layer_norm(values, norm_gain, norm_shift):
    centred = values - lax.optimization_barrier(jnp.mean(values, axis=-1, keepdims=True))
    variance = lax.optimization_barrier(jnp.mean(centred * centred, axis=-1, keepdims=True))
    return centred * lax.rsqrt(variance + epsilon) * norm_gain + norm_shift

def rotary_tables(row_count):
    halfway = ROT // 2
    frequency = jnp.exp(jnp.arange(halfway, dtype=jnp.float32) * (-2.0 * math.log(10000.0) / ROT))
    angles = jnp.arange(row_count, dtype=jnp.float32)[:, None] * frequency[None, :]
    cosine_table = jnp.concatenate([jnp.cos(angles), jnp.cos(angles)], axis=1)[:, None, :]
    sine_table = jnp.concatenate([jnp.sin(angles), jnp.sin(angles)], axis=1)[:, None, :]
    return (cosine_table, sine_table)

def rotate(values, cosine_table, sine_table):
    halfway = ROT // 2
    leading = values[..., :ROT]
    turned = jnp.concatenate([-leading[..., halfway:], leading[..., :halfway]], axis=-1)
    return jnp.concatenate([leading * cosine_table + turned * sine_table, values[..., ROT:]], axis=-1)

def layer(params, source, seq_limit):
    gain_one, shift_one, gain_two, shift_two, weight_triple, bias_triple, weight_output, bias_output, weight_upward, bias_upward, weight_downward, bias_downward = params
    positions = jnp.arange(LEN)
    valid = (positions < seq_limit).astype(jnp.float32)[:, None]
    first_low = low(layer_norm(source, gain_one, shift_one))
    triple = low_back(jnp.dot(first_low, weight_triple, precision=highest) + bias_triple)
    triple_split = triple.reshape(LEN, 3, HEADS, HEAD_DIM)
    cosine_table, sine_table = rotary_tables(LEN)
    queries = low(rotate(triple_split[:, 0], cosine_table, sine_table))
    key_rows = low(rotate(triple_split[:, 1], cosine_table, sine_table))
    value_rows = low(triple_split[:, 2])
    scores = low_back(jnp.einsum('qhd,khd->hqk', queries, key_rows, precision=highest) * HEAD_DIM ** (-0.5))
    allowed = (positions[None, :] <= positions[:, None]) & (positions[None, :] < seq_limit)
    probs_low = low(jax.nn.softmax(jnp.where(allowed[None], scores, masked_score), axis=-1))
    context = low_back(low(jnp.einsum('hqk,khd->qhd', probs_low, value_rows, precision=highest).reshape(LEN, D)))
    attention_out = jnp.dot(context, weight_output, precision=highest) + bias_output
    second_low = low(layer_norm(source, gain_two, shift_two))
    upward = low_back(jnp.dot(second_low, weight_upward, precision=highest) + bias_upward)
    active = low(jax.nn.gelu(upward, approximate=False))
    mixer_out = jnp.dot(active, weight_downward, precision=highest) + bias_downward
    return (source + attention_out + mixer_out) * valid

def sequence_grads(params, source, cot_rows, seq_limit):
    output, pullback = jax.vjp(lambda weights, source_rows: layer(weights, source_rows, seq_limit), params, source)
    grad_params, grad_source = pullback(cot_rows)
    return (output, grad_params, grad_source)

def grad_norm(grad_params):
    return jnp.sqrt(reduce(lambda left, right: left + right, [jnp.sum(piece * piece) for piece in grad_params]))

def reference(block_input, cotangent, lengths, first_gain, first_shift, second_gain, second_shift, triple_weight, triple_bias, output_weight, output_bias, upward_weight, upward_bias, downward_weight, downward_bias):
    params = tuple((piece.astype(jnp.float32) for piece in (first_gain, first_shift, second_gain, second_shift, triple_weight, triple_bias, output_weight, output_bias, upward_weight, upward_bias, downward_weight, downward_bias)))
    sources = block_input.astype(jnp.float32).reshape(SEQS, LEN, D)
    cot_all = cotangent.astype(jnp.float32).reshape(SEQS, LEN, D)

    def first_pass(unused, pieces):
        source, cot_rows, seq_limit = pieces
        output, grad_params, grad_source = sequence_grads(params, source, cot_rows, seq_limit)
        return (unused, (output.astype(jnp.bfloat16), grad_source.astype(jnp.bfloat16), grad_norm(grad_params)))
    unused, (outputs, input_grads, norm_list) = lax.scan(first_pass, jnp.zeros((), jnp.float32), (sources, cot_all, lengths))
    mean_norm = jnp.mean(norm_list)

    def second_pass(running, pieces):
        source, cot_rows, seq_limit, own_norm = pieces
        grad_params = sequence_grads(params, source, cot_rows, seq_limit)[1]
        factor = jnp.minimum(1.0, mean_norm / own_norm) / SEQS
        return (tuple((previous + factor * piece for previous, piece in zip(running, grad_params))), None)
    totals = lax.scan(second_pass, tuple((jnp.zeros_like(piece) for piece in params)), (sources, cot_all, lengths, norm_list))[0]
    return (outputs.reshape(SEQS * LEN, D), input_grads.reshape(SEQS * LEN, D), totals[0], totals[1], totals[2], totals[3], totals[4], totals[5], totals[6], totals[7], totals[8], totals[9], totals[10], totals[11], norm_list)
```

```python
import math
import numpy as np
import jax
import jax.numpy as jnp
from jax import lax
from jax.experimental import pallas as pl
from jax.experimental.pallas import tpu as pltpu
from jax.sharding import PartitionSpec as P

HEADS = 12
HEAD_DIM = 64
ROT = 16
EPS = 1e-05
MASKED = -1e30
BF = jnp.bfloat16
F32 = jnp.float32
GROUPS = 3
VMEM_LIMIT = 60 * 1024 * 1024


def mm(a, b):
    return jnp.dot(a, b, preferred_element_type=F32)


def mm_rt(a, b):
    return lax.dot_general(a, b, (((1,), (1,)), ((), ())), preferred_element_type=F32)


def mm_lt(a, b):
    return lax.dot_general(a, b, (((0,), (0,)), ((), ())), preferred_element_type=F32)


def rotary_tables(rows, width):
    half = ROT // 2
    freq = np.exp(np.arange(half, dtype=np.float32) * np.float32(-2.0 * math.log(10000.0) / ROT))
    ang = np.arange(rows, dtype=np.float32)[:, None] * freq.astype(np.float32)[None, :]
    cos, sin = np.cos(ang), np.sin(ang)
    keep = np.ones((rows, HEAD_DIM), np.float32)
    up = np.zeros((rows, HEAD_DIM), np.float32)
    down = np.zeros((rows, HEAD_DIM), np.float32)
    keep[:, :half] = cos
    keep[:, half:ROT] = cos
    up[:, :half] = -sin
    down[:, half:ROT] = sin
    rep = width // HEAD_DIM
    return tuple(np.tile(t, (1, rep)).astype(np.float32) for t in (keep, up, down))


def norm_parts(values):
    centred = values - jnp.mean(values, axis=-1, keepdims=True)
    inverse = lax.rsqrt(jnp.mean(centred * centred, axis=-1, keepdims=True) + EPS)
    return centred * inverse, inverse


def norm_back(e, gain, normed, inverse):
    t = e * gain
    t_mean = jnp.mean(t, axis=-1, keepdims=True)
    cross = jnp.mean(t * normed, axis=-1, keepdims=True)
    return inverse * (t - t_mean - normed * cross)


def attn_kernel(len_ref, x_ref, g_ref, gain_ref, shift_ref, w3_ref, b3_ref, wo_ref, keep_ref, up_ref, down_ref,
                dw3_ref, dwo_ref, db3_ref, dgain_ref, dshift_ref, sq_ref, ao_ref, ff_ref,
                n1, n1t, gl, gf, q_s, k_s, v_s, dc_s, d3, ctx, dq, dk, dv):
    step = pl.program_id(0)
    last = pl.num_programs(0) - 1
    rows, d = x_ref.shape
    gw = wo_ref.shape[0]
    qb = 256
    nb = rows // qb
    seq = len_ref[0]

    @pl.when(step == 0)
    def _():
        def prep(i, c):
            r = pl.ds(pl.multiple_of(i * qb, qb), qb)
            normed, _ = norm_parts(x_ref[r, :].astype(F32))
            low = normed * gain_ref[...] + shift_ref[...]
            n1[r, :] = low.astype(BF)
            valid = (lax.broadcasted_iota(jnp.int32, (qb, 1), 0) + i * qb < seq).astype(F32)
            gl[r, :] = (g_ref[r, :].astype(F32) * valid).astype(BF)
            gf[r, :] = jnp.zeros((qb, d), F32)
            ao_ref[r, :] = jnp.zeros((qb, d), F32)
            return c
        lax.fori_loop(0, nb, prep, 0)
        n1t[...] = n1[...].astype(F32).T.astype(BF)
        sq_ref[...] = jnp.zeros_like(sq_ref)

    def project(i, c):
        r = pl.ds(pl.multiple_of(i * qb, qb), qb)
        t = mm(n1[r, :], w3_ref[0]) + b3_ref[0]
        keep = jnp.concatenate([keep_ref[r, :]] * (gw // 128), axis=1)
        up = jnp.concatenate([up_ref[r, :]] * (gw // 128), axis=1)
        down = jnp.concatenate([down_ref[r, :]] * (gw // 128), axis=1)
        for at, ref, scale in ((0, q_s, HEAD_DIM ** -0.5), (1, k_s, None)):
            v = t[:, at * gw:(at + 1) * gw]
            half = ROT // 2
            turned = v * keep + pltpu.roll(v, gw - half, 1) * up + pltpu.roll(v, half, 1) * down
            low = turned.astype(BF)
            ref[r, :] = low if scale is None else (low.astype(F32) * scale).astype(BF)
        v_s[r, :] = t[:, 2 * gw:].astype(BF)
        dc_s[r, :] = mm_rt(gl[r, :], wo_ref[...]).astype(BF)
        for ref in (ctx, dq, dk, dv):
            ref[r, :] = jnp.zeros((qb, gw), F32)
        return c
    lax.fori_loop(0, nb, project, 0)

    key_bias = jnp.where(lax.broadcasted_iota(jnp.int32, (1, rows), 1) < seq, 0.0, MASKED).astype(F32)
    causal = lax.broadcasted_iota(jnp.int32, (qb, qb), 1) <= lax.broadcasted_iota(jnp.int32, (qb, qb), 0)

    def head(h, c):
        lane = lax.broadcasted_iota(jnp.int32, (1, gw), 1) // HEAD_DIM
        mask = jnp.where(lane == h, 1.0, 0.0).astype(F32)
        mask_low = mask.astype(BF)
        for i in range(nb):
            lo, kl = i * qb, (i + 1) * qb
            qm = q_s[lo:kl, :] * mask_low
            dcm = dc_s[lo:kl, :] * mask_low
            s = mm_rt(qm, k_s[:kl, :]) + key_bias[:, :kl]
            diag = jnp.where(causal, s[:, lo:], MASKED)
            s = diag if i == 0 else jnp.concatenate([s[:, :lo], diag], axis=1)
            dp = mm_rt(dcm, v_s[:kl, :])
            e = jnp.exp(s - jnp.max(s, axis=1, keepdims=True))
            p = e * (1.0 / jnp.sum(e, axis=1, keepdims=True))
            p_low = p.astype(BF)
            inner = jnp.sum(p * dp, axis=1, keepdims=True)
            ds = (p * (dp - inner)).astype(BF)
            ctx[lo:kl, :] += mm(p_low, v_s[:kl, :]) * mask
            dq[lo:kl, :] += mm(ds, k_s[:kl, :]) * mask
            dv[:kl, :] += mm_lt(p_low, dcm)
            dk[:kl, :] += mm_lt(ds, qm)
        return c
    lax.fori_loop(0, gw // HEAD_DIM, head, 0)

    def finish(i, c):
        r = pl.ds(pl.multiple_of(i * qb, qb), qb)
        keep = jnp.concatenate([keep_ref[r, :]] * (gw // 128), axis=1)
        up = jnp.concatenate([up_ref[r, :]] * (gw // 128), axis=1)
        down = jnp.concatenate([down_ref[r, :]] * (gw // 128), axis=1)
        half = ROT // 2
        for at, ref, scale in ((0, dq, HEAD_DIM ** -0.5), (1, dk, 1.0)):
            v = ref[r, :] * scale
            turned = v * keep - pltpu.roll(v, gw - half, 1) * up - pltpu.roll(v, half, 1) * down
            d3[r, at * gw:(at + 1) * gw] = turned.astype(BF)
        d3[r, 2 * gw:] = dv[r, :].astype(BF)
        low = ctx[r, :].astype(BF)
        ao_ref[r, :] += mm(low, wo_ref[...])
        gf[r, :] += mm_rt(d3[r, :], w3_ref[0])
        return c
    lax.fori_loop(0, nb, finish, 0)

    dw3 = mm(n1t[...], d3[...])
    dw3_ref[0] = dw3.astype(BF)
    dwo = mm_lt(ctx[...].astype(BF), gl[...])
    dwo_ref[...] = dwo.astype(BF)
    db3 = jnp.sum(d3[...].astype(F32), axis=0, keepdims=True)
    db3_ref[0] = db3
    sq_ref[...] += jnp.sum(dw3 * dw3, axis=0, keepdims=True) + jnp.sum(dwo * dwo, axis=0, keepdims=True) + db3 * db3

    @pl.when(step == last)
    def _():
        def back(i, c):
            r = pl.ds(pl.multiple_of(i * qb, qb), qb)
            normed, inverse = norm_parts(x_ref[r, :].astype(F32))
            e = gf[r, :]
            ff_ref[r, :] = norm_back(e, gain_ref[...], normed, inverse)
            return (c[0] + jnp.sum(e * normed, axis=0, keepdims=True), c[1] + jnp.sum(e, axis=0, keepdims=True))
        zero = jnp.zeros((1, d), F32)
        dgain, dshift = lax.fori_loop(0, nb, back, (zero, zero))
        dgain_ref[...] = dgain
        dshift_ref[...] = dshift
        sq_ref[...] += dgain * dgain + dshift * dshift


def attention(lengths, x, g, gain, shift, w3, b3, wo):
    rows, d = x.shape
    gw = d // GROUPS
    tables = [jnp.asarray(t) for t in rotary_tables(rows, 128)]
    whole = lambda *shape: pl.BlockSpec(shape, lambda j: (0,) * len(shape))
    grid_spec = pl.GridSpec(
        grid=(GROUPS,),
        in_specs=[
            pl.BlockSpec(memory_space=pltpu.SMEM),
            whole(rows, d), whole(rows, d), whole(1, d), whole(1, d),
            pl.BlockSpec((1, d, d), lambda j: (j, 0, 0)),
            pl.BlockSpec((1, 1, d), lambda j: (j, 0, 0)),
            pl.BlockSpec((gw, d), lambda j: (j, 0)),
            whole(rows, 128), whole(rows, 128), whole(rows, 128),
        ],
        out_specs=[
            pl.BlockSpec((1, d, d), lambda j: (j, 0, 0)),
            pl.BlockSpec((gw, d), lambda j: (j, 0)),
            pl.BlockSpec((1, 1, d), lambda j: (j, 0, 0)),
            whole(1, d), whole(1, d), whole(1, d),
            whole(rows, d), whole(rows, d),
        ],
        scratch_shapes=[
            pltpu.VMEM((rows, d), BF), pltpu.VMEM((d, rows), BF), pltpu.VMEM((rows, d), BF), pltpu.VMEM((rows, d), F32),
            pltpu.VMEM((rows, gw), BF), pltpu.VMEM((rows, gw), BF), pltpu.VMEM((rows, gw), BF), pltpu.VMEM((rows, gw), BF),
            pltpu.VMEM((rows, d), BF),
            pltpu.VMEM((rows, gw), F32), pltpu.VMEM((rows, gw), F32), pltpu.VMEM((rows, gw), F32), pltpu.VMEM((rows, gw), F32),
        ],
    )
    flops = 2 * 3 * rows * (d * 3 * d + d * d) + 12 * HEADS * rows * rows * HEAD_DIM
    return pl.pallas_call(
        attn_kernel,
        grid_spec=grid_spec,
        out_shape=[
            jax.ShapeDtypeStruct((GROUPS, d, d), BF),
            jax.ShapeDtypeStruct((d, d), BF),
            jax.ShapeDtypeStruct((GROUPS, 1, d), F32),
            jax.ShapeDtypeStruct((1, d), F32), jax.ShapeDtypeStruct((1, d), F32), jax.ShapeDtypeStruct((1, d), F32),
            jax.ShapeDtypeStruct((rows, d), F32), jax.ShapeDtypeStruct((rows, d), F32),
        ],
        compiler_params=pltpu.CompilerParams(vmem_limit_bytes=VMEM_LIMIT),
        cost_estimate=pl.CostEstimate(flops=flops * 3, bytes_accessed=30_000_000, transcendentals=HEADS * rows * rows),
        name="attention",
    )(lengths, x, g, gain, shift, w3, b3, wo, *tables)


ERF_P = 0.3275911
ERF_A = (0.254829592, -0.284496736, 1.421413741, -1.453152027, 1.061405429)


def gelu_parts(u):
    z = jnp.abs(u) * (2.0 ** -0.5)
    t = 1.0 / (1.0 + ERF_P * z)
    bell = jnp.exp(-0.5 * (u * u))
    a1, a2, a3, a4, a5 = (0.5 * a for a in ERF_A)
    tail = ((((a5 * t + a4) * t + a3) * t + a2) * t + a1) * t * bell
    cdf = jnp.where(u >= 0.0, 1.0 - tail, tail)
    return u * cdf, cdf + u * bell * (1.0 / math.sqrt(2.0 * math.pi))


def ffn_kernel(len_ref, x_ref, g_ref, gain_ref, shift_ref, wu_ref, bu_ref, wd_ref, bias_ref, ao_ref, ff_ref,
               dwu_ref, dwd_ref, dbu_ref, dgain_ref, dshift_ref, dbd_ref, sq_ref, out_ref, gx_ref,
               n2, n2t, gl, gs, act, gup, acc):
    step = pl.program_id(0)
    last = pl.num_programs(0) - 1
    rows, d = x_ref.shape
    fc = wu_ref.shape[2]
    rb = 256
    nb = rows // rb
    seq = len_ref[0]

    @pl.when(step == 0)
    def _():
        def prep(i, c):
            r = pl.ds(pl.multiple_of(i * rb, rb), rb)
            normed, _ = norm_parts(x_ref[r, :].astype(F32))
            low = normed * gain_ref[...] + shift_ref[...]
            n2[r, :] = low.astype(BF)
            valid = (lax.broadcasted_iota(jnp.int32, (rb, 1), 0) + i * rb < seq).astype(F32)
            gl[r, :] = (g_ref[r, :].astype(F32) * valid).astype(BF)
            gs[r, :] = jnp.zeros((rb, d), F32)
            acc[r, :] = jnp.zeros((rb, d), F32)
            return c
        lax.fori_loop(0, nb, prep, 0)
        n2t[...] = n2[...].astype(F32).T.astype(BF)
        sq_ref[...] = jnp.zeros_like(sq_ref)

    def rows_step(i, dbu):
        r = pl.ds(pl.multiple_of(i * rb, rb), rb)
        u = mm(n2[r, :], wu_ref[0]) + bu_ref[0]
        da = mm_rt(gl[r, :], wd_ref[0])
        a, slope = gelu_parts(u)
        a_low = a.astype(BF)
        act[r, :] = a_low
        gu = (da * slope).astype(BF)
        gup[r, :] = gu
        acc[r, :] += mm(a_low, wd_ref[0])
        gs[r, :] += mm_rt(gu, wu_ref[0])
        return dbu + jnp.sum(gu.astype(F32), axis=0, keepdims=True)
    dbu = lax.fori_loop(0, nb, rows_step, jnp.zeros((1, fc), F32))
    dbu_ref[0] = dbu

    dwu = mm(n2t[...], gup[...])
    dwu_ref[0] = dwu.astype(BF)
    dwd = mm_lt(act[...], gl[...])
    dwd_ref[0] = dwd.astype(BF)
    wide = jnp.sum(dwu * dwu, axis=0, keepdims=True) + dbu * dbu
    total = jnp.sum(dwd * dwd, axis=0, keepdims=True)
    sq_ref[:, :d] += total
    sq_ref[:, :fc] += wide

    @pl.when(step == last)
    def _():
        def back(i, c):
            r = pl.ds(pl.multiple_of(i * rb, rb), rb)
            x = x_ref[r, :].astype(F32)
            normed, inverse = norm_parts(x)
            e = gs[r, :]
            grad_rows = gl[r, :].astype(F32)
            gx_ref[r, :] = (grad_rows + ff_ref[r, :] + norm_back(e, gain_ref[...], normed, inverse)).astype(BF)
            valid = (lax.broadcasted_iota(jnp.int32, (rb, 1), 0) + i * rb < seq).astype(F32)
            out_ref[r, :] = ((x + ao_ref[r, :] + acc[r, :] + bias_ref[...]) * valid).astype(BF)
            return (c[0] + jnp.sum(e * normed, axis=0, keepdims=True), c[1] + jnp.sum(e, axis=0, keepdims=True),
                    c[2] + jnp.sum(grad_rows, axis=0, keepdims=True))
        zero = jnp.zeros((1, d), F32)
        dgain, dshift, dbd = lax.fori_loop(0, nb, back, (zero, zero, zero))
        dgain_ref[...] = dgain
        dshift_ref[...] = dshift
        dbd_ref[...] = dbd
        sq_ref[:, :d] += dgain * dgain + dshift * dshift + 2.0 * dbd * dbd


def ffn(lengths, x, g, gain, shift, wu3, bu3, wd3, bias, ao, ff):
    rows, d = x.shape
    chunks, _, fc = wu3.shape
    whole = lambda *shape: pl.BlockSpec(shape, lambda j: (0,) * len(shape))
    grid_spec = pl.GridSpec(
        grid=(chunks,),
        in_specs=[
            pl.BlockSpec(memory_space=pltpu.SMEM),
            whole(rows, d), whole(rows, d), whole(1, d), whole(1, d),
            pl.BlockSpec((1, d, fc), lambda j: (j, 0, 0)),
            pl.BlockSpec((1, 1, fc), lambda j: (j, 0, 0)),
            pl.BlockSpec((1, fc, d), lambda j: (j, 0, 0)),
            whole(1, d), whole(rows, d), whole(rows, d),
        ],
        out_specs=[
            pl.BlockSpec((1, d, fc), lambda j: (j, 0, 0)),
            pl.BlockSpec((1, fc, d), lambda j: (j, 0, 0)),
            pl.BlockSpec((1, 1, fc), lambda j: (j, 0, 0)),
            whole(1, d), whole(1, d), whole(1, d), whole(1, max(d, fc)),
            whole(rows, d), whole(rows, d),
        ],
        scratch_shapes=[
            pltpu.VMEM((rows, d), BF), pltpu.VMEM((d, rows), BF), pltpu.VMEM((rows, d), BF), pltpu.VMEM((rows, d), F32),
            pltpu.VMEM((rows, fc), BF), pltpu.VMEM((rows, fc), BF), pltpu.VMEM((rows, d), F32),
        ],
    )
    return pl.pallas_call(
        ffn_kernel,
        grid_spec=grid_spec,
        out_shape=[
            jax.ShapeDtypeStruct((chunks, d, fc), BF), jax.ShapeDtypeStruct((chunks, fc, d), BF),
            jax.ShapeDtypeStruct((chunks, 1, fc), F32),
            jax.ShapeDtypeStruct((1, d), F32), jax.ShapeDtypeStruct((1, d), F32), jax.ShapeDtypeStruct((1, d), F32),
            jax.ShapeDtypeStruct((1, max(d, fc)), F32),
            jax.ShapeDtypeStruct((rows, d), BF), jax.ShapeDtypeStruct((rows, d), BF),
        ],
        compiler_params=pltpu.CompilerParams(vmem_limit_bytes=VMEM_LIMIT),
        cost_estimate=pl.CostEstimate(flops=2 * 6 * rows * d * fc * chunks * 2, bytes_accessed=40_000_000, transcendentals=rows * fc * chunks),
        name="feedforward",
    )(lengths, x, g, gain, shift, wu3, bu3, wd3, bias, ao, ff)


def xor_permute(value, axis, size, bit):
    return lax.ppermute(value, axis, [(i, i ^ bit) for i in range(size)])


def all_norms(own, sizes):
    rep, fsdp = sizes
    me = lax.axis_index("rep") * fsdp + lax.axis_index("fsdp")
    row = jnp.where(jnp.arange(rep * fsdp) == me, own, 0.0)
    for axis, size in (("fsdp", fsdp), ("rep", rep)):
        if size & (size - 1):
            row = lax.psum(row, axis)
            continue
        bit = 1
        while bit < size:
            row = row + xor_permute(row, axis, size, bit)
            bit *= 2
    return row


def per_device(sizes, block_input, cotangent, lengths, first_gain, first_shift, second_gain, second_shift, triple_weight, triple_bias,
               output_weight, output_bias, upward_weight, upward_bias, downward_weight, downward_bias):
    rep, n = sizes
    rows, d = block_input.shape
    dn = first_gain.shape[0]
    fn = upward_bias.shape[0]
    f = fn * n
    gw = d // GROUPS
    chunks = f // d
    gather = lambda v: lax.all_gather(v, "fsdp", axis=0, tiled=True)

    small = jnp.concatenate([first_gain, first_shift, second_gain, second_shift, output_bias, downward_bias, triple_bias, upward_bias])
    small = gather(small.reshape(1, -1)).astype(F32)
    cut = lambda at, width: small[:, at:at + width].reshape(1, -1)
    gain1, shift1, gain2, shift2, bias_o, bias_d = (cut(i * dn, dn) for i in range(6))
    bias_t = cut(6 * dn, 3 * dn)
    bias_u = cut(9 * dn, fn)
    wt = gather(triple_weight)
    wo = gather(output_weight)
    wu = gather(upward_weight)
    wd = gather(downward_weight)

    by_group = lambda v: jnp.stack([jnp.concatenate([v[:, a * d + j * gw:a * d + (j + 1) * gw] for a in range(3)], axis=1) for j in range(GROUPS)])
    dw3, dwo, db3, dgain1, dshift1, sq1, ao, ff = attention(lengths, block_input, cotangent, gain1, shift1, by_group(wt), by_group(bias_t), wo)
    wu4 = jnp.stack([wu[:, j * d:(j + 1) * d] for j in range(chunks)])
    dwu4, dwd4, dbu, dgain2, dshift2, dbd, sq2, out, gx = ffn(
        lengths, block_input, cotangent, gain2, shift2, wu4, bias_u.reshape(chunks, 1, d), wd.reshape(chunks, d, d), bias_o + bias_d, ao, ff)

    own = jnp.sqrt(jnp.sum(sq1) + jnp.sum(sq2))
    norms = all_norms(own, sizes)
    factor = jnp.minimum(1.0, jnp.mean(norms) / own) / norms.shape[0]

    shards = lambda v: v.reshape(v.shape[0], n, dn, d).swapaxes(0, 1).reshape(n, -1, d)
    ungroup = lambda v: jnp.concatenate([v[:, 0, a * gw:(a + 1) * gw] for a in range(3)], axis=0).reshape(n, 3 * dn)
    vec = lambda v: v.reshape(n, -1)
    smalls = jnp.concatenate([vec(dgain1), vec(dshift1), vec(dgain2), vec(dshift2), vec(dbd), ungroup(db3), vec(dbu)], axis=1)
    small_rows = 8
    smalls = jnp.pad(smalls, ((0, 0), (0, small_rows * d - smalls.shape[1]))).reshape(n, small_rows, d)
    scale = lambda v: (v.astype(F32) * factor).astype(BF)
    pack = jnp.concatenate([scale(shards(dw3)), scale(shards(dwo[None])), scale(shards(dwu4)), scale(dwd4.reshape(n, fn, d)), scale(smalls)], axis=1)
    mine = lax.psum_scatter(pack, "fsdp", scatter_dimension=0, tiled=True)[0]
    mine = lax.psum(mine, "rep").astype(F32)

    at = 0
    def take(count):
        nonlocal at
        at += count
        return mine[at - count:at]
    t3 = take(3 * dn).reshape(GROUPS, dn, d)
    g_triple = jnp.concatenate([t3[j, :, a * gw:(a + 1) * gw] for a in range(3) for j in range(GROUPS)], axis=1)
    g_out = take(dn)
    up = take(chunks * dn).reshape(chunks, dn, d)
    g_up = jnp.concatenate([up[j] for j in range(chunks)], axis=1)
    g_down = take(fn)
    sm = take(small_rows).reshape(-1)
    part = lambda at, width: sm[at:at + width]
    g1, s1, g2, s2, bd = (part(i * dn, dn) for i in range(5))
    return (out, gx, g1, s1, g2, s2, g_triple, part(5 * dn, 3 * dn), g_out, bd, g_up, part(8 * dn, fn), g_down, bd, norms)


def solution(mesh):
    rows = P(("rep", "fsdp"), None)
    vec, mat = P("fsdp"), P("fsdp", None)
    sizes = (mesh.shape["rep"], mesh.shape["fsdp"])
    return jax.shard_map(
        lambda *args: per_device(sizes, *args),
        mesh=mesh,
        in_specs=(rows, rows, P(("rep", "fsdp")), vec, vec, vec, vec, mat, vec, mat, vec, mat, vec, mat, vec),
        out_specs=(rows, rows, vec, vec, vec, vec, mat, vec, mat, vec, mat, vec, mat, vec, P()),
        check_vma=False,
    )
```

```python
import math
import numpy as np
import jax
import jax.numpy as jnp
from jax import lax
from jax.experimental import pallas as pl
from jax.experimental.pallas import tpu as pltpu
from jax.sharding import PartitionSpec as P

HEADS = 12
HEAD_DIM = 64
ROT = 16
EPS = 1e-05
MASKED = -1e30
BF = jnp.bfloat16
F32 = jnp.float32
GROUPS = 3
VMEM_LIMIT = 60 * 1024 * 1024


def mm(a, b):
    return jnp.dot(a, b, preferred_element_type=F32)


def mm_rt(a, b):
    return lax.dot_general(a, b, (((1,), (1,)), ((), ())), preferred_element_type=F32)


def mm_lt(a, b):
    return lax.dot_general(a, b, (((0,), (0,)), ((), ())), preferred_element_type=F32)


def rotary_tables(rows, width):
    half = ROT // 2
    freq = np.exp(np.arange(half, dtype=np.float32) * np.float32(-2.0 * math.log(10000.0) / ROT))
    ang = np.arange(rows, dtype=np.float32)[:, None] * freq.astype(np.float32)[None, :]
    cos, sin = np.cos(ang), np.sin(ang)
    keep = np.ones((rows, HEAD_DIM), np.float32)
    up = np.zeros((rows, HEAD_DIM), np.float32)
    down = np.zeros((rows, HEAD_DIM), np.float32)
    keep[:, :half] = cos
    keep[:, half:ROT] = cos
    up[:, :half] = -sin
    down[:, half:ROT] = sin
    rep = width // HEAD_DIM
    return tuple(np.tile(t, (1, rep)).astype(np.float32) for t in (keep, up, down))


def norm_parts(values):
    centred = values - jnp.mean(values, axis=-1, keepdims=True)
    inverse = lax.rsqrt(jnp.mean(centred * centred, axis=-1, keepdims=True) + EPS)
    return centred * inverse, inverse


def norm_back(e, gain, normed, inverse):
    t = e * gain
    t_mean = jnp.mean(t, axis=-1, keepdims=True)
    cross = jnp.mean(t * normed, axis=-1, keepdims=True)
    return inverse * (t - t_mean - normed * cross)


SMALL = 16


def write_halves(value, tmp, keep_ref, send_ref, core, dn, at=None):
    tmp[...] = value.astype(BF)
    for z in range(keep_ref.shape[0]):
        mine = pl.ds(pl.multiple_of((2 * z + core) * dn, 16), dn)
        other = pl.ds(pl.multiple_of((2 * z + 1 - core) * dn, 16), dn)
        keep_ref[z, 0] = tmp[mine, :]
        send_ref[z, 0] = tmp[other, :]


def attn_kernel(split, sc_ref, x_ref, g_ref, par_ref, b3_ref, keep_ref, up_ref, down_ref, *rest):
    nw = split["pieces"]
    w_refs, rest = rest[:nw], rest[nw:]
    nd = 2 if split["on"] else 1
    dw_refs, rest = rest[:nd], rest[nd:]
    sm_ref, ao_ref, ff_ref, rest = rest[0], rest[1], rest[2], rest[3:]
    w, n1, n1t, gl, gf, q_s, k_s, v_s, dc_s, d3, ctx_all, ctx, dq, dk, dv, tmp, sems = rest
    step = pl.program_id(0)
    last = pl.num_programs(0) - 1
    rows, d = x_ref.shape
    gw = d // GROUPS
    qb = 256
    nb = rows // qb
    seq = sc_ref[0]
    gain, shift = par_ref[0:1, :], par_ref[1:2, :]

    def copies():
        if not split["on"]:
            return [pltpu.make_async_copy(w_refs[0].at[m], w.at[m], sems.at[m]) for m in range(GROUPS + 1)]
        z, core, rep = sc_ref[1], sc_ref[2], sc_ref[3]
        dn, nz, nr = split["dn"], split["nz"], split["nr"]
        own, sib, near, sibs = w_refs[0], w_refs[1], w_refs[2:2 + nr], w_refs[2 + nr]
        place = lambda zz, cc: pl.ds(pl.multiple_of((zz * 2 + cc) * dn, 16), dn)
        out = []
        for m in range(nr):
            out.append((own.at[m], w.at[m, place(z, core)], m))
            out.append((sib.at[m], w.at[m, place(z, 1 - core)], m))
        for j in range(nr):
            for k in range(1, nz):
                m, zz = rep ^ j, z ^ k
                out.append((near[j].at[k - 1], w.at[m, place(zz, core)], j))
                out.append((sibs.at[j, k - 1], w.at[m, place(zz, 1 - core)], j))
        return [pltpu.make_async_copy(a, b, sems.at[i]) for i, (a, b, _) in enumerate(out)]

    @pl.when(step == 0)
    def _():
        for c in copies():
            c.start()

        def prep(i, c):
            r = pl.ds(pl.multiple_of(i * qb, qb), qb)
            normed, _ = norm_parts(x_ref[r, :].astype(F32))
            low = normed * gain + shift
            n1[r, :] = low.astype(BF)
            valid = (lax.broadcasted_iota(jnp.int32, (qb, 1), 0) + i * qb < seq).astype(F32)
            gl[r, :] = (g_ref[r, :].astype(F32) * valid).astype(BF)
            gf[r, :] = jnp.zeros((qb, d), F32)
            return c
        lax.fori_loop(0, nb, prep, 0)
        n1t[...] = n1[...].astype(F32).T.astype(BF)
        sm_ref[...] = jnp.zeros_like(sm_ref)
        for c in copies():
            c.wait()

    @pl.when(step < GROUPS)
    def _():
        w3 = w.at[step]
        wo = w.at[GROUPS, pl.ds(pl.multiple_of(step * gw, gw), gw)]

        def project(i, c):
            r = pl.ds(pl.multiple_of(i * qb, qb), qb)
            t = mm(n1[r, :], w3[...]) + b3_ref[0]
            keep = jnp.concatenate([keep_ref[r, :]] * (gw // 128), axis=1)
            up = jnp.concatenate([up_ref[r, :]] * (gw // 128), axis=1)
            down = jnp.concatenate([down_ref[r, :]] * (gw // 128), axis=1)
            half = ROT // 2
            for at, ref, scale in ((0, q_s, HEAD_DIM ** -0.5), (1, k_s, None)):
                v = t[:, at * gw:(at + 1) * gw]
                turned = v * keep + pltpu.roll(v, gw - half, 1) * up + pltpu.roll(v, half, 1) * down
                low = turned.astype(BF)
                ref[r, :] = low if scale is None else (low.astype(F32) * scale).astype(BF)
            v_s[r, :] = t[:, 2 * gw:].astype(BF)
            dc_s[r, :] = mm_rt(gl[r, :], wo[...]).astype(BF)
            for ref in (ctx, dq, dk, dv):
                ref[r, :] = jnp.zeros((qb, gw), F32)
            return c
        lax.fori_loop(0, nb, project, 0)

        key_bias = jnp.where(lax.broadcasted_iota(jnp.int32, (1, rows), 1) < seq, 0.0, MASKED).astype(F32)
        causal = lax.broadcasted_iota(jnp.int32, (qb, qb), 1) <= lax.broadcasted_iota(jnp.int32, (qb, qb), 0)

        def head(h, c):
            lane = lax.broadcasted_iota(jnp.int32, (1, gw), 1) // HEAD_DIM
            mask = jnp.where(lane == h, 1.0, 0.0).astype(F32)
            mask_low = mask.astype(BF)
            for i in range(nb):
                lo, kl = i * qb, (i + 1) * qb
                qm = q_s[lo:kl, :] * mask_low
                dcm = dc_s[lo:kl, :] * mask_low
                s = mm_rt(qm, k_s[:kl, :]) + key_bias[:, :kl]
                diag = jnp.where(causal, s[:, lo:], MASKED)
                s = diag if i == 0 else jnp.concatenate([s[:, :lo], diag], axis=1)
                dp = mm_rt(dcm, v_s[:kl, :])
                e = jnp.exp(s - jnp.max(s, axis=1, keepdims=True))
                p = e * (1.0 / jnp.sum(e, axis=1, keepdims=True))
                p_low = p.astype(BF)
                inner = jnp.sum(p * dp, axis=1, keepdims=True)
                ds = (p * (dp - inner)).astype(BF)
                ctx[lo:kl, :] += mm(p_low, v_s[:kl, :]) * mask
                dq[lo:kl, :] += mm(ds, k_s[:kl, :]) * mask
                dv[:kl, :] += mm_lt(p_low, dcm)
                dk[:kl, :] += mm_lt(ds, qm)
            return c
        lax.fori_loop(0, gw // HEAD_DIM, head, 0)

        def finish(i, c):
            r = pl.ds(pl.multiple_of(i * qb, qb), qb)
            keep = jnp.concatenate([keep_ref[r, :]] * (gw // 128), axis=1)
            up = jnp.concatenate([up_ref[r, :]] * (gw // 128), axis=1)
            down = jnp.concatenate([down_ref[r, :]] * (gw // 128), axis=1)
            half = ROT // 2
            for at, ref, scale in ((0, dq, HEAD_DIM ** -0.5), (1, dk, 1.0)):
                v = ref[r, :] * scale
                turned = v * keep - pltpu.roll(v, gw - half, 1) * up - pltpu.roll(v, half, 1) * down
                d3[r, at * gw:(at + 1) * gw] = turned.astype(BF)
            d3[r, 2 * gw:] = dv[r, :].astype(BF)
            ctx_all[r, pl.ds(pl.multiple_of(step * gw, gw), gw)] = ctx[r, :].astype(BF)
            gf[r, :] += mm_rt(d3[r, :], w3[...])
            return c
        lax.fori_loop(0, nb, finish, 0)
        db3 = jnp.sum(d3[...].astype(F32), axis=0, keepdims=True)
        sm_ref[pl.ds(2 + step, 1), :] = db3
        sm_ref[5:6, :] += db3 * db3

    def store(dw):
        sm_ref[5:6, :] += jnp.sum(dw * dw, axis=0, keepdims=True)
        if split["on"]:
            write_halves(dw, tmp, dw_refs[0], dw_refs[1], sc_ref[2], split["dn"])
        else:
            dw_refs[0][0] = dw.astype(BF)

    @pl.when(step < GROUPS)
    def _():
        store(mm(n1t[...], d3[...]))

    @pl.when(step == last)
    def _():
        store(mm_lt(ctx_all[...], gl[...]))

        def back(i, c):
            r = pl.ds(pl.multiple_of(i * qb, qb), qb)
            ao_ref[r, :] = mm(ctx_all[r, :], w[GROUPS])
            normed, inverse = norm_parts(x_ref[r, :].astype(F32))
            e = gf[r, :]
            ff_ref[r, :] = norm_back(e, gain, normed, inverse)
            return (c[0] + jnp.sum(e * normed, axis=0, keepdims=True), c[1] + jnp.sum(e, axis=0, keepdims=True))
        zero = jnp.zeros((1, d), F32)
        dgain, dshift = lax.fori_loop(0, nb, back, (zero, zero))
        sm_ref[0:1, :] = dgain
        sm_ref[1:2, :] = dshift
        sm_ref[5:6, :] += dgain * dgain + dshift * dshift


def attention(split, scalars, x, g, par, b3, weights):
    rows, d = x.shape
    gw = d // GROUPS
    tables = [jnp.asarray(t) for t in rotary_tables(rows, 128)]
    whole = lambda *shape: pl.BlockSpec(shape, lambda j: (0,) * len(shape))
    any_ = pl.BlockSpec(memory_space=pl.ANY)
    split = dict(split, pieces=len(weights))
    if split["on"]:
        nz, dn = split["nz"], split["dn"]
        dw_specs = [pl.BlockSpec((nz, 1, dn, d), lambda j: (0, j, 0, 0))] * 2
        dw_shapes = [jax.ShapeDtypeStruct((nz, GROUPS + 1, dn, d), BF)] * 2
    else:
        dw_specs = [pl.BlockSpec((1, d, d), lambda j: (j, 0, 0))]
        dw_shapes = [jax.ShapeDtypeStruct((GROUPS + 1, d, d), BF)]
    grid_spec = pl.GridSpec(
        grid=(GROUPS + 1,),
        in_specs=[
            pl.BlockSpec(memory_space=pltpu.SMEM),
            whole(rows, d), whole(rows, d), whole(*par.shape),
            pl.BlockSpec((1, 1, d), lambda j: (jnp.minimum(j, GROUPS - 1), 0, 0)),
            whole(rows, 128), whole(rows, 128), whole(rows, 128),
        ] + [any_] * len(weights),
        out_specs=dw_specs + [whole(8, d), whole(rows, d), whole(rows, d)],
        scratch_shapes=[
            pltpu.VMEM((GROUPS + 1, d, d), BF),
            pltpu.VMEM((rows, d), BF), pltpu.VMEM((d, rows), BF), pltpu.VMEM((rows, d), BF), pltpu.VMEM((rows, d), F32),
            pltpu.VMEM((rows, gw), BF), pltpu.VMEM((rows, gw), BF), pltpu.VMEM((rows, gw), BF), pltpu.VMEM((rows, gw), BF),
            pltpu.VMEM((rows, d), BF), pltpu.VMEM((rows, d), BF),
            pltpu.VMEM((rows, gw), F32), pltpu.VMEM((rows, gw), F32), pltpu.VMEM((rows, gw), F32), pltpu.VMEM((rows, gw), F32),
            pltpu.VMEM((d, d), BF), pltpu.SemaphoreType.DMA((64,)),
        ],
    )
    flops = 2 * 3 * rows * (d * 3 * d + d * d) + 12 * HEADS * rows * rows * HEAD_DIM
    return pl.pallas_call(
        lambda *refs: attn_kernel(split, *refs),
        grid_spec=grid_spec,
        out_shape=dw_shapes + [
            jax.ShapeDtypeStruct((8, d), F32),
            jax.ShapeDtypeStruct((rows, d), F32), jax.ShapeDtypeStruct((rows, d), F32),
        ],
        compiler_params=pltpu.CompilerParams(vmem_limit_bytes=VMEM_LIMIT),
        cost_estimate=pl.CostEstimate(flops=flops * 3, bytes_accessed=30_000_000, transcendentals=HEADS * rows * rows),
        name="attention",
    )(scalars, x, g, par, b3, *tables, *weights)


ERF_P = 0.3275911
ERF_A = (0.254829592, -0.284496736, 1.421413741, -1.453152027, 1.061405429)


def gelu_parts(u):
    z = jnp.abs(u) * (2.0 ** -0.5)
    t = 1.0 / (1.0 + ERF_P * z)
    bell = jnp.exp(-0.5 * (u * u))
    a1, a2, a3, a4, a5 = (0.5 * a for a in ERF_A)
    tail = ((((a5 * t + a4) * t + a3) * t + a2) * t + a1) * t * bell
    cdf = jnp.where(u >= 0.0, 1.0 - tail, tail)
    return u * cdf, cdf + u * bell * (1.0 / math.sqrt(2.0 * math.pi))


def ffn_kernel(split, sc_ref, x_ref, g_ref, par_ref, wu_ref, bu_ref, wd_ref, ao_ref, ff_ref, sm1_ref, *rest):
    nd = 4 if split["on"] else 2
    dw_refs, rest = rest[:nd], rest[nd:]
    sm_ref, norm_ref, out_ref, gx_ref = rest[:4]
    n2, n2t, gl, gs, act, gup, acc, sq, tmp = rest[4:]
    step = pl.program_id(0)
    last = pl.num_programs(0) - 1
    rows, d = x_ref.shape
    fc = wu_ref.shape[1]
    rb = 256
    nb = rows // rb
    seq = sc_ref[0]
    gain, shift = par_ref[2:3, :], par_ref[3:4, :]

    @pl.when(step == 0)
    def _():
        def prep(i, c):
            r = pl.ds(pl.multiple_of(i * rb, rb), rb)
            normed, _ = norm_parts(x_ref[r, :].astype(F32))
            low = normed * gain + shift
            n2[r, :] = low.astype(BF)
            valid = (lax.broadcasted_iota(jnp.int32, (rb, 1), 0) + i * rb < seq).astype(F32)
            gl[r, :] = (g_ref[r, :].astype(F32) * valid).astype(BF)
            gs[r, :] = jnp.zeros((rb, d), F32)
            acc[r, :] = jnp.zeros((rb, d), F32)
            return c
        lax.fori_loop(0, nb, prep, 0)
        n2t[...] = n2[...].astype(F32).T.astype(BF)
        sq[...] = jnp.zeros_like(sq)
        sm_ref[...] = jnp.zeros_like(sm_ref)

    def rows_step(i, dbu):
        r = pl.ds(pl.multiple_of(i * rb, rb), rb)
        u = mm(n2[r, :], wu_ref[...]) + bu_ref[0]
        da = mm_rt(gl[r, :], wd_ref[...])
        a, slope = gelu_parts(u)
        a_low = a.astype(BF)
        act[r, :] = a_low
        gu = (da * slope).astype(BF)
        gup[r, :] = gu
        acc[r, :] += mm(a_low, wd_ref[...])
        gs[r, :] += mm_rt(gu, wu_ref[...])
        return dbu + jnp.sum(gu.astype(F32), axis=0, keepdims=True)
    dbu = lax.fori_loop(0, nb, rows_step, jnp.zeros((1, fc), F32))
    sm_ref[pl.ds(8 + step, 1), :] = dbu

    dwu = mm(n2t[...], gup[...])
    total = jnp.sum(dwu * dwu, axis=0, keepdims=True) + dbu * dbu
    if split["on"]:
        write_halves(dwu, tmp, dw_refs[0], dw_refs[1], sc_ref[2], split["dn"])
    else:
        dw_refs[0][0] = dwu.astype(BF)
    dwd = mm_lt(act[...], gl[...])
    total += jnp.sum(dwd * dwd, axis=0, keepdims=True)
    if split["on"]:
        tmp[...] = dwd.astype(BF)
        core, dn, nr = sc_ref[2], split["dn"], split["nr"]
        for m in range(nr):
            dw_refs[2][0, m] = tmp[pl.ds(pl.multiple_of((core * nr + m) * dn, 16), dn), :]
            dw_refs[3][0, m] = tmp[pl.ds(pl.multiple_of(((1 - core) * nr + m) * dn, 16), dn), :]
    else:
        dw_refs[1][0] = dwd.astype(BF)
    sq[...] += total

    @pl.when(step == last)
    def _():
        def back(i, c):
            r = pl.ds(pl.multiple_of(i * rb, rb), rb)
            x = x_ref[r, :].astype(F32)
            normed, inverse = norm_parts(x)
            e = gs[r, :]
            grad_rows = gl[r, :].astype(F32)
            gx_ref[r, :] = (grad_rows + ff_ref[r, :] + norm_back(e, gain, normed, inverse)).astype(BF)
            valid = (lax.broadcasted_iota(jnp.int32, (rb, 1), 0) + i * rb < seq).astype(F32)
            bias = par_ref[4:5, :] + par_ref[5:6, :]
            out_ref[r, :] = ((x + ao_ref[r, :] + acc[r, :] + bias) * valid).astype(BF)
            return (c[0] + jnp.sum(e * normed, axis=0, keepdims=True), c[1] + jnp.sum(e, axis=0, keepdims=True),
                    c[2] + jnp.sum(grad_rows, axis=0, keepdims=True))
        zero = jnp.zeros((1, d), F32)
        dgain, dshift, dbd = lax.fori_loop(0, nb, back, (zero, zero, zero))
        sm_ref[0:2, :] = sm1_ref[0:2, :]
        sm_ref[2:3, :] = dgain
        sm_ref[3:4, :] = dshift
        sm_ref[4:5, :] = dbd
        sm_ref[5:8, :] = sm1_ref[2:5, :]
        final = sq[...] + sm1_ref[5:6, :] + dgain * dgain + dshift * dshift + 2.0 * dbd * dbd
        own = jnp.sqrt(jnp.sum(final, axis=1, keepdims=True))
        here = lax.broadcasted_iota(jnp.int32, norm_ref.shape, 1) == sc_ref[4]
        norm_ref[...] = jnp.where(here, own, 0.0)


def ffn(split, scalars, x, g, par, wu, bu, wd, ao, ff, sm1, norm_width):
    rows, d = x.shape
    chunks = wu.shape[1] // d
    fc = d
    whole = lambda *shape: pl.BlockSpec(shape, lambda j: (0,) * len(shape))
    if split["on"]:
        nz, dn, nr = split["nz"], split["dn"], split["nr"]
        dw_specs = [pl.BlockSpec((nz, 1, dn, d), lambda j: (0, j, 0, 0))] * 2 + [pl.BlockSpec((1, nr, dn, d), lambda j: (j, 0, 0, 0))] * 2
        dw_shapes = [jax.ShapeDtypeStruct((nz, chunks, dn, d), BF)] * 2 + [jax.ShapeDtypeStruct((nz, nr, dn, d), BF)] * 2
    else:
        dw_specs = [pl.BlockSpec((1, d, fc), lambda j: (j, 0, 0)), pl.BlockSpec((1, fc, d), lambda j: (j, 0, 0))]
        dw_shapes = [jax.ShapeDtypeStruct((chunks, d, fc), BF), jax.ShapeDtypeStruct((chunks, fc, d), BF)]
    grid_spec = pl.GridSpec(
        grid=(chunks,),
        in_specs=[
            pl.BlockSpec(memory_space=pltpu.SMEM),
            whole(rows, d), whole(rows, d), whole(*par.shape),
            pl.BlockSpec((d, fc), lambda j: (0, j)),
            pl.BlockSpec((1, 1, fc), lambda j: (j, 0, 0)),
            pl.BlockSpec((fc, d), lambda j: (j, 0)),
            whole(rows, d), whole(rows, d), whole(8, d),
        ],
        out_specs=dw_specs + [whole(SMALL, d), whole(1, norm_width), whole(rows, d), whole(rows, d)],
        scratch_shapes=[
            pltpu.VMEM((rows, d), BF), pltpu.VMEM((d, rows), BF), pltpu.VMEM((rows, d), BF), pltpu.VMEM((rows, d), F32),
            pltpu.VMEM((rows, fc), BF), pltpu.VMEM((rows, fc), BF), pltpu.VMEM((rows, d), F32), pltpu.VMEM((1, d), F32),
            pltpu.VMEM((d, d), BF),
        ],
    )
    return pl.pallas_call(
        lambda *refs: ffn_kernel(split, *refs),
        grid_spec=grid_spec,
        out_shape=dw_shapes + [
            jax.ShapeDtypeStruct((SMALL, d), F32), jax.ShapeDtypeStruct((1, norm_width), F32),
            jax.ShapeDtypeStruct((rows, d), BF), jax.ShapeDtypeStruct((rows, d), BF),
        ],
        compiler_params=pltpu.CompilerParams(vmem_limit_bytes=VMEM_LIMIT),
        cost_estimate=pl.CostEstimate(flops=2 * 6 * rows * d * fc * chunks * 2, bytes_accessed=40_000_000, transcendentals=rows * fc * chunks),
        name="feedforward",
    )(scalars, x, g, par, wu, bu, wd, ao, ff, sm1)


def xor_permute(value, axis, size, bit):
    return lax.ppermute(value, axis, [(i, i ^ bit) for i in range(size)])


def butterfly(value, axis, size):
    if size & (size - 1):
        return lax.psum(value, axis)
    bit = 1
    while bit < size:
        value = value + xor_permute(value, axis, size, bit)
        bit *= 2
    return value


def per_device(sizes, block_input, cotangent, lengths, first_gain, first_shift, second_gain, second_shift, triple_weight, triple_bias,
               output_weight, output_bias, upward_weight, upward_bias, downward_weight, downward_bias):
    rep, n = sizes
    rows, d = block_input.shape
    dn, fn = first_gain.shape[0], upward_bias.shape[0]
    gw = d // GROUPS
    chunks = fn * n // d
    nz = n // 2
    split = dict(on=rep == 4 and n == 8 and dn % 16 == 0 and chunks == nz == rep, dn=dn, nz=nz, nr=rep)
    ri, fi = lax.axis_index("rep"), lax.axis_index("fsdp")
    z, core = fi // 2, fi % 2
    scalars = jnp.stack([lengths[0], z, core, ri, ri * n + fi]).astype(jnp.int32)
    gather = lambda v: lax.all_gather(v, "fsdp", axis=0, tiled=True)
    group_cols = lambda v, j: jnp.concatenate([v[:, a * d + j * gw:a * d + (j + 1) * gw] for a in range(3)], axis=1)
    mats = jnp.stack([group_cols(triple_weight, j) for j in range(GROUPS)] + [output_weight])

    small = jnp.concatenate([first_gain, first_shift, second_gain, second_shift, output_bias, downward_bias, triple_bias, upward_bias])
    small = jnp.where(jnp.arange(n)[:, None] == fi, small[None], 0.0).astype(BF)

    if split["on"]:
        quarter = lax.dynamic_index_in_dim(mats, ri, 0, keepdims=False)
        far = jnp.stack([xor_permute(quarter, "fsdp", n, 2 * k) for k in range(1, nz)])
        sib_own = xor_permute(mats, "fsdp", n, 1)
        small = butterfly(small, "fsdp", n)
        near = [far] + [xor_permute(far, "rep", rep, j) for j in range(1, rep)]
        sibs = xor_permute(jnp.stack(near), "fsdp", n, 1)
        weights = [mats, sib_own] + near + [sibs]
        late_up, late_down, _ = lax.optimization_barrier((upward_weight, downward_weight, far[0, 0, 0]))
        wu, wd = gather(late_up), gather(late_down)
    else:
        small = butterfly(small, "fsdp", n)
        weights = [lax.all_gather(mats, "fsdp", axis=1, tiled=True)]
        wu, wd = gather(upward_weight), gather(downward_weight)

    small = small.astype(F32)
    par = small[:, :6 * dn].reshape(n, 6, dn).swapaxes(0, 1).reshape(6, d)
    par = jnp.pad(par, ((0, 2), (0, 0)))
    bias_t = small[:, 6 * dn:9 * dn].reshape(1, 3 * d)
    b3 = jnp.stack([group_cols(bias_t, j) for j in range(GROUPS)])
    bu = small[:, 9 * dn:].reshape(chunks, 1, d)

    *dwa, sm1, ao, ff = attention(split, scalars, block_input, cotangent, par, b3, weights)
    width = -(-rep * n // 128) * 128
    *dwf, smalls, norm_row, out, gx = ffn(split, scalars, block_input, cotangent, par, wu, bu, wd, ao, ff, sm1, width)

    norm_row = butterfly(butterfly(norm_row, "fsdp", n), "rep", rep)
    norms = norm_row[0, :rep * n]
    mean = jnp.mean(norms)
    factor_of = lambda at: jnp.minimum(1.0, mean / lax.dynamic_index_in_dim(norms, at, 0, keepdims=False)) / (rep * n)
    me = ri * n + fi
    factor = factor_of(me)

    if split["on"]:
        other = factor_of(me ^ 1)
        zh, zl, y, x = z // 2, z % 2, ri // 2, ri % 2
        places = dict(x=(3, x, "rep", rep, 1), y=(2, y, "rep", rep, 2), lo=(1, zl, "fsdp", n, 2), hi=(0, zh, "fsdp", n, 4))

        def hop(held, name):
            axis, bit, mesh_axis, size, flip = places[name]
            send = lax.dynamic_slice_in_dim(held, 1 - bit, 1, axis)
            got = xor_permute(send, mesh_axis, size, flip)
            keep = lax.dynamic_slice_in_dim(held, bit, 1, axis)
            return (keep.astype(F32) + got.astype(F32)).astype(BF)

        def paired(keep, send):
            got = xor_permute(send, "fsdp", n, 1)
            both = keep.astype(F32) * factor + got.astype(F32) * other
            return both.astype(BF).reshape(2, 2, 2, 2, dn, d)

        smalls = smalls * factor + xor_permute(smalls, "fsdp", n, 1) * other
        smalls = jnp.broadcast_to(smalls.astype(BF), (2, 2, 2, 2, SMALL, d))
        part_a = paired(dwa[0], dwa[1])
        part_u = paired(dwf[0], dwf[1])
        part_d = jnp.concatenate([paired(dwf[2], dwf[3]), smalls], axis=4)
        for name in ("x", "y", "lo"):
            part_a = hop(part_a, name)
        for name in ("y", "lo", "x"):
            part_u = hop(part_u, name)
        for name in ("lo", "x", "y"):
            part_d = hop(part_d, name)
        mine = hop(jnp.concatenate([part_a, part_u, part_d], axis=4), "hi").reshape(3 * dn + SMALL, d)
        smalls = mine[3 * dn:].astype(F32)
        mine = mine[:3 * dn]
        around = [mine] + [xor_permute(mine, "rep", rep, j) for j in range(1, rep)]
        flip = lambda bit, a, b: (jnp.where(bit == 1, b, a), jnp.where(bit == 1, a, b))
        a0, a1 = flip(x, around[0], around[1])
        a2, a3 = flip(x, around[2], around[3])
        a0, a2 = flip(y, a0, a2)
        a1, a3 = flip(y, a1, a3)
        final = jnp.stack([a0, a1, a2, a3]).astype(F32)
        g_att, g_up, g_down = final[:, :dn], final[:, dn:2 * dn], final[:, 2 * dn:].reshape(fn, d)
        smalls = smalls.reshape(SMALL, d)
    else:
        scale = lambda v: (v.astype(F32) * factor).astype(BF)
        shards = lambda v: v.reshape(v.shape[0], n, dn, d).swapaxes(0, 1).reshape(n, -1, d)
        pack = jnp.concatenate([scale(shards(dwa[0])), scale(shards(dwf[0])), scale(dwf[1].reshape(n, fn, d))], axis=1)
        mine = lax.psum_scatter(pack, "fsdp", scatter_dimension=0, tiled=True)[0]
        mine = lax.psum(mine, "rep").astype(F32)
        g_att = mine[:4 * dn].reshape(4, dn, d)
        g_up = mine[4 * dn:(4 + chunks) * dn].reshape(chunks, dn, d)
        g_down = mine[(4 + chunks) * dn:]
        smalls = lax.psum(scale(smalls), ("rep", "fsdp")).astype(F32)

    g_triple = jnp.concatenate([g_att[j, :, a * gw:(a + 1) * gw] for a in range(3) for j in range(GROUPS)], axis=1)
    g_upward = jnp.concatenate([g_up[j] for j in range(chunks)], axis=1)
    own = lambda v, width: lax.dynamic_slice_in_dim(v, fi * width, width, 0)
    g1, s1, g2, s2, bd = (own(smalls[i], dn) for i in range(5))
    b_triple = own(jnp.concatenate([smalls[5 + j, a * gw:(a + 1) * gw] for a in range(3) for j in range(GROUPS)]), 3 * dn)
    b_up = own(smalls[8:8 + chunks].reshape(-1), fn)
    return (out, gx, g1, s1, g2, s2, g_triple, b_triple, g_att[GROUPS], bd, g_upward, b_up, g_down, bd, norms)


def solution(mesh):
    rows = P(("rep", "fsdp"), None)
    vec, mat = P("fsdp"), P("fsdp", None)
    sizes = (mesh.shape["rep"], mesh.shape["fsdp"])
    return jax.shard_map(
        lambda *args: per_device(sizes, *args),
        mesh=mesh,
        in_specs=(rows, rows, P(("rep", "fsdp")), vec, vec, vec, vec, mat, vec, mat, vec, mat, vec, mat, vec),
        out_specs=(rows, rows, vec, vec, vec, vec, mat, vec, mat, vec, mat, vec, mat, vec, P()),
        check_vma=False,
    )
```

```python
import math
import numpy as np
import jax
import jax.numpy as jnp
from jax import lax
from jax.experimental import pallas as pl
from jax.experimental.pallas import tpu as pltpu
from jax.sharding import PartitionSpec as P

HEADS = 12
HEAD_DIM = 64
ROT = 16
EPS = 1e-05
MASKED = -1e30
BF = jnp.bfloat16
F32 = jnp.float32
GROUPS = 3
MIB = 1024 * 1024


def mm(a, b):
    return jnp.dot(a, b, preferred_element_type=F32)


def mm_rt(a, b):
    return lax.dot_general(a, b, (((1,), (1,)), ((), ())), preferred_element_type=F32)


def mm_lt(a, b):
    return lax.dot_general(a, b, (((0,), (0,)), ((), ())), preferred_element_type=F32)


def rotary_tables(rows, width):
    half = ROT // 2
    freq = np.exp(np.arange(half, dtype=np.float32) * np.float32(-2.0 * math.log(10000.0) / ROT))
    ang = np.arange(rows, dtype=np.float32)[:, None] * freq.astype(np.float32)[None, :]
    cos, sin = np.cos(ang), np.sin(ang)
    keep = np.ones((rows, HEAD_DIM), np.float32)
    up = np.zeros((rows, HEAD_DIM), np.float32)
    down = np.zeros((rows, HEAD_DIM), np.float32)
    keep[:, :half] = cos
    keep[:, half:ROT] = cos
    up[:, :half] = -sin
    down[:, half:ROT] = sin
    rep = width // HEAD_DIM
    return tuple(np.tile(t, (1, rep)).astype(np.float32) for t in (keep, up, down))


def norm_parts(values):
    centred = values - jnp.mean(values, axis=-1, keepdims=True)
    inverse = lax.rsqrt(jnp.mean(centred * centred, axis=-1, keepdims=True) + EPS)
    return centred * inverse, inverse


def norm_back(e, gain, normed, inverse):
    t = e * gain
    t_mean = jnp.mean(t, axis=-1, keepdims=True)
    cross = jnp.mean(t * normed, axis=-1, keepdims=True)
    return inverse * (t - t_mean - normed * cross)


SMALL = 16
BLOCK = 256
QKV_BIAS = 6
UP_BIAS = QKV_BIAS + GROUPS
VM = pl.BlockSpec(memory_space=pltpu.VMEM)
SM = pl.BlockSpec(memory_space=pltpu.SMEM)
ANY = pl.BlockSpec(memory_space=pl.ANY)


def block(i):
    return pl.ds(pl.multiple_of(i * BLOCK, BLOCK), BLOCK)


def params(mib):
    return pltpu.CompilerParams(vmem_limit_bytes=mib * MIB)


def valid_rows(i, seq):
    return (lax.broadcasted_iota(jnp.int32, (BLOCK, 1), 0) + i * BLOCK < seq).astype(F32)


def prepare_kernel(plan, waits, sc_ref, x_ref, g_ref, par_ref, up_ref, down_ref, *rest):
    n1, n1t, n2, n2t, gl, vec_out, token, pick, sems = rest[waits:]
    d = x_ref.shape[1]
    if plan["on"]:
        dn, rep = plan["dn"], sc_ref[3]
        cut = [pltpu.make_async_copy(up_ref.at[:, pl.ds(pl.multiple_of(rep * d, 128), d)], pick.at[0], sems.at[0]),
               pltpu.make_async_copy(down_ref.at[pl.ds(pl.multiple_of(rep * dn, 16), dn)], pick.at[1], sems.at[1])]

        @pl.when(pl.program_id(0) == 0)
        def _():
            for c in cut:
                c.start()

        @pl.when(pl.program_id(0) == pl.num_programs(0) - 1)
        def _():
            for c in cut:
                c.wait()

    token[...] = jnp.zeros_like(token)
    vec_out[...] = par_ref[...]
    normed, _ = norm_parts(x_ref[...].astype(F32))
    one = (normed * par_ref[0:1, :] + par_ref[1:2, :]).astype(BF)
    two = (normed * par_ref[2:3, :] + par_ref[3:4, :]).astype(BF)
    n1[...] = one
    n2[...] = two
    n1t[...] = one.astype(F32).T.astype(BF)
    n2t[...] = two.astype(F32).T.astype(BF)
    gl[...] = (g_ref[...].astype(F32) * valid_rows(pl.program_id(0), sc_ref[0])).astype(BF)


def prepare(plan, scalars, x, g, par, up, down, waits):
    rows, d = x.shape
    flat, turned = jax.ShapeDtypeStruct((rows, d), BF), jax.ShapeDtypeStruct((d, rows), BF)
    by_rows, by_cols = pl.BlockSpec((BLOCK, d), lambda i: (i, 0)), pl.BlockSpec((d, BLOCK), lambda i: (0, i))
    return pl.pallas_call(
        lambda *refs: prepare_kernel(plan, len(waits), *refs),
        grid_spec=pl.GridSpec(grid=(rows // BLOCK,), in_specs=[SM, by_rows, by_rows, pl.BlockSpec(par.shape, lambda i: (0, 0)), ANY, ANY] + [ANY] * len(waits),
                              out_specs=[by_rows, by_cols, by_rows, by_cols, by_rows, pl.BlockSpec(par.shape, lambda i: (0, 0)), pl.BlockSpec((1, d), lambda i: (0, 0)), pl.BlockSpec((2, plan["dn"], d), lambda i: (0, 0, 0))],
                              scratch_shapes=[pltpu.SemaphoreType.DMA((2,))]),
        out_shape=[flat, turned, flat, turned, flat, jax.ShapeDtypeStruct(par.shape, F32), jax.ShapeDtypeStruct((1, d), BF),
                   jax.ShapeDtypeStruct((2, plan["dn"], d), BF)], compiler_params=params(60), name="prepare",
        cost_estimate=pl.CostEstimate(flops=40 * rows * d, bytes_accessed=14 * rows * d, transcendentals=rows),
    )(scalars, x, g, par, up, down, *waits)


def attn_kernel(plan, first, base, sc_ref, n1, gl, b3_ref, keep_ref, up_ref, down_ref, *rest):
    nw = plan["pieces"] if first else 2
    w_refs, rest = rest[:nw], rest[nw:]
    d3, ctx_low, sm_ref, token, rest = rest[0].at[0], rest[1].at[0], rest[2].at[0], rest[3], rest[4:]
    token[...] = jnp.zeros_like(token)
    rows, d = n1.shape
    gw = d // GROUPS
    qb = BLOCK
    nb = rows // qb
    seq = sc_ref[0]
    if first:
        w_out, rest = rest[0], rest[1:]
    q_s, k_s, v_s, dc_s, ctx, dq, dk, dv, qm, km, vm, dcm, pall, dall = rest[:14]

    if first:
        w, sems = rest[14:]
        if plan["on"]:
            z, core, rep = sc_ref[1], sc_ref[2], sc_ref[3]
            dn, nz, nr = plan["dn"], plan["nz"], plan["nr"]
            own, sib, near, sibs = w_refs[0], w_refs[1], w_refs[2:2 + nr], w_refs[2 + nr]
            place = lambda zz, cc: pl.ds(pl.multiple_of((zz * 2 + cc) * dn, 16), dn)
            pairs = []
            for m in range(nr):
                pairs.append((own.at[m], w.at[m, place(z, core)]))
                pairs.append((sib.at[m], w.at[m, place(z, 1 - core)]))
            for j in range(nr):
                for k in range(1, nz):
                    m, zz = rep ^ j, z ^ k
                    pairs.append((near[j].at[k - 1], w.at[m, place(zz, core)]))
                    pairs.append((sibs.at[j, k - 1], w.at[m, place(zz, 1 - core)]))
        else:
            pairs = [(w_refs[0].at[m], w.at[m]) for m in range(GROUPS + 1)]
        copies = [pltpu.make_async_copy(a, b, sems.at[i]) for i, (a, b) in enumerate(pairs)]
        for c in copies:
            c.start()
        for c in copies:
            c.wait()
        back = pltpu.make_async_copy(w, w_out, sems.at[len(pairs)])
        back.start()
        w3, wo = w.at[0], w.at[GROUPS, 0:gw]
    else:
        w3, wo = w_refs[0].at[0], w_refs[1].at[0]
    half = ROT // 2

    def tables(r):
        return tuple(jnp.concatenate([t[r, :]] * (gw // 128), axis=1) for t in (keep_ref, up_ref, down_ref))

    def project(i, c):
        r = block(i)
        t = mm(n1[r, :], w3[...]) + b3_ref[pl.ds(QKV_BIAS + base + pl.program_id(0), 1), :]
        keep, up, down = tables(r)
        for at, ref, scale in ((0, q_s, HEAD_DIM ** -0.5), (1, k_s, None)):
            v = t[:, at * gw:(at + 1) * gw]
            low = (v * keep + pltpu.roll(v, gw - half, 1) * up + pltpu.roll(v, half, 1) * down).astype(BF)
            ref[r, :] = low if scale is None else (low.astype(F32) * scale).astype(BF)
        v_s[r, :] = t[:, 2 * gw:].astype(BF)
        dc_s[r, :] = mm_rt(gl[r, :], wo[...]).astype(BF)
        return c
    lax.fori_loop(0, nb, project, 0, unroll=True)

    key_bias = jnp.where(lax.broadcasted_iota(jnp.int32, (1, rows), 1) < seq, 0.0, MASKED).astype(F32)
    causal = lax.broadcasted_iota(jnp.int32, (qb, qb), 1) <= lax.broadcasted_iota(jnp.int32, (qb, qb), 0)

    heads = gw // HEAD_DIM

    def head(h, c):
        lane = lax.broadcasted_iota(jnp.int32, (1, gw), 1) // HEAD_DIM
        mask = jnp.where(lane == h, 1.0, 0.0).astype(BF)
        for ref, out in ((q_s, qm), (k_s, km), (v_s, vm), (dc_s, dcm)):
            out[h] = ref[...] * mask
        for i in range(nb):
            lo, kl = i * qb, (i + 1) * qb
            s = mm_rt(qm[h, lo:kl, :], k_s[:kl, :]) + key_bias[:, :kl]
            diag = jnp.where(causal, s[:, lo:], MASKED)
            s = diag if i == 0 else jnp.concatenate([s[:, :lo], diag], axis=1)
            dp = mm_rt(dcm[h, lo:kl, :], v_s[:kl, :])
            e = jnp.exp(s - jnp.max(s, axis=1, keepdims=True))
            p = e * (1.0 / jnp.sum(e, axis=1, keepdims=True))
            pall[h, lo:kl, :kl] = p.astype(BF)
            inner = jnp.sum(p * dp, axis=1, keepdims=True)
            dall[h, lo:kl, :kl] = (p * (dp - inner)).astype(BF)
        return c
    lax.fori_loop(0, heads, head, 0, unroll=2)
    for i in range(nb):
        lo, kl = i * qb, (i + 1) * qb
        ctx[lo:kl, :] = sum(mm(pall[h, lo:kl, :kl], vm[h, :kl, :]) for h in range(heads))
        dq[lo:kl, :] = sum(mm(dall[h, lo:kl, :kl], km[h, :kl, :]) for h in range(heads))
        dv[lo:kl, :] = sum(mm_lt(pall[h, lo:, lo:kl], dcm[h, lo:, :]) for h in range(heads))
        dk[lo:kl, :] = sum(mm_lt(dall[h, lo:, lo:kl], qm[h, lo:, :]) for h in range(heads))

    def finish(i, total):
        r = block(i)
        keep, up, down = tables(r)
        parts = []
        for ref, scale in ((dq, HEAD_DIM ** -0.5), (dk, 1.0)):
            v = ref[r, :] * scale
            parts.append(v * keep - pltpu.roll(v, gw - half, 1) * up - pltpu.roll(v, half, 1) * down)
        low = jnp.concatenate(parts + [dv[r, :]], axis=1).astype(BF)
        d3[r, :] = low
        ctx_low[r, :] = ctx[r, :].astype(BF)
        return total + jnp.sum(low.astype(F32), axis=0, keepdims=True)
    db3 = lax.fori_loop(0, nb, finish, jnp.zeros((1, d), F32), unroll=True)
    sm_ref[...] = jnp.broadcast_to(db3, sm_ref.shape)
    if first:
        back.wait()


def attention(plan, groups, scalars, n1, gl, b3, tables, weights):
    rows, d = n1.shape
    gw = d // GROUPS
    first, count, base = groups[0] == 0, len(groups), groups[0]
    plan = dict(plan, pieces=len(weights))
    whole = lambda *shape: pl.BlockSpec(shape, lambda j: (0,) * len(shape))
    stacked = lambda *shape: pl.BlockSpec((1,) + shape, lambda j: (j,) + (0,) * len(shape))
    out_shape = [jax.ShapeDtypeStruct((count, rows, d), BF), jax.ShapeDtypeStruct((count, rows, gw), BF), jax.ShapeDtypeStruct((count, 8, d), F32), jax.ShapeDtypeStruct((1, d), BF)]
    out_specs = [stacked(rows, d), stacked(rows, gw), stacked(8, d), whole(1, d)]
    heads = gw // HEAD_DIM
    scratch = [pltpu.VMEM((rows, gw), BF)] * 4 + [pltpu.VMEM((rows, gw), F32)] * 4
    scratch += [pltpu.VMEM((heads, rows, gw), BF)] * 4 + [pltpu.VMEM((heads, rows, rows), BF)] * 2
    if first:
        out_shape.append(jax.ShapeDtypeStruct((GROUPS + 1, d, d), BF))
        out_specs.append(ANY)
        scratch += [pltpu.VMEM((GROUPS + 1, d, d), BF), pltpu.SemaphoreType.DMA((64,))]
        w_specs = [ANY] * len(weights)
    else:
        weights = [weights[0], weights[0]]
        w_specs = [pl.BlockSpec((1, d, d), lambda j: (base + j, 0, 0)), pl.BlockSpec((1, gw, d), lambda j: (GROUPS, base + j, 0))]
    flops = count * (2 * rows * d * (d + gw) + 12 * HEADS // GROUPS * rows * rows * HEAD_DIM)
    return pl.pallas_call(
        lambda *refs: attn_kernel(plan, first, base, *refs),
        grid_spec=pl.GridSpec(
            grid=(count,),
            in_specs=[SM, whole(rows, d), whole(rows, d), whole(*b3.shape)] + [whole(rows, 128)] * 3 + w_specs,
            out_specs=out_specs, scratch_shapes=scratch),
        out_shape=out_shape, compiler_params=params(60), name="attend_first" if first else "attend_rest",
        cost_estimate=pl.CostEstimate(flops=4 * flops, bytes_accessed=8_000_000, transcendentals=count * HEADS * rows * rows // GROUPS),
    )(scalars, n1, gl, b3, *tables, *weights)


def write_halves(value, tmp, keep_ref, send_ref, core, dn):
    tmp[...] = value.astype(BF)
    for z in range(keep_ref.shape[0]):
        mine = pl.ds(pl.multiple_of((2 * z + core) * dn, 16), dn)
        other = pl.ds(pl.multiple_of((2 * z + 1 - core) * dn, 16), dn)
        keep_ref[z, 0] = tmp[mine, :]
        send_ref[z, 0] = tmp[other, :]


def closing_kernel(plan, sc_ref, x_ref, gl, n1t, par_ref, w, d3a, d3b, ctxa, ctxb, sma, smb, *rest):
    nd = 2 if plan["on"] else 1
    dw_refs, rest = rest[:nd], rest[nd:]
    sm_ref, ff_ref, gf, tmp = rest
    step = pl.program_id(0)
    rows, d = x_ref.shape
    nb = rows // BLOCK

    def store(dw):
        if plan["on"]:
            write_halves(dw, tmp, dw_refs[0], dw_refs[1], sc_ref[2], plan["dn"])
        else:
            dw_refs[0][0] = dw.astype(BF)
        return jnp.sum(dw * dw, axis=0, keepdims=True)

    def group(first, d3, db3):
        def body(i, c):
            r = block(i)
            part = mm_rt(d3[0, r, :], w[0])
            gf[r, :] = part if first else gf[r, :] + part
            return c
        lax.fori_loop(0, nb, body, 0, unroll=True)
        total = store(mm(n1t[...], d3[0])) + db3 * db3
        sm_ref[pl.ds(2 + step, 1), :] = db3
        sm_ref[5:6, :] = total if first else sm_ref[5:6, :] + total

    @pl.when(step == 0)
    def _():
        group(True, d3a, sma[0, 0:1, :])

    @pl.when(jnp.logical_and(step > 0, step < GROUPS))
    def _():
        group(False, d3b, smb[0, 0:1, :])

    @pl.when(step == GROUPS)
    def _():
        total = store(mm_lt(jnp.concatenate([ctxa[0]] + [ctxb[g] for g in range(GROUPS - 1)], axis=1), gl[...]))

        def back(i, c):
            r = block(i)
            normed, inverse = norm_parts(x_ref[r, :].astype(F32))
            e = gf[r, :]
            ff_ref[r, :] = norm_back(e, par_ref[0:1, :], normed, inverse)
            return (c[0] + jnp.sum(e * normed, axis=0, keepdims=True), c[1] + jnp.sum(e, axis=0, keepdims=True))
        zero = jnp.zeros((1, d), F32)
        dgain, dshift = lax.fori_loop(0, nb, back, (zero, zero), unroll=True)
        sm_ref[0:1, :] = dgain
        sm_ref[1:2, :] = dshift
        sm_ref[5:6, :] += total + dgain * dgain + dshift * dshift


def closing(plan, scalars, x, gl, n1t, par, w, d3a, d3b, ctxa, ctxb, sma, smb):
    rows, d = x.shape
    gw = d // GROUPS
    whole = lambda *shape: pl.BlockSpec(shape, lambda j: (0,) * len(shape))
    later = lambda *shape: pl.BlockSpec((1,) + shape, lambda j: (jnp.clip(j - 1, 0, GROUPS - 2),) + (0,) * len(shape))
    if plan["on"]:
        nz, dn = plan["nz"], plan["dn"]
        dw_specs = [pl.BlockSpec((nz, 1, dn, d), lambda j: (0, j, 0, 0))] * 2
        dw_shapes = [jax.ShapeDtypeStruct((nz, GROUPS + 1, dn, d), BF)] * 2
    else:
        dw_specs = [pl.BlockSpec((1, d, d), lambda j: (j, 0, 0))]
        dw_shapes = [jax.ShapeDtypeStruct((GROUPS + 1, d, d), BF)]
    return pl.pallas_call(
        lambda *refs: closing_kernel(plan, *refs),
        grid_spec=pl.GridSpec(
            grid=(GROUPS + 1,),
            in_specs=[SM, whole(rows, d), whole(rows, d), whole(d, rows), whole(*par.shape),
                      pl.BlockSpec((1, d, d), lambda j: (jnp.minimum(j, GROUPS - 1), 0, 0)),
                      whole(1, rows, d), later(rows, d), whole(1, rows, gw), whole(GROUPS - 1, rows, gw), whole(1, 8, d), later(8, d)],
            out_specs=dw_specs + [whole(8, d), whole(rows, d)],
            scratch_shapes=[pltpu.VMEM((rows, d), F32), pltpu.VMEM((d, d), BF)],
        ),
        out_shape=dw_shapes + [jax.ShapeDtypeStruct((8, d), F32), jax.ShapeDtypeStruct((rows, d), F32)],
        compiler_params=params(60), name="closing",
        cost_estimate=pl.CostEstimate(flops=4 * rows * d * 7 * d, bytes_accessed=8_000_000, transcendentals=rows),
    )(scalars, x, gl, n1t, par, w, d3a, d3b, ctxa, ctxb, sma, smb)


ERF_P = 0.3275911
ERF_A = (0.254829592, -0.284496736, 1.421413741, -1.453152027, 1.061405429)


def gelu_parts(u):
    z = jnp.abs(u) * (2.0 ** -0.5)
    t = 1.0 / (1.0 + ERF_P * z)
    bell = jnp.exp(-0.5 * (u * u))
    a1, a2, a3, a4, a5 = (0.5 * a for a in ERF_A)
    tail = ((((a5 * t + a4) * t + a3) * t + a2) * t + a1) * t * bell
    cdf = jnp.where(u >= 0.0, 1.0 - tail, tail)
    return u * cdf, cdf + u * bell * (1.0 / math.sqrt(2.0 * math.pi))


def ffn_kernel(plan, sc_ref, x_ref, gl, n2, n2t, par_ref, ff_ref, sm1_ref, *rest):
    nw = plan["pieces"]
    w_refs, rest = rest[:nw], rest[nw:]
    nd = 4 if plan["on"] else 2
    dw_refs, rest = rest[:nd], rest[nd:]
    sm_ref, norm_ref, act_ref, wd_ref, gx_ref = rest[:5]
    wu_s, wd_s, gs, gup, sq, tmp, x_s, ff_s, up_sems, down_sems, late_sems = rest[5:]
    late = [pltpu.make_async_copy(x_ref, x_s, late_sems.at[0]), pltpu.make_async_copy(ff_ref, ff_s, late_sems.at[1])]
    step = pl.program_id(0)
    last = pl.num_programs(0) - 1
    rows, d = x_ref.shape
    fc = d
    nb = rows // BLOCK

    @pl.when(step == 0)
    def _():
        if plan["on"]:
            z, core, rep = sc_ref[1], sc_ref[2], sc_ref[3]
            dn, nz, nr = plan["dn"], plan["nz"], plan["nr"]
            own_up, own_down, sib_up, sib_down = w_refs[:4]
            near, sibs = w_refs[4:4 + nr], w_refs[4 + nr]

            def up(src, m, zz, cc):
                dst = wu_s.at[m, pl.ds(pl.multiple_of((zz * 2 + cc) * dn, 16), dn)]
                pltpu.make_async_copy(src, dst, up_sems.at[m]).start()

            def down(src, b, zz, cc):
                dst = wd_s.at[zz, pl.ds(pl.multiple_of((cc * nr + b) * dn, 16), dn)]
                pltpu.make_async_copy(src, dst, down_sems.at[zz]).start()
            for m in range(nr):
                cols, part = pl.ds(m * d, d), pl.ds(m * dn, dn)
                up(own_up.at[:, cols], m, z, core)
                up(sib_up.at[:, cols], m, z, 1 - core)
                down(own_down.at[part], m, z, core)
                down(sib_down.at[part], m, z, 1 - core)
            for j in range(nr):
                for k in range(1, nz):
                    up(near[j].at[k - 1, 0], rep ^ j, z ^ k, core)
                    up(sibs.at[j, k - 1, 0], rep ^ j, z ^ k, 1 - core)
                    down(near[j].at[k - 1, 1], rep ^ j, z ^ k, core)
                    down(sibs.at[j, k - 1, 1], rep ^ j, z ^ k, 1 - core)
        else:
            for m in range(wu_s.shape[0]):
                pltpu.make_async_copy(w_refs[0].at[m], wu_s.at[m], up_sems.at[m]).start()
                pltpu.make_async_copy(w_refs[1].at[m], wd_s.at[m], down_sems.at[m]).start()
        for c in late:
            c.start()
        gs[...] = jnp.zeros_like(gs)
        sq[...] = jnp.zeros_like(sq)
        sm_ref[...] = jnp.zeros_like(sm_ref)

    pltpu.make_async_copy(wu_s.at[step], wu_s.at[step], up_sems.at[step]).wait()
    pltpu.make_async_copy(wd_s.at[step], wd_s.at[step], down_sems.at[step]).wait()
    wu, wd = wu_s.at[step], wd_s.at[step]
    wd_ref[0] = wd[...]

    def rows_step(i, dbu):
        r = block(i)
        u = mm(n2[r, :], wu[...]) + par_ref[pl.ds(UP_BIAS + step, 1), :]
        da = mm_rt(gl[r, :], wd[...])
        a, slope = gelu_parts(u)
        act_ref[0, r, :] = a.astype(BF)
        gu = (da * slope).astype(BF)
        gup[r, :] = gu
        gs[r, :] += mm_rt(gu, wu[...])
        return dbu + jnp.sum(gu.astype(F32), axis=0, keepdims=True)
    dbu = lax.fori_loop(0, nb, rows_step, jnp.zeros((1, fc), F32), unroll=True)
    sm_ref[pl.ds(8 + step, 1), :] = dbu

    dwu = mm(n2t[...], gup[...])
    total = jnp.sum(dwu * dwu, axis=0, keepdims=True) + dbu * dbu
    if plan["on"]:
        write_halves(dwu, tmp, dw_refs[0], dw_refs[1], sc_ref[2], plan["dn"])
    else:
        dw_refs[0][0] = dwu.astype(BF)
    dwd = mm_lt(act_ref[0], gl[...])
    total += jnp.sum(dwd * dwd, axis=0, keepdims=True)
    if plan["on"]:
        tmp[...] = dwd.astype(BF)
        core, dn, nr = sc_ref[2], plan["dn"], plan["nr"]
        for m in range(nr):
            dw_refs[2][0, m] = tmp[pl.ds(pl.multiple_of((core * nr + m) * dn, 16), dn), :]
            dw_refs[3][0, m] = tmp[pl.ds(pl.multiple_of(((1 - core) * nr + m) * dn, 16), dn), :]
    else:
        dw_refs[1][0] = dwd.astype(BF)
    sq[...] += total

    @pl.when(step == last)
    def _():
        for c in late:
            c.wait()

        def back(i, c):
            r = block(i)
            normed, inverse = norm_parts(x_s[r, :].astype(F32))
            e = gs[r, :]
            grad_rows = gl[r, :].astype(F32)
            gx_ref[r, :] = (grad_rows + ff_s[r, :] + norm_back(e, par_ref[2:3, :], normed, inverse)).astype(BF)
            return (c[0] + jnp.sum(e * normed, axis=0, keepdims=True), c[1] + jnp.sum(e, axis=0, keepdims=True),
                    c[2] + jnp.sum(grad_rows, axis=0, keepdims=True))
        zero = jnp.zeros((1, d), F32)
        dgain, dshift, dbd = lax.fori_loop(0, nb, back, (zero, zero, zero), unroll=True)
        sm_ref[0:2, :] = sm1_ref[0:2, :]
        sm_ref[2:3, :] = dgain
        sm_ref[3:4, :] = dshift
        sm_ref[4:5, :] = dbd
        sm_ref[5:8, :] = sm1_ref[2:5, :]
        final = sq[...] + sm1_ref[5:6, :] + dgain * dgain + dshift * dshift + 2.0 * dbd * dbd
        own = jnp.sqrt(jnp.sum(final, axis=1, keepdims=True))
        here = lax.broadcasted_iota(jnp.int32, norm_ref.shape, 1) == sc_ref[4]
        norm_ref[...] = jnp.where(here, own, 0.0)


def ffn(plan, chunks, scalars, x, gl, n2, n2t, par, ff, sm1, weights, norm_width):
    rows, d = x.shape
    plan = dict(plan, pieces=len(weights))
    whole = lambda *shape: pl.BlockSpec(shape, lambda j: (0,) * len(shape))
    if plan["on"]:
        nz, dn, nr = plan["nz"], plan["dn"], plan["nr"]
        dw_specs = [pl.BlockSpec((nz, 1, dn, d), lambda j: (0, j, 0, 0))] * 2 + [pl.BlockSpec((1, nr, dn, d), lambda j: (j, 0, 0, 0))] * 2
        dw_shapes = [jax.ShapeDtypeStruct((nz, chunks, dn, d), BF)] * 2 + [jax.ShapeDtypeStruct((nz, nr, dn, d), BF)] * 2
    else:
        dw_specs = [pl.BlockSpec((1, d, d), lambda j: (j, 0, 0))] * 2
        dw_shapes = [jax.ShapeDtypeStruct((chunks, d, d), BF)] * 2
    return pl.pallas_call(
        lambda *refs: ffn_kernel(plan, *refs),
        grid_spec=pl.GridSpec(
            grid=(chunks,),
            in_specs=[SM, ANY, whole(rows, d), whole(rows, d), whole(d, rows), whole(*par.shape), ANY, whole(8, d)] + [ANY] * len(weights),
            out_specs=dw_specs + [whole(SMALL, d), whole(1, norm_width), pl.BlockSpec((1, rows, d), lambda j: (j, 0, 0)),
                                  pl.BlockSpec((1, d, d), lambda j: (j, 0, 0)), whole(rows, d)],
            scratch_shapes=[
                pltpu.VMEM((chunks, d, d), BF), pltpu.VMEM((chunks, d, d), BF), pltpu.VMEM((rows, d), F32), pltpu.VMEM((rows, d), BF),
                pltpu.VMEM((1, d), F32), pltpu.VMEM((d, d), BF), pltpu.VMEM((rows, d), BF), pltpu.VMEM((rows, d), F32),
                pltpu.SemaphoreType.DMA((chunks,)), pltpu.SemaphoreType.DMA((chunks,)), pltpu.SemaphoreType.DMA((2,)),
            ],
        ),
        out_shape=dw_shapes + [
            jax.ShapeDtypeStruct((SMALL, d), F32), jax.ShapeDtypeStruct((1, norm_width), F32),
            jax.ShapeDtypeStruct((chunks, rows, d), BF), jax.ShapeDtypeStruct((chunks, d, d), BF), jax.ShapeDtypeStruct((rows, d), BF),
        ],
        compiler_params=params(60), name="feedforward",
        cost_estimate=pl.CostEstimate(flops=2 * 5 * rows * d * d * chunks * 2, bytes_accessed=40_000_000, transcendentals=rows * d * chunks),
    )(scalars, x, gl, n2, n2t, par, ff, sm1, *weights)


def output_kernel(sc_ref, x_ref, par_ref, token, wo, wd, act, *rest):
    ctxs, out_ref = rest[:2], rest[2]
    d = x_ref.shape[1]
    gw = d // GROUPS
    total = x_ref[...].astype(F32) + par_ref[4:5, :] + par_ref[5:6, :]
    for g in range(GROUPS):
        ctx = ctxs[0][0] if g == 0 else ctxs[1][g - 1]
        total += mm(ctx, wo[0, g * gw:(g + 1) * gw, :])
    for j in range(wd.shape[0]):
        total += mm(act[j], wd[j])
    out_ref[...] = (total * valid_rows(pl.program_id(0), sc_ref[0])).astype(BF)


def output(scalars, x, par, token, w, wd, act, ctxs):
    rows, d = x.shape
    gw = d // GROUPS
    chunks = wd.shape[0]
    return pl.pallas_call(
        output_kernel,
        grid_spec=pl.GridSpec(
            grid=(rows // BLOCK,),
            in_specs=[SM, pl.BlockSpec((BLOCK, d), lambda i: (i, 0)), pl.BlockSpec(par.shape, lambda i: (0, 0)), pl.BlockSpec(token.shape, lambda i: (0, 0)),
                      pl.BlockSpec((1, d, d), lambda i: (GROUPS, 0, 0)), pl.BlockSpec((chunks, d, d), lambda i: (0, 0, 0)),
                      pl.BlockSpec((chunks, BLOCK, d), lambda i: (0, i, 0))] + [pl.BlockSpec((1, BLOCK, gw), lambda i: (0, i, 0)), pl.BlockSpec((GROUPS - 1, BLOCK, gw), lambda i: (0, i, 0))],
            out_specs=pl.BlockSpec((BLOCK, d), lambda i: (i, 0)),
        ),
        out_shape=jax.ShapeDtypeStruct((rows, d), BF),
        compiler_params=params(60), name="output",
        cost_estimate=pl.CostEstimate(flops=2 * rows * d * d * (chunks + 1), bytes_accessed=18_000_000, transcendentals=0),
    )(scalars, x, par, token, w, wd, act, *ctxs)


def spread(rows_ref, lane):
    norms = rows_ref
    at = lax.broadcasted_iota(jnp.int32, norms.shape, 1)
    own = jnp.sum(jnp.where(at == lane, norms, 0.0), axis=1, keepdims=True)
    return own


def mix_kernel(seqs, sending, sc_ref, r0, r1, ak, ag, uk, ug, dk, dg, sm, smg, token, a_out, u_out, d_out, norm_out):
    norms = r0[...] + r1[...]
    norm_out[...] = norms
    mean = jnp.sum(norms, axis=1, keepdims=True) * (1.0 / seqs)
    me = sc_ref[4]
    factor = jnp.minimum(1.0, mean / spread(norms, me)) * (1.0 / seqs)
    other = jnp.minimum(1.0, mean / spread(norms, me ^ 1)) * (1.0 / seqs)
    mixed = lambda k, g: k.astype(F32) * factor + g.astype(F32) * other
    a_out[...] = mixed(ak[...].reshape(-1, ak.shape[-1]), ag[...].reshape(-1, ag.shape[-1])).astype(BF).reshape(a_out.shape)
    u_out[...] = mixed(uk[...].reshape(-1, uk.shape[-1]), ug[...].reshape(-1, ug.shape[-1])).astype(BF).reshape(u_out.shape)
    dn = dk.shape[4]
    small = mixed(sm[...], smg[...]).astype(BF)
    for x in range(2):
        d_out[0, 0, 0, x, :dn] = mixed(dk[0, 0, 0, x], dg[0, 0, 0, x]).astype(BF)
        d_out[0, 0, 0, x, dn:] = small


def mix(seqs, sending, scalars, norm_rows, halves, smalls, token):
    flip = 1 if sending else 0
    dn, d = halves[0].shape[2:]
    whole = lambda *shape: pl.BlockSpec(shape, lambda i, sc: (0,) * len(shape))
    xb, yb, lob = (lambda sc: flip ^ (sc[3] % 2)), (lambda sc: flip ^ (sc[3] // 2)), (lambda sc: flip ^ (sc[1] % 2))
    a_in = pl.BlockSpec((1, 2, 1, dn, d), lambda i, sc: (i, 0, xb(sc), 0, 0))
    u_in = pl.BlockSpec((1, 1, 2, dn, d), lambda i, sc: (i, yb(sc), 0, 0, 0))
    d_in = pl.BlockSpec((1, 1, 1, 2, dn, d), lambda i, sc: (i // 2, lob(sc), i % 2, 0, 0, 0))
    ak, ag, uk, ug = (v.reshape(4, 2, 2, dn, d) for v in halves[:4])
    dk, dg = (v.reshape(2, 2, 2, 2, dn, d) for v in halves[4:])
    width = norm_rows[0].shape[1]
    a, u, dd, norms = pl.pallas_call(
        lambda *refs: mix_kernel(seqs, sending, *refs),
        grid_spec=pltpu.PrefetchScalarGridSpec(
            num_scalar_prefetch=1, grid=(4,),
            in_specs=[whole(1, width)] * 2 + [a_in, a_in, u_in, u_in, d_in, d_in, whole(SMALL, d), whole(SMALL, d), whole(*token.shape)],
            out_specs=[pl.BlockSpec((1, 2, 1, dn, d), lambda i, sc: (i, 0, 0, 0, 0)), pl.BlockSpec((1, 1, 2, dn, d), lambda i, sc: (i, 0, 0, 0, 0)),
                       pl.BlockSpec((1, 1, 1, 2, dn + SMALL, d), lambda i, sc: (i // 2, 0, i % 2, 0, 0, 0)), whole(1, width)],
        ),
        out_shape=[jax.ShapeDtypeStruct((4, 2, 1, dn, d), BF), jax.ShapeDtypeStruct((4, 1, 2, dn, d), BF),
                   jax.ShapeDtypeStruct((2, 1, 2, 2, dn + SMALL, d), BF), jax.ShapeDtypeStruct((1, width), F32)],
        compiler_params=params(60), name="mix_send" if sending else "mix_keep",
        cost_estimate=pl.CostEstimate(flops=16_000_000, bytes_accessed=10_600_000, transcendentals=0),
    )(scalars, *norm_rows, ak, ag, uk, ug, dk, dg, *smalls, token)
    return a.reshape(2, 2, 2, 1, dn, d), u.reshape(2, 2, 1, 2, dn, d), dd, norms


AXES = dict(hi=0, lo=1, y=2, x=3)


def side(name, sc, flip):
    bit = {"hi": sc[1] // 2, "lo": sc[1] % 2, "y": sc[3] // 2, "x": sc[3] % 2}[name]
    return flip ^ bit


def fold_kernel(sc_ref, ms, gs, mk, gk, send, keep):
    d = ms.shape[-1]
    add = lambda a, b, out: (a[...].reshape(-1, d).astype(F32) + b[...].reshape(-1, d).astype(F32)).astype(BF).reshape(out.shape)
    send[...] = add(ms, gs, send)
    keep[...] = add(mk, gk, keep)


def fold(scalars, name, mine, got):
    axis = AXES[name]
    shape = mine.shape
    blk = (1,) + tuple(1 if i == axis else s for i, s in enumerate(shape) if i > 0)
    spec = lambda flip: pl.BlockSpec(blk, lambda i, sc: (i,) + tuple(side(name, sc, flip) if k == axis else 0 for k in range(1, 6)))
    out = pl.BlockSpec(blk, lambda i, sc: (i, 0, 0, 0, 0, 0))
    half = jax.ShapeDtypeStruct((shape[0],) + blk[1:], BF)
    return pl.pallas_call(
        fold_kernel,
        grid_spec=pltpu.PrefetchScalarGridSpec(num_scalar_prefetch=1, grid=(shape[0],), in_specs=[spec(1), spec(1), spec(0), spec(0)], out_specs=[out, out]),
        out_shape=[half, half], compiler_params=params(16), name="fold_" + name,
        cost_estimate=pl.CostEstimate(flops=mine.size, bytes_accessed=6 * mine.size, transcendentals=0),
    )(scalars, mine, got, mine, got)


def last_fold_kernel(sc_ref, *refs):
    ins, (send, keep) = refs[:12], refs[12:]
    at = 0
    for p in range(3):
        ms, gs, mk, gk = ins[4 * p:4 * p + 4]
        rows = ms.shape[4]
        for a, b, out in ((ms, gs, send), (mk, gk, keep)):
            out[at:at + rows, :] = (a[0, 0, 0, 0].astype(F32) + b[0, 0, 0, 0].astype(F32)).astype(BF)
        at += rows


def last_fold(scalars, parts):
    specs, args, total = [], [], 0
    for mine, got in parts:
        blk = (1,) + mine.shape[1:]
        spec = lambda flip, blk=blk: pl.BlockSpec(blk, lambda i, sc: (side("hi", sc, flip), 0, 0, 0, 0, 0))
        specs += [spec(1), spec(1), spec(0), spec(0)]
        args += [mine, got, mine, got]
        total += mine.shape[4]
    d = parts[0][0].shape[5]
    out = pl.BlockSpec((total, d), lambda i, sc: (0, 0))
    half = jax.ShapeDtypeStruct((total, d), BF)
    return pl.pallas_call(
        last_fold_kernel,
        grid_spec=pltpu.PrefetchScalarGridSpec(num_scalar_prefetch=1, grid=(1,), in_specs=specs, out_specs=[out, out]),
        out_shape=[half, half], compiler_params=params(16), name="last_fold",
        cost_estimate=pl.CostEstimate(flops=2 * total * d, bytes_accessed=12 * total * d, transcendentals=0),
    )(scalars, *args)


def xor_permute(value, axis, size, bit):
    return lax.ppermute(value, axis, [(i, i ^ bit) for i in range(size)])


def butterfly(value, axis, size):
    if size & (size - 1):
        return lax.psum(value, axis)
    bit = 1
    while bit < size:
        value = value + xor_permute(value, axis, size, bit)
        bit *= 2
    return value


def after(value, other):
    return value + other[(slice(0, 1),) * other.ndim].reshape((1,) * value.ndim).astype(value.dtype) * 0


def per_device(sizes, block_input, cotangent, lengths, first_gain, first_shift, second_gain, second_shift, triple_weight, triple_bias,
               output_weight, output_bias, upward_weight, upward_bias, downward_weight, downward_bias):
    rep, n = sizes
    rows, d = block_input.shape
    dn, fn = first_gain.shape[0], upward_bias.shape[0]
    gw = d // GROUPS
    chunks = fn * n // d
    nz = n // 2
    plan = dict(on=rep == 4 and n == 8 and dn % 16 == 0 and chunks == nz == rep, dn=dn, nz=nz, nr=rep)
    ri, fi = lax.axis_index("rep"), lax.axis_index("fsdp")
    z, core = fi // 2, fi % 2
    me = ri * n + fi
    scalars = jnp.stack([lengths[0], z, core, ri, me]).astype(jnp.int32)
    group_cols = lambda v, j: jnp.concatenate([v[:, a * d + j * gw:a * d + (j + 1) * gw] for a in range(3)], axis=1)
    mats = jnp.stack([group_cols(triple_weight, j) for j in range(GROUPS)] + [output_weight])
    small = [first_gain, first_shift, second_gain, second_shift, output_bias, downward_bias, triple_bias, upward_bias]
    wide_row = max(v.shape[0] for v in small)
    low = jnp.asarray(-jnp.inf, BF)
    small = [lax.pad(v.reshape(1, -1), low, ((i, 7 - i, 0), (0, wide_row - v.shape[0], 0))) for i, v in enumerate(small)]
    while len(small) > 1:
        small = [jnp.maximum(a, b) for a, b in zip(small[::2], small[1::2])]
    small = jnp.maximum(small[0], jnp.asarray(-1e4, BF))
    small = jnp.where(jnp.arange(n)[:, None, None] == fi, small[None], 0.0).astype(BF)

    along_z = lambda v: [xor_permute(v, "fsdp", n, 2 * k) for k in range(1, nz)]
    along_rep = lambda v: [xor_permute(v, "rep", rep, j) for j in range(1, rep)]
    to_core = lambda v: xor_permute(v, "fsdp", n, 1)

    def unpack(small):
        small = small.astype(F32)
        par = small[:, :6, :dn].swapaxes(0, 1).reshape(6, d)
        bias_t = small[:, 6, :3 * dn].reshape(1, 3 * d)
        vecs = jnp.concatenate([par] + [group_cols(bias_t, j) for j in range(GROUPS)] + [small[:, 7, :fn].reshape(chunks, d)])
        return jnp.pad(vecs, ((0, -vecs.shape[0] % 8), (0, 0)))

    if plan["on"]:
        quarter = lax.dynamic_index_in_dim(mats, ri, 0, keepdims=False)
        small = small + to_core(small)
        far = along_z(quarter)
        a, b, c = along_z(small)
        small = (small + a) + (b + c)
        sib_own = to_core(mats)
        wide_own = [upward_weight, downward_weight, to_core(upward_weight), to_core(downward_weight)]
        n1, n1t, n2, n2t, gl, par, ready, pick = prepare(plan, scalars, block_input, cotangent, unpack(small), upward_weight, downward_weight, [sib_own] + wide_own[2:])
        far = jnp.stack(far) + ready
        near = [far] + along_rep(far)
    else:
        small = butterfly(small, "fsdp", n)
        weights = [lax.all_gather(mats, "fsdp", axis=1, tiled=True)]
        n1, n1t, n2, n2t, gl, par, ready, _ = prepare(plan, scalars, block_input, cotangent, unpack(small), upward_weight, downward_weight, [])
    tables = [jnp.asarray(t) for t in rotary_tables(rows, 128)]

    if plan["on"]:
        wide_far = jnp.stack(along_z(pick))
        weights = [mats, sib_own] + near + [to_core(jnp.stack(near))]
    d3a, ctxa, sma, token_a, w = attention(plan, (0,), scalars, n1, gl, par, tables, weights)
    if plan["on"]:
        wide_far = wide_far + token_a
        wide_near = [wide_far] + along_rep(wide_far)
    d3b, ctxb, smb, token_b = attention(plan, (1, 2), scalars, n1, gl, par, tables, [w])
    if plan["on"]:
        wide_sibs = to_core(jnp.stack(wide_near) + token_b)
        wide_weights = wide_own + wide_near + [wide_sibs]
    else:
        up = lax.all_gather(upward_weight, "fsdp", axis=0, tiled=True)
        down = lax.all_gather(downward_weight, "fsdp", axis=0, tiled=True)
        wide_weights = [jnp.stack([up[:, j * d:(j + 1) * d] for j in range(chunks)]), down.reshape(chunks, d, d)]
    *dwa, sm1, ff = closing(plan, scalars, block_input, gl, n1t, par, w, d3a, d3b, ctxa, ctxb, sma, smb)
    width = -(-rep * n // 128) * 128
    *dwf, smalls, norm_row, act, wd, gx = ffn(plan, chunks, scalars, block_input, gl, n2, n2t, par, ff, sm1, wide_weights, width)

    if plan["on"]:
        a, b, c = along_z(norm_row)
        norm_row = (norm_row + a) + (b + c)
        a, b, c = along_rep(norm_row)
        norm_row = (norm_row + a) + (b + c)
        norm_rows = (norm_row, to_core(norm_row))
        halves = []
        for keep, send in ((dwa[0], dwa[1]), (dwf[0], dwf[1]), (dwf[2], dwf[3])):
            halves += [keep, to_core(send)]
        pair = (smalls, to_core(smalls))
        steps = dict(x=("rep", rep, 1), y=("rep", rep, 2), lo=("fsdp", n, 2), hi=("fsdp", n, 4))
        move = lambda v, name: xor_permute(v, *steps[name])
        *sends, norm_row = mix(rep * n, True, scalars, norm_rows, halves, pair, ready)
        norms = norm_row[0, :rep * n]
        *mines, token = mix(rep * n, False, scalars, norm_rows, halves, pair, norm_row)
        out = output(scalars, block_input, par, token, w, wd, act, (ctxa, ctxb))
        parts = []
        for send, mine, order in zip(sends, mines, (("x", "y", "lo"), ("y", "lo", "x"), ("lo", "x", "y"))):
            got = move(send, order[0])
            for name in order[1:]:
                send, mine = fold(scalars, name, mine, got)
                got = move(send, name)
            parts.append((mine, got))
        send, mine = last_fold(scalars, parts)
        got = move(send, "hi")
        mine = (mine.astype(F32) + got.astype(F32)).astype(BF)
        x, y = ri % 2, ri // 2
        smalls = mine[3 * dn:].astype(F32)
        mine = mine[:3 * dn]
        around = [mine] + along_rep(mine)
        flip = lambda bit, a, b: (jnp.where(bit == 1, b, a), jnp.where(bit == 1, a, b))
        a0, a1 = flip(x, around[0], around[1])
        a2, a3 = flip(x, around[2], around[3])
        a0, a2 = flip(y, a0, a2)
        a1, a3 = flip(y, a1, a3)
        final = jnp.stack([a0, a1, a2, a3]).astype(F32)
        g_att, g_up, g_down = final[:, :dn], final[:, dn:2 * dn], final[:, 2 * dn:].reshape(fn, d)
        smalls = smalls.reshape(SMALL, d)
    else:
        norms = butterfly(butterfly(norm_row, "fsdp", n), "rep", rep)[0, :rep * n]
        factor = jnp.minimum(1.0, jnp.mean(norms) / lax.dynamic_index_in_dim(norms, me, 0, keepdims=False)) / (rep * n)
        out = output(scalars, block_input, par, ready, w, wd, act, (ctxa, ctxb))
        scale = lambda v: (v.astype(F32) * factor).astype(BF)
        shards = lambda v: v.reshape(v.shape[0], n, dn, d).swapaxes(0, 1).reshape(n, -1, d)
        pack = jnp.concatenate([scale(shards(dwa[0])), scale(shards(dwf[0])), scale(dwf[1].reshape(n, fn, d))], axis=1)
        mine = lax.psum_scatter(pack, "fsdp", scatter_dimension=0, tiled=True)[0]
        mine = lax.psum(mine, "rep").astype(F32)
        g_att = mine[:4 * dn].reshape(4, dn, d)
        g_up = mine[4 * dn:(4 + chunks) * dn].reshape(chunks, dn, d)
        g_down = mine[(4 + chunks) * dn:]
        smalls = lax.psum(scale(smalls), ("rep", "fsdp")).astype(F32)

    g_triple = jnp.concatenate([g_att[j, :, a * gw:(a + 1) * gw] for a in range(3) for j in range(GROUPS)], axis=1)
    g_upward = jnp.concatenate([g_up[j] for j in range(chunks)], axis=1)
    own = lambda v, width: lax.dynamic_slice_in_dim(v, fi * width, width, 0)
    g1, s1, g2, s2, bd = (own(smalls[i], dn) for i in range(5))
    b_triple = own(jnp.concatenate([smalls[5 + j, a * gw:(a + 1) * gw] for a in range(3) for j in range(GROUPS)]), 3 * dn)
    b_up = own(smalls[8:8 + chunks].reshape(-1), fn)
    return (out, gx, g1, s1, g2, s2, g_triple, b_triple, g_att[GROUPS], bd, g_upward, b_up, g_down, bd, norms)


def solution(mesh):
    rows = P(("rep", "fsdp"), None)
    vec, mat = P("fsdp"), P("fsdp", None)
    sizes = (mesh.shape["rep"], mesh.shape["fsdp"])
    return jax.shard_map(
        lambda *args: per_device(sizes, *args),
        mesh=mesh,
        in_specs=(rows, rows, P(("rep", "fsdp")), vec, vec, vec, vec, mat, vec, mat, vec, mat, vec, mat, vec),
        out_specs=(rows, rows, vec, vec, vec, vec, mat, vec, mat, vec, mat, vec, mat, vec, P()),
        check_vma=False,
    )
```

```python
import math
import numpy as np
import jax
import jax.numpy as jnp
from jax import lax
from jax.experimental import pallas as pl
from jax.experimental.pallas import tpu as pltpu
from jax.sharding import PartitionSpec as P

HEADS = 12
HEAD_DIM = 64
ROT = 16
EPS = 1e-05
MASKED = -1e30
BF = jnp.bfloat16
F32 = jnp.float32
GROUPS = 3
MIB = 1024 * 1024


def mm(a, b):
    return jnp.dot(a, b, preferred_element_type=F32)


def mm_rt(a, b):
    return lax.dot_general(a, b, (((1,), (1,)), ((), ())), preferred_element_type=F32)


def mm_lt(a, b):
    return lax.dot_general(a, b, (((0,), (0,)), ((), ())), preferred_element_type=F32)


def rotary_tables(rows, width):
    half = ROT // 2
    freq = np.exp(np.arange(half, dtype=np.float32) * np.float32(-2.0 * math.log(10000.0) / ROT))
    ang = np.arange(rows, dtype=np.float32)[:, None] * freq.astype(np.float32)[None, :]
    cos, sin = np.cos(ang), np.sin(ang)
    keep = np.ones((rows, HEAD_DIM), np.float32)
    up = np.zeros((rows, HEAD_DIM), np.float32)
    down = np.zeros((rows, HEAD_DIM), np.float32)
    keep[:, :half] = cos
    keep[:, half:ROT] = cos
    up[:, :half] = -sin
    down[:, half:ROT] = sin
    rep = width // HEAD_DIM
    return tuple(np.tile(t, (1, rep)).astype(np.float32) for t in (keep, up, down))


def norm_parts(values):
    centred = values - jnp.mean(values, axis=-1, keepdims=True)
    inverse = lax.rsqrt(jnp.mean(centred * centred, axis=-1, keepdims=True) + EPS)
    return centred * inverse, inverse


def norm_back(e, gain, normed, inverse):
    t = e * gain
    t_mean = jnp.mean(t, axis=-1, keepdims=True)
    cross = jnp.mean(t * normed, axis=-1, keepdims=True)
    return inverse * (t - t_mean - normed * cross)


SMALL = 16
BLOCK = 256
QKV_BIAS = 6
UP_BIAS = QKV_BIAS + GROUPS
VM = pl.BlockSpec(memory_space=pltpu.VMEM)
SM = pl.BlockSpec(memory_space=pltpu.SMEM)
ANY = pl.BlockSpec(memory_space=pl.ANY)


def block(i):
    return pl.ds(pl.multiple_of(i * BLOCK, BLOCK), BLOCK)


def params(mib):
    return pltpu.CompilerParams(vmem_limit_bytes=mib * MIB)


def valid_rows(i, seq):
    return (lax.broadcasted_iota(jnp.int32, (BLOCK, 1), 0) + i * BLOCK < seq).astype(F32)


def unpack_small(small, dn, d, vec_out):
    n = small.shape[0]
    gw = d // GROUPS
    line = lambda row, width: jnp.concatenate([small[s, row:row + 1, :width] for s in range(n)], axis=1)
    vec_out[...] = jnp.zeros_like(vec_out)
    for i in range(6):
        vec_out[i:i + 1, :] = line(i, dn)
    qkv = line(6, 3 * dn)
    for j in range(GROUPS):
        vec_out[QKV_BIAS + j:QKV_BIAS + j + 1, :] = jnp.concatenate([qkv[:, a * d + j * gw:a * d + (j + 1) * gw] for a in range(3)], axis=1)
    up = line(7, small.shape[2])
    for j in range(up.shape[1] // d):
        vec_out[UP_BIAS + j:UP_BIAS + j + 1, :] = up[:, j * d:(j + 1) * d]


def prepare_kernel(plan, waits, sc_ref, x_ref, g_ref, packed, up_ref, down_ref, *rest):
    n1, n1t, n2, n2t, gl, vec_out, token, pick, sems = rest[waits:]
    d = x_ref.shape[1]
    par_ref = vec_out
    if plan["on"]:
        dn, rep = plan["dn"], sc_ref[3]
        cut = [pltpu.make_async_copy(up_ref.at[:, pl.ds(pl.multiple_of(rep * d, 128), d)], pick.at[0], sems.at[0]),
               pltpu.make_async_copy(down_ref.at[pl.ds(pl.multiple_of(rep * dn, 16), dn)], pick.at[1], sems.at[1])]

        @pl.when(pl.program_id(0) == 0)
        def _():
            for c in cut:
                c.start()
            unpack_small(packed[0].astype(F32) + packed[1].astype(F32) + packed[2].astype(F32) + packed[3].astype(F32), dn, d, vec_out)

        @pl.when(pl.program_id(0) == pl.num_programs(0) - 1)
        def _():
            for c in cut:
                c.wait()

    else:
        vec_out[...] = packed[...]
    token[...] = jnp.zeros_like(token)
    normed, _ = norm_parts(x_ref[...].astype(F32))
    one = (normed * par_ref[0:1, :] + par_ref[1:2, :]).astype(BF)
    two = (normed * par_ref[2:3, :] + par_ref[3:4, :]).astype(BF)
    n1[...] = one
    n2[...] = two
    n1t[...] = one.astype(F32).T.astype(BF)
    n2t[...] = two.astype(F32).T.astype(BF)
    gl[...] = (g_ref[...].astype(F32) * valid_rows(pl.program_id(0), sc_ref[0])).astype(BF)


def prepare(plan, scalars, x, g, par, up, down, waits):
    rows, d = x.shape
    flat, turned = jax.ShapeDtypeStruct((rows, d), BF), jax.ShapeDtypeStruct((d, rows), BF)
    vecs = (16, d) if plan["on"] else par.shape
    by_rows, by_cols = pl.BlockSpec((BLOCK, d), lambda i: (i, 0)), pl.BlockSpec((d, BLOCK), lambda i: (0, i))
    return pl.pallas_call(
        lambda *refs: prepare_kernel(plan, len(waits), *refs),
        grid_spec=pl.GridSpec(grid=(rows // BLOCK,), in_specs=[SM, by_rows, by_rows, pl.BlockSpec(par.shape, lambda i: (0,) * par.ndim), ANY, ANY] + [ANY] * len(waits),
                              out_specs=[by_rows, by_cols, by_rows, by_cols, by_rows, pl.BlockSpec(vecs, lambda i: (0, 0)), pl.BlockSpec((1, d), lambda i: (0, 0)), pl.BlockSpec((2, plan["dn"], d), lambda i: (0, 0, 0))],
                              scratch_shapes=[pltpu.SemaphoreType.DMA((2,))]),
        out_shape=[flat, turned, flat, turned, flat, jax.ShapeDtypeStruct(vecs, F32), jax.ShapeDtypeStruct((1, d), BF),
                   jax.ShapeDtypeStruct((2, plan["dn"], d), BF)], compiler_params=params(60), name="prepare",
        cost_estimate=pl.CostEstimate(flops=40 * rows * d, bytes_accessed=14 * rows * d, transcendentals=rows),
    )(scalars, x, g, par, up, down, *waits)


def attn_kernel(plan, first, base, sc_ref, n1, gl, b3_ref, keep_ref, up_ref, down_ref, *rest):
    nw = plan["pieces"] if first else 2
    w_refs, rest = rest[:nw], rest[nw:]
    d3, ctx_low, sm_ref, token, rest = rest[0].at[0], rest[1].at[0], rest[2].at[0], rest[3], rest[4:]
    token[...] = jnp.zeros_like(token)
    rows, d = n1.shape
    gw = d // GROUPS
    qb = BLOCK
    nb = rows // qb
    seq = sc_ref[0]
    if first:
        w_out, rest = rest[0], rest[1:]
    q_s, k_s, v_s, dc_s, ctx, dq, dk, dv, qm, km, vm, dcm, pall, dall = rest[:14]

    if first:
        w, sems = rest[14:]
        if plan["on"]:
            z, core, rep = sc_ref[1], sc_ref[2], sc_ref[3]
            dn, nz, nr = plan["dn"], plan["nz"], plan["nr"]
            own, sib, near, sibs = w_refs[0], w_refs[1], w_refs[2:2 + nr], w_refs[2 + nr]
            place = lambda zz, cc: pl.ds(pl.multiple_of((zz * 2 + cc) * dn, 16), dn)
            pairs = []
            for m in range(nr):
                pairs.append((own.at[m], w.at[m, place(z, core)]))
                pairs.append((sib.at[m], w.at[m, place(z, 1 - core)]))
            for j in range(nr):
                for k in range(1, nz):
                    m, zz = rep ^ j, z ^ k
                    pairs.append((near[j].at[k - 1], w.at[m, place(zz, core)]))
                    pairs.append((sibs.at[j, k - 1], w.at[m, place(zz, 1 - core)]))
        else:
            pairs = [(w_refs[0].at[m], w.at[m]) for m in range(GROUPS + 1)]
        copies = [pltpu.make_async_copy(a, b, sems.at[i]) for i, (a, b) in enumerate(pairs)]
        for c in copies:
            c.start()
        for c in copies:
            c.wait()
        back = pltpu.make_async_copy(w, w_out, sems.at[len(pairs)])
        back.start()
        w3, wo = w.at[0], w.at[GROUPS, 0:gw]
    else:
        w3, wo = w_refs[0].at[0], w_refs[1].at[0]
    half = ROT // 2

    def tables(r):
        return tuple(jnp.concatenate([t[r, :]] * (gw // 128), axis=1) for t in (keep_ref, up_ref, down_ref))

    def project(i, c):
        r = block(i)
        t = mm(n1[r, :], w3[...]) + b3_ref[pl.ds(QKV_BIAS + base + pl.program_id(0), 1), :]
        keep, up, down = tables(r)
        for at, ref, scale in ((0, q_s, HEAD_DIM ** -0.5), (1, k_s, None)):
            v = t[:, at * gw:(at + 1) * gw]
            low = (v * keep + pltpu.roll(v, gw - half, 1) * up + pltpu.roll(v, half, 1) * down).astype(BF)
            ref[r, :] = low if scale is None else (low.astype(F32) * scale).astype(BF)
        v_s[r, :] = t[:, 2 * gw:].astype(BF)
        dc_s[r, :] = mm_rt(gl[r, :], wo[...]).astype(BF)
        return c
    lax.fori_loop(0, nb, project, 0, unroll=True)

    key_bias = jnp.where(lax.broadcasted_iota(jnp.int32, (1, rows), 1) < seq, 0.0, MASKED).astype(F32)
    causal = lax.broadcasted_iota(jnp.int32, (qb, qb), 1) <= lax.broadcasted_iota(jnp.int32, (qb, qb), 0)

    heads = gw // HEAD_DIM

    def head(h, c):
        lane = lax.broadcasted_iota(jnp.int32, (1, gw), 1) // HEAD_DIM
        mask = jnp.where(lane == h, 1.0, 0.0).astype(BF)
        for ref, out in ((q_s, qm), (k_s, km), (v_s, vm), (dc_s, dcm)):
            out[h] = ref[...] * mask
        for i in range(nb):
            lo, kl = i * qb, (i + 1) * qb
            s = mm_rt(qm[h, lo:kl, :], k_s[:kl, :]) + key_bias[:, :kl]
            diag = jnp.where(causal, s[:, lo:], MASKED)
            s = diag if i == 0 else jnp.concatenate([s[:, :lo], diag], axis=1)
            dp = mm_rt(dcm[h, lo:kl, :], v_s[:kl, :])
            e = jnp.exp(s - jnp.max(s, axis=1, keepdims=True))
            p = e * (1.0 / jnp.sum(e, axis=1, keepdims=True))
            pall[h, lo:kl, :kl] = p.astype(BF)
            inner = jnp.sum(p * dp, axis=1, keepdims=True)
            dall[h, lo:kl, :kl] = (p * (dp - inner)).astype(BF)
        return c
    lax.fori_loop(0, heads, head, 0, unroll=2)
    for i in range(nb):
        lo, kl = i * qb, (i + 1) * qb
        ctx[lo:kl, :] = sum(mm(pall[h, lo:kl, :kl], vm[h, :kl, :]) for h in range(heads))
        dq[lo:kl, :] = sum(mm(dall[h, lo:kl, :kl], km[h, :kl, :]) for h in range(heads))
        dv[lo:kl, :] = sum(mm_lt(pall[h, lo:, lo:kl], dcm[h, lo:, :]) for h in range(heads))
        dk[lo:kl, :] = sum(mm_lt(dall[h, lo:, lo:kl], qm[h, lo:, :]) for h in range(heads))

    def finish(i, total):
        r = block(i)
        keep, up, down = tables(r)
        parts = []
        for ref, scale in ((dq, HEAD_DIM ** -0.5), (dk, 1.0)):
            v = ref[r, :] * scale
            parts.append(v * keep - pltpu.roll(v, gw - half, 1) * up - pltpu.roll(v, half, 1) * down)
        low = jnp.concatenate(parts + [dv[r, :]], axis=1).astype(BF)
        d3[r, :] = low
        ctx_low[r, :] = ctx[r, :].astype(BF)
        return total + jnp.sum(low.astype(F32), axis=0, keepdims=True)
    db3 = lax.fori_loop(0, nb, finish, jnp.zeros((1, d), F32), unroll=True)
    sm_ref[...] = jnp.broadcast_to(db3, sm_ref.shape)
    if first:
        back.wait()


def attention(plan, groups, scalars, n1, gl, b3, tables, weights):
    rows, d = n1.shape
    gw = d // GROUPS
    first, count, base = groups[0] == 0, len(groups), groups[0]
    plan = dict(plan, pieces=len(weights))
    whole = lambda *shape: pl.BlockSpec(shape, lambda j: (0,) * len(shape))
    stacked = lambda *shape: pl.BlockSpec((1,) + shape, lambda j: (j,) + (0,) * len(shape))
    out_shape = [jax.ShapeDtypeStruct((count, rows, d), BF), jax.ShapeDtypeStruct((count, rows, gw), BF), jax.ShapeDtypeStruct((count, 8, d), F32), jax.ShapeDtypeStruct((1, d), BF)]
    out_specs = [stacked(rows, d), stacked(rows, gw), stacked(8, d), whole(1, d)]
    heads = gw // HEAD_DIM
    scratch = [pltpu.VMEM((rows, gw), BF)] * 4 + [pltpu.VMEM((rows, gw), F32)] * 4
    scratch += [pltpu.VMEM((heads, rows, gw), BF)] * 4 + [pltpu.VMEM((heads, rows, rows), BF)] * 2
    if first:
        out_shape.append(jax.ShapeDtypeStruct((GROUPS + 1, d, d), BF))
        out_specs.append(ANY)
        scratch += [pltpu.VMEM((GROUPS + 1, d, d), BF), pltpu.SemaphoreType.DMA((64,))]
        w_specs = [ANY] * len(weights)
    else:
        weights = [weights[0], weights[0]]
        w_specs = [pl.BlockSpec((1, d, d), lambda j: (base + j, 0, 0)), pl.BlockSpec((1, gw, d), lambda j: (GROUPS, base + j, 0))]
    flops = count * (2 * rows * d * (d + gw) + 12 * HEADS // GROUPS * rows * rows * HEAD_DIM)
    return pl.pallas_call(
        lambda *refs: attn_kernel(plan, first, base, *refs),
        grid_spec=pl.GridSpec(
            grid=(count,),
            in_specs=[SM, whole(rows, d), whole(rows, d), whole(*b3.shape)] + [whole(rows, 128)] * 3 + w_specs,
            out_specs=out_specs, scratch_shapes=scratch),
        out_shape=out_shape, compiler_params=params(60), name="attend_first" if first else "attend_rest",
        cost_estimate=pl.CostEstimate(flops=4 * flops, bytes_accessed=8_000_000, transcendentals=count * HEADS * rows * rows // GROUPS),
    )(scalars, n1, gl, b3, *tables, *weights)


def write_halves(value, tmp, keep_ref, send_ref, core, dn):
    tmp[...] = value.astype(BF)
    for z in range(keep_ref.shape[0]):
        mine = pl.ds(pl.multiple_of((2 * z + core) * dn, 16), dn)
        other = pl.ds(pl.multiple_of((2 * z + 1 - core) * dn, 16), dn)
        keep_ref[z, 0] = tmp[mine, :]
        send_ref[z, 0] = tmp[other, :]


def closing_kernel(plan, sc_ref, x_ref, gl, n1t, par_ref, w, d3a, d3b, ctxa, ctxb, sma, smb, *rest):
    nd = 2 if plan["on"] else 1
    dw_refs, rest = rest[:nd], rest[nd:]
    sm_ref, ff_ref, gf, tmp = rest
    step = pl.program_id(0)
    rows, d = x_ref.shape
    nb = rows // BLOCK

    def store(dw):
        if plan["on"]:
            write_halves(dw, tmp, dw_refs[0], dw_refs[1], sc_ref[2], plan["dn"])
        else:
            dw_refs[0][0] = dw.astype(BF)
        return jnp.sum(dw * dw, axis=0, keepdims=True)

    def group(first, d3, db3):
        def body(i, c):
            r = block(i)
            part = mm_rt(d3[0, r, :], w[0])
            gf[r, :] = part if first else gf[r, :] + part
            return c
        lax.fori_loop(0, nb, body, 0, unroll=True)
        total = store(mm(n1t[...], d3[0])) + db3 * db3
        sm_ref[pl.ds(2 + step, 1), :] = db3
        sm_ref[5:6, :] = total if first else sm_ref[5:6, :] + total

    @pl.when(step == 0)
    def _():
        group(True, d3a, sma[0, 0:1, :])

    @pl.when(jnp.logical_and(step > 0, step < GROUPS))
    def _():
        group(False, d3b, smb[0, 0:1, :])

    @pl.when(step == GROUPS)
    def _():
        total = store(mm_lt(jnp.concatenate([ctxa[0]] + [ctxb[g] for g in range(GROUPS - 1)], axis=1), gl[...]))

        def back(i, c):
            r = block(i)
            normed, inverse = norm_parts(x_ref[r, :].astype(F32))
            e = gf[r, :]
            ff_ref[r, :] = norm_back(e, par_ref[0:1, :], normed, inverse)
            return (c[0] + jnp.sum(e * normed, axis=0, keepdims=True), c[1] + jnp.sum(e, axis=0, keepdims=True))
        zero = jnp.zeros((1, d), F32)
        dgain, dshift = lax.fori_loop(0, nb, back, (zero, zero), unroll=True)
        sm_ref[0:1, :] = dgain
        sm_ref[1:2, :] = dshift
        sm_ref[5:6, :] += total + dgain * dgain + dshift * dshift


def closing(plan, scalars, x, gl, n1t, par, w, d3a, d3b, ctxa, ctxb, sma, smb):
    rows, d = x.shape
    gw = d // GROUPS
    whole = lambda *shape: pl.BlockSpec(shape, lambda j: (0,) * len(shape))
    later = lambda *shape: pl.BlockSpec((1,) + shape, lambda j: (jnp.clip(j - 1, 0, GROUPS - 2),) + (0,) * len(shape))
    if plan["on"]:
        nz, dn = plan["nz"], plan["dn"]
        dw_specs = [pl.BlockSpec((nz, 1, dn, d), lambda j: (0, j, 0, 0))] * 2
        dw_shapes = [jax.ShapeDtypeStruct((nz, GROUPS + 1, dn, d), BF)] * 2
    else:
        dw_specs = [pl.BlockSpec((1, d, d), lambda j: (j, 0, 0))]
        dw_shapes = [jax.ShapeDtypeStruct((GROUPS + 1, d, d), BF)]
    return pl.pallas_call(
        lambda *refs: closing_kernel(plan, *refs),
        grid_spec=pl.GridSpec(
            grid=(GROUPS + 1,),
            in_specs=[SM, whole(rows, d), whole(rows, d), whole(d, rows), whole(*par.shape),
                      pl.BlockSpec((1, d, d), lambda j: (jnp.minimum(j, GROUPS - 1), 0, 0)),
                      whole(1, rows, d), later(rows, d), whole(1, rows, gw), whole(GROUPS - 1, rows, gw), whole(1, 8, d), later(8, d)],
            out_specs=dw_specs + [whole(8, d), whole(rows, d)],
            scratch_shapes=[pltpu.VMEM((rows, d), F32), pltpu.VMEM((d, d), BF)],
        ),
        out_shape=dw_shapes + [jax.ShapeDtypeStruct((8, d), F32), jax.ShapeDtypeStruct((rows, d), F32)],
        compiler_params=params(60), name="closing",
        cost_estimate=pl.CostEstimate(flops=4 * rows * d * 7 * d, bytes_accessed=8_000_000, transcendentals=rows),
    )(scalars, x, gl, n1t, par, w, d3a, d3b, ctxa, ctxb, sma, smb)


ERF_P = 0.3275911
ERF_A = (0.254829592, -0.284496736, 1.421413741, -1.453152027, 1.061405429)


def gelu_parts(u):
    z = jnp.abs(u) * (2.0 ** -0.5)
    t = 1.0 / (1.0 + ERF_P * z)
    bell = jnp.exp(-0.5 * (u * u))
    a1, a2, a3, a4, a5 = (0.5 * a for a in ERF_A)
    tail = ((((a5 * t + a4) * t + a3) * t + a2) * t + a1) * t * bell
    cdf = jnp.where(u >= 0.0, 1.0 - tail, tail)
    return u * cdf, cdf + u * bell * (1.0 / math.sqrt(2.0 * math.pi))


def ffn_kernel(plan, sc_ref, x_ref, gl, n2, n2t, par_ref, ff_ref, sm1_ref, *rest):
    nw = plan["pieces"]
    w_refs, rest = rest[:nw], rest[nw:]
    nd = 4 if plan["on"] else 2
    dw_refs, rest = rest[:nd], rest[nd:]
    sm_ref, norm_ref, act_ref, wd_ref, gx_ref = rest[:5]
    wu_s, wd_s, gs, gup, sq, tmp, x_s, ff_s, up_sems, down_sems, late_sems = rest[5:]
    late = [pltpu.make_async_copy(x_ref, x_s, late_sems.at[0]), pltpu.make_async_copy(ff_ref, ff_s, late_sems.at[1])]
    step = pl.program_id(0)
    last = pl.num_programs(0) - 1
    rows, d = x_ref.shape
    fc = d
    nb = rows // BLOCK

    @pl.when(step == 0)
    def _():
        if plan["on"]:
            z, core, rep = sc_ref[1], sc_ref[2], sc_ref[3]
            dn, nz, nr = plan["dn"], plan["nz"], plan["nr"]
            own_up, own_down, sib_up, sib_down = w_refs[:4]
            near, sibs = w_refs[4:4 + nr], w_refs[4 + nr]

            def up(src, m, zz, cc):
                dst = wu_s.at[m, pl.ds(pl.multiple_of((zz * 2 + cc) * dn, 16), dn)]
                pltpu.make_async_copy(src, dst, up_sems.at[m]).start()

            def down(src, b, zz, cc):
                dst = wd_s.at[zz, pl.ds(pl.multiple_of((cc * nr + b) * dn, 16), dn)]
                pltpu.make_async_copy(src, dst, down_sems.at[zz]).start()
            for m in range(nr):
                cols, part = pl.ds(m * d, d), pl.ds(m * dn, dn)
                up(own_up.at[:, cols], m, z, core)
                up(sib_up.at[:, cols], m, z, 1 - core)
                down(own_down.at[part], m, z, core)
                down(sib_down.at[part], m, z, 1 - core)
            for j in range(nr):
                for k in range(1, nz):
                    up(near[j].at[k - 1, 0], rep ^ j, z ^ k, core)
                    up(sibs.at[j, k - 1, 0], rep ^ j, z ^ k, 1 - core)
                    down(near[j].at[k - 1, 1], rep ^ j, z ^ k, core)
                    down(sibs.at[j, k - 1, 1], rep ^ j, z ^ k, 1 - core)
        else:
            for m in range(wu_s.shape[0]):
                pltpu.make_async_copy(w_refs[0].at[m], wu_s.at[m], up_sems.at[m]).start()
                pltpu.make_async_copy(w_refs[1].at[m], wd_s.at[m], down_sems.at[m]).start()
        for c in late:
            c.start()
        gs[...] = jnp.zeros_like(gs)
        sq[...] = jnp.zeros_like(sq)
        sm_ref[...] = jnp.zeros_like(sm_ref)

    pltpu.make_async_copy(wu_s.at[step], wu_s.at[step], up_sems.at[step]).wait()
    pltpu.make_async_copy(wd_s.at[step], wd_s.at[step], down_sems.at[step]).wait()
    wu, wd = wu_s.at[step], wd_s.at[step]
    wd_ref[0] = wd[...]

    def rows_step(i, dbu):
        r = block(i)
        u = mm(n2[r, :], wu[...]) + par_ref[pl.ds(UP_BIAS + step, 1), :]
        da = mm_rt(gl[r, :], wd[...])
        a, slope = gelu_parts(u)
        act_ref[0, r, :] = a.astype(BF)
        gu = (da * slope).astype(BF)
        gup[r, :] = gu
        gs[r, :] += mm_rt(gu, wu[...])
        return dbu + jnp.sum(gu.astype(F32), axis=0, keepdims=True)
    dbu = lax.fori_loop(0, nb, rows_step, jnp.zeros((1, fc), F32), unroll=True)
    sm_ref[pl.ds(8 + step, 1), :] = dbu

    dwu = mm(n2t[...], gup[...])
    total = jnp.sum(dwu * dwu, axis=0, keepdims=True) + dbu * dbu
    if plan["on"]:
        write_halves(dwu, tmp, dw_refs[0], dw_refs[1], sc_ref[2], plan["dn"])
    else:
        dw_refs[0][0] = dwu.astype(BF)
    dwd = mm_lt(act_ref[0], gl[...])
    total += jnp.sum(dwd * dwd, axis=0, keepdims=True)
    if plan["on"]:
        tmp[...] = dwd.astype(BF)
        core, dn, nr = sc_ref[2], plan["dn"], plan["nr"]
        for m in range(nr):
            dw_refs[2][0, m] = tmp[pl.ds(pl.multiple_of((core * nr + m) * dn, 16), dn), :]
            dw_refs[3][0, m] = tmp[pl.ds(pl.multiple_of(((1 - core) * nr + m) * dn, 16), dn), :]
    else:
        dw_refs[1][0] = dwd.astype(BF)
    sq[...] += total

    @pl.when(step == last)
    def _():
        for c in late:
            c.wait()

        def back(i, c):
            r = block(i)
            normed, inverse = norm_parts(x_s[r, :].astype(F32))
            e = gs[r, :]
            grad_rows = gl[r, :].astype(F32)
            gx_ref[r, :] = (grad_rows + ff_s[r, :] + norm_back(e, par_ref[2:3, :], normed, inverse)).astype(BF)
            return (c[0] + jnp.sum(e * normed, axis=0, keepdims=True), c[1] + jnp.sum(e, axis=0, keepdims=True),
                    c[2] + jnp.sum(grad_rows, axis=0, keepdims=True))
        zero = jnp.zeros((1, d), F32)
        dgain, dshift, dbd = lax.fori_loop(0, nb, back, (zero, zero, zero), unroll=True)
        sm_ref[0:2, :] = sm1_ref[0:2, :]
        sm_ref[2:3, :] = dgain
        sm_ref[3:4, :] = dshift
        sm_ref[4:5, :] = dbd
        sm_ref[5:8, :] = sm1_ref[2:5, :]
        final = sq[...] + sm1_ref[5:6, :] + dgain * dgain + dshift * dshift + 2.0 * dbd * dbd
        own = jnp.sqrt(jnp.sum(final, axis=1, keepdims=True))
        here = lax.broadcasted_iota(jnp.int32, norm_ref.shape, 1) == sc_ref[4]
        norm_ref[...] = jnp.where(here, own, 0.0)


def ffn(plan, chunks, scalars, x, gl, n2, n2t, par, ff, sm1, weights, norm_width):
    rows, d = x.shape
    plan = dict(plan, pieces=len(weights))
    whole = lambda *shape: pl.BlockSpec(shape, lambda j: (0,) * len(shape))
    if plan["on"]:
        nz, dn, nr = plan["nz"], plan["dn"], plan["nr"]
        dw_specs = [pl.BlockSpec((nz, 1, dn, d), lambda j: (0, j, 0, 0))] * 2 + [pl.BlockSpec((1, nr, dn, d), lambda j: (j, 0, 0, 0))] * 2
        dw_shapes = [jax.ShapeDtypeStruct((nz, chunks, dn, d), BF)] * 2 + [jax.ShapeDtypeStruct((nz, nr, dn, d), BF)] * 2
    else:
        dw_specs = [pl.BlockSpec((1, d, d), lambda j: (j, 0, 0))] * 2
        dw_shapes = [jax.ShapeDtypeStruct((chunks, d, d), BF)] * 2
    return pl.pallas_call(
        lambda *refs: ffn_kernel(plan, *refs),
        grid_spec=pl.GridSpec(
            grid=(chunks,),
            in_specs=[SM, ANY, whole(rows, d), whole(rows, d), whole(d, rows), whole(*par.shape), ANY, whole(8, d)] + [ANY] * len(weights),
            out_specs=dw_specs + [whole(SMALL, d), whole(1, norm_width), pl.BlockSpec((1, rows, d), lambda j: (j, 0, 0)),
                                  pl.BlockSpec((1, d, d), lambda j: (j, 0, 0)), whole(rows, d)],
            scratch_shapes=[
                pltpu.VMEM((chunks, d, d), BF), pltpu.VMEM((chunks, d, d), BF), pltpu.VMEM((rows, d), F32), pltpu.VMEM((rows, d), BF),
                pltpu.VMEM((1, d), F32), pltpu.VMEM((d, d), BF), pltpu.VMEM((rows, d), BF), pltpu.VMEM((rows, d), F32),
                pltpu.SemaphoreType.DMA((chunks,)), pltpu.SemaphoreType.DMA((chunks,)), pltpu.SemaphoreType.DMA((2,)),
            ],
        ),
        out_shape=dw_shapes + [
            jax.ShapeDtypeStruct((SMALL, d), F32), jax.ShapeDtypeStruct((1, norm_width), F32),
            jax.ShapeDtypeStruct((chunks, rows, d), BF), jax.ShapeDtypeStruct((chunks, d, d), BF), jax.ShapeDtypeStruct((rows, d), BF),
        ],
        compiler_params=params(60), name="feedforward",
        cost_estimate=pl.CostEstimate(flops=2 * 5 * rows * d * d * chunks * 2, bytes_accessed=40_000_000, transcendentals=rows * d * chunks),
    )(scalars, x, gl, n2, n2t, par, ff, sm1, *weights)


def output_kernel(sc_ref, x_ref, par_ref, token, wo, wd, act, *rest):
    ctxs, out_ref = rest[:2], rest[2]
    d = x_ref.shape[1]
    gw = d // GROUPS
    total = x_ref[...].astype(F32) + par_ref[4:5, :] + par_ref[5:6, :]
    for g in range(GROUPS):
        ctx = ctxs[0][0] if g == 0 else ctxs[1][g - 1]
        total += mm(ctx, wo[0, g * gw:(g + 1) * gw, :])
    for j in range(wd.shape[0]):
        total += mm(act[j], wd[j])
    out_ref[...] = (total * valid_rows(pl.program_id(0), sc_ref[0])).astype(BF)


def output(scalars, x, par, token, w, wd, act, ctxs):
    rows, d = x.shape
    gw = d // GROUPS
    chunks = wd.shape[0]
    return pl.pallas_call(
        output_kernel,
        grid_spec=pl.GridSpec(
            grid=(rows // BLOCK,),
            in_specs=[SM, pl.BlockSpec((BLOCK, d), lambda i: (i, 0)), pl.BlockSpec(par.shape, lambda i: (0, 0)), pl.BlockSpec(token.shape, lambda i: (0, 0)),
                      pl.BlockSpec((1, d, d), lambda i: (GROUPS, 0, 0)), pl.BlockSpec((chunks, d, d), lambda i: (0, 0, 0)),
                      pl.BlockSpec((chunks, BLOCK, d), lambda i: (0, i, 0))] + [pl.BlockSpec((1, BLOCK, gw), lambda i: (0, i, 0)), pl.BlockSpec((GROUPS - 1, BLOCK, gw), lambda i: (0, i, 0))],
            out_specs=pl.BlockSpec((BLOCK, d), lambda i: (i, 0)),
        ),
        out_shape=jax.ShapeDtypeStruct((rows, d), BF),
        compiler_params=params(60), name="output",
        cost_estimate=pl.CostEstimate(flops=2 * rows * d * d * (chunks + 1), bytes_accessed=18_000_000, transcendentals=0),
    )(scalars, x, par, token, w, wd, act, *ctxs)


def spread(rows_ref, lane):
    norms = rows_ref
    at = lax.broadcasted_iota(jnp.int32, norms.shape, 1)
    own = jnp.sum(jnp.where(at == lane, norms, 0.0), axis=1, keepdims=True)
    return own


def mix_kernel(seqs, flip, sc_ref, r0, r1, sm, smg, dk, dg, uk, ug, ak, ag, token, d_out, u_out, a_out, norm_out, ins, outs, dins, douts, in_sems, out_sems):
    xb, yb, lob = flip ^ (sc_ref[3] % 2), flip ^ (sc_ref[3] // 2), flip ^ (sc_ref[1] % 2)
    dn = dk.shape[4]
    jobs = []
    for i in range(4):
        zh, y = i // 2, i % 2
        jobs.append(([v.at[zh, lob, y] for v in (dk, dg)], 0, i, d_out.at[zh, 0, y]))
    for i in range(4):
        jobs.append(([v.at[i, yb] for v in (uk, ug)], 0, 4 + i, u_out.at[i, 0]))
    for i in range(4):
        jobs.append(([v.at[i, :, xb] for v in (ak, ag)], 1, 8 + i, a_out.at[i, :, 0]))
    reads = [[pltpu.make_async_copy(src, ins.at[at, t], in_sems.at[2 * at + t]) for t, src in enumerate(srcs)] for srcs, _, at, _ in jobs]
    for pair in reads:
        for c in pair:
            c.start()
    norms = r0[...] + r1[...]
    norm_out[...] = norms
    mean = jnp.sum(norms, axis=1, keepdims=True) * (1.0 / seqs)
    me = sc_ref[4]
    factor = jnp.minimum(1.0, mean / spread(norms, me)) * (1.0 / seqs)
    other = jnp.minimum(1.0, mean / spread(norms, me ^ 1)) * (1.0 / seqs)
    factor, other = factor[0, 0], other[0, 0]
    mixed = lambda k, g: (k.astype(F32) * factor + g.astype(F32) * other).astype(BF)
    small = mixed(sm[...], smg[...])
    writes = []
    for pair, (_, _, at, dst) in zip(reads, jobs):
        for c in pair:
            c.wait()
        for t in range(2):
            low = mixed(ins[at, 0, t], ins[at, 1, t])
            if at < 4:
                douts[at, t, :dn] = low
                douts[at, t, dn:] = small
            else:
                outs[at - 4, t] = low
        writes.append(pltpu.make_async_copy(douts.at[at] if at < 4 else outs.at[at - 4], dst, out_sems.at[at]))
        writes[-1].start()
    for c in writes:
        c.wait()


def mix(seqs, sending, scalars, norm_rows, halves, smalls, token):
    flip = 1 if sending else 0
    dn, d = halves[0].shape[2:]
    ak, ag, uk, ug = (v.reshape(4, 2, 2, dn, d) for v in halves[:4])
    dk, dg = (v.reshape(2, 2, 2, 2, dn, d) for v in halves[4:])
    width = norm_rows[0].shape[1]
    dd, u, a, norms = pl.pallas_call(
        lambda *refs: mix_kernel(seqs, flip, *refs),
        in_specs=[SM] + [VM] * 4 + [ANY] * 7, out_specs=[ANY] * 3 + [VM],
        out_shape=[jax.ShapeDtypeStruct((2, 1, 2, 2, dn + SMALL, d), BF), jax.ShapeDtypeStruct((4, 1, 2, dn, d), BF),
                   jax.ShapeDtypeStruct((4, 2, 1, dn, d), BF), jax.ShapeDtypeStruct((1, width), F32)],
        scratch_shapes=[pltpu.VMEM((12, 2, 2, dn, d), BF), pltpu.VMEM((8, 2, dn, d), BF), pltpu.VMEM((1, 1), F32), pltpu.VMEM((4, 2, dn + SMALL, d), BF),
                        pltpu.SemaphoreType.DMA((24,)), pltpu.SemaphoreType.DMA((12,))],
        compiler_params=params(60), name="mix_send" if sending else "mix_keep",
        cost_estimate=pl.CostEstimate(flops=16_000_000, bytes_accessed=10_600_000, transcendentals=0),
    )(scalars, *norm_rows, *smalls, dk, dg, uk, ug, ak, ag, token)
    return a.reshape(2, 2, 2, 1, dn, d), u.reshape(2, 2, 1, 2, dn, d), dd, norms


AXES = dict(hi=0, lo=1, y=2, x=3)


def side(name, sc, flip):
    bit = {"hi": sc[1] // 2, "lo": sc[1] % 2, "y": sc[3] // 2, "x": sc[3] % 2}[name]
    return flip ^ bit


def fold_kernel(sc_ref, ms, gs, mk, gk, *rest):
    send, keep = rest[-2:]
    d = ms.shape[-1]
    add = lambda a, b, out: (a[...].reshape(-1, d).astype(F32) + b[...].reshape(-1, d).astype(F32)).astype(BF).reshape(out.shape)
    send[...] = add(ms, gs, send)
    keep[...] = add(mk, gk, keep)


def fold(scalars, name, mine, got, waits=()):
    axis = AXES[name]
    shape = mine.shape
    blk = (1,) + tuple(1 if i == axis else s for i, s in enumerate(shape) if i > 0)
    spec = lambda flip: pl.BlockSpec(blk, lambda i, sc: (i,) + tuple(side(name, sc, flip) if k == axis else 0 for k in range(1, 6)))
    out = pl.BlockSpec(blk, lambda i, sc: (i, 0, 0, 0, 0, 0))
    half = jax.ShapeDtypeStruct((shape[0],) + blk[1:], BF)
    return pl.pallas_call(
        fold_kernel,
        grid_spec=pltpu.PrefetchScalarGridSpec(num_scalar_prefetch=1, grid=(shape[0],), in_specs=[spec(1), spec(1), spec(0), spec(0)] + [ANY] * len(waits), out_specs=[out, out]),
        out_shape=[half, half], compiler_params=params(16), name="fold_" + name,
        cost_estimate=pl.CostEstimate(flops=mine.size, bytes_accessed=6 * mine.size, transcendentals=0),
    )(scalars, mine, got, mine, got, *waits)


def last_fold_kernel(sc_ref, *refs):
    ins, (send1, send2, keep1, keep2) = refs[:12], refs[12:]
    first = send1.shape[0]
    at = 0
    for p in range(3):
        ms, gs, mk, gk = ins[4 * p:4 * p + 4]
        rows = ms.shape[4]
        for a, b, out1, out2 in ((ms, gs, send1, send2), (mk, gk, keep1, keep2)):
            low = (a[0, 0, 0, 0].astype(F32) + b[0, 0, 0, 0].astype(F32)).astype(BF)
            split = min(max(first - at, 0), rows)
            if split > 0:
                out1[at:at + split, :] = low[:split]
            if split < rows:
                out2[at + split - first:at + rows - first, :] = low[split:]
        at += rows


def last_fold(scalars, parts, first):
    specs, args, total = [], [], 0
    for mine, got in parts:
        blk = (1,) + mine.shape[1:]
        spec = lambda flip, blk=blk: pl.BlockSpec(blk, lambda i, sc: (side("hi", sc, flip), 0, 0, 0, 0, 0))
        specs += [spec(1), spec(1), spec(0), spec(0)]
        args += [mine, got, mine, got]
        total += mine.shape[4]
    d = parts[0][0].shape[5]
    sizes = (first, total - first)
    out = [pl.BlockSpec((s, d), lambda i, sc: (0, 0)) for s in sizes]
    half = [jax.ShapeDtypeStruct((s, d), BF) for s in sizes]
    return pl.pallas_call(
        last_fold_kernel,
        grid_spec=pltpu.PrefetchScalarGridSpec(num_scalar_prefetch=1, grid=(1,), in_specs=specs, out_specs=out + out),
        out_shape=half + half, compiler_params=params(16), name="last_fold",
        cost_estimate=pl.CostEstimate(flops=2 * total * d, bytes_accessed=12 * total * d, transcendentals=0),
    )(scalars, *args)


def xor_permute(value, axis, size, bit):
    return lax.ppermute(value, axis, [(i, i ^ bit) for i in range(size)])


def butterfly(value, axis, size):
    if size & (size - 1):
        return lax.psum(value, axis)
    bit = 1
    while bit < size:
        value = value + xor_permute(value, axis, size, bit)
        bit *= 2
    return value


def after(value, other):
    return value + other[(slice(0, 1),) * other.ndim].reshape((1,) * value.ndim).astype(value.dtype) * 0


def per_device(sizes, block_input, cotangent, lengths, first_gain, first_shift, second_gain, second_shift, triple_weight, triple_bias,
               output_weight, output_bias, upward_weight, upward_bias, downward_weight, downward_bias):
    rep, n = sizes
    rows, d = block_input.shape
    dn, fn = first_gain.shape[0], upward_bias.shape[0]
    gw = d // GROUPS
    chunks = fn * n // d
    nz = n // 2
    plan = dict(on=rep == 4 and n == 8 and dn % 16 == 0 and chunks == nz == rep, dn=dn, nz=nz, nr=rep)
    ri, fi = lax.axis_index("rep"), lax.axis_index("fsdp")
    z, core = fi // 2, fi % 2
    me = ri * n + fi
    scalars = jnp.stack([lengths[0], z, core, ri, me]).astype(jnp.int32)
    group_cols = lambda v, j: jnp.concatenate([v[:, a * d + j * gw:a * d + (j + 1) * gw] for a in range(3)], axis=1)
    mats = jnp.stack([group_cols(triple_weight, j) for j in range(GROUPS)] + [output_weight])
    small = [first_gain, first_shift, second_gain, second_shift, output_bias, downward_bias, triple_bias, upward_bias]
    wide_row = max(v.shape[0] for v in small)
    low = jnp.asarray(-jnp.inf, BF)
    small = [lax.pad(v.reshape(1, -1), low, ((i, 7 - i, 0), (0, wide_row - v.shape[0], 0))) for i, v in enumerate(small)]
    while len(small) > 1:
        small = [jnp.maximum(a, b) for a, b in zip(small[::2], small[1::2])]
    small = jnp.maximum(small[0], jnp.asarray(-1e4, BF))
    small = jnp.where(jnp.arange(n)[:, None, None] == fi, small[None], 0.0).astype(BF)

    along_z = lambda v: [xor_permute(v, "fsdp", n, 2 * k) for k in range(1, nz)]
    along_rep = lambda v: [xor_permute(v, "rep", rep, j) for j in range(1, rep)]
    to_core = lambda v: xor_permute(v, "fsdp", n, 1)

    def unpack(small):
        small = small.astype(F32)
        par = small[:, :6, :dn].swapaxes(0, 1).reshape(6, d)
        bias_t = small[:, 6, :3 * dn].reshape(1, 3 * d)
        vecs = jnp.concatenate([par] + [group_cols(bias_t, j) for j in range(GROUPS)] + [small[:, 7, :fn].reshape(chunks, d)])
        return jnp.pad(vecs, ((0, -vecs.shape[0] % 8), (0, 0)))

    if plan["on"]:
        quarter = lax.dynamic_index_in_dim(mats, ri, 0, keepdims=False)
        small = small + to_core(small)
        far = along_z(quarter)
        small = jnp.stack([small] + along_z(small))
        sib_own = to_core(mats)
        wide_own = [upward_weight, downward_weight, to_core(upward_weight), to_core(downward_weight)]
        n1, n1t, n2, n2t, gl, par, ready, pick = prepare(plan, scalars, block_input, cotangent, small, upward_weight, downward_weight, [sib_own] + wide_own[2:])
        far = jnp.stack(far) + ready
        near = [far] + along_rep(far)
    else:
        small = butterfly(small, "fsdp", n)
        weights = [lax.all_gather(mats, "fsdp", axis=1, tiled=True)]
        n1, n1t, n2, n2t, gl, par, ready, _ = prepare(plan, scalars, block_input, cotangent, unpack(small), upward_weight, downward_weight, [])
    tables = [jnp.asarray(t) for t in rotary_tables(rows, 128)]

    if plan["on"]:
        wide_far = jnp.stack(along_z(pick))
        weights = [mats, sib_own] + near + [to_core(jnp.stack(near))]
    d3a, ctxa, sma, token_a, w = attention(plan, (0,), scalars, n1, gl, par, tables, weights)
    if plan["on"]:
        wide_far = wide_far + token_a
        wide_near = [wide_far] + along_rep(wide_far)
    d3b, ctxb, smb, token_b = attention(plan, (1, 2), scalars, n1, gl, par, tables, [w])
    if plan["on"]:
        wide_sibs = to_core(jnp.stack(wide_near) + token_b)
        wide_weights = wide_own + wide_near + [wide_sibs]
    else:
        up = lax.all_gather(upward_weight, "fsdp", axis=0, tiled=True)
        down = lax.all_gather(downward_weight, "fsdp", axis=0, tiled=True)
        wide_weights = [jnp.stack([up[:, j * d:(j + 1) * d] for j in range(chunks)]), down.reshape(chunks, d, d)]
    *dwa, sm1, ff = closing(plan, scalars, block_input, gl, n1t, par, w, d3a, d3b, ctxa, ctxb, sma, smb)
    width = -(-rep * n // 128) * 128
    *dwf, smalls, norm_row, act, wd, gx = ffn(plan, chunks, scalars, block_input, gl, n2, n2t, par, ff, sm1, wide_weights, width)

    if plan["on"]:
        a, b, c = along_z(norm_row)
        norm_row = (norm_row + a) + (b + c)
        a, b, c = along_rep(norm_row)
        norm_row = (norm_row + a) + (b + c)
        norm_rows = (norm_row, to_core(norm_row))
        halves = []
        for keep, send in ((dwa[0], dwa[1]), (dwf[0], dwf[1]), (dwf[2], dwf[3])):
            halves += [keep, to_core(send)]
        pair = (smalls, to_core(smalls))
        steps = dict(x=("rep", rep, 1), y=("rep", rep, 2), lo=("fsdp", n, 2), hi=("fsdp", n, 4))
        move = lambda v, name: xor_permute(v, *steps[name])
        *sends, norm_row = mix(rep * n, True, scalars, norm_rows, halves, pair, ready)
        norms = norm_row[0, :rep * n]
        *mines, token = mix(rep * n, False, scalars, norm_rows, halves, pair, norm_row)
        out = output(scalars, block_input, par, token, w, wd, act, (ctxa, ctxb))
        parts = []
        for send, mine, order in zip(sends, mines, (("x", "y", "lo"), ("y", "lo", "x"), ("lo", "x", "y"))):
            got = move(send, order[0])
            for name in order[1:]:
                send, mine = fold(scalars, name, mine, got, (out,) if name == order[1] else ())
                got = move(send, name)
            parts.append((mine, got))
        first = 3 * dn // 2
        send_1, send_2, mine_1, mine_2 = last_fold(scalars, parts, first)
        add = lambda mine, send: (mine.astype(F32) + move(send, "hi").astype(F32)).astype(BF)
        mine_1 = add(mine_1, send_1)
        around_1 = [mine_1] + along_rep(mine_1)
        mine_2 = add(mine_2, send_2)
        smalls = mine_2[first:].astype(F32)
        mine_2 = mine_2[:first]
        around_2 = [mine_2] + along_rep(mine_2)
        around = [jnp.concatenate([p, q]) for p, q in zip(around_1, around_2)]
        x, y = ri % 2, ri // 2
        flip = lambda bit, a, b: (jnp.where(bit == 1, b, a), jnp.where(bit == 1, a, b))
        a0, a1 = flip(x, around[0], around[1])
        a2, a3 = flip(x, around[2], around[3])
        a0, a2 = flip(y, a0, a2)
        a1, a3 = flip(y, a1, a3)
        final = jnp.stack([a0, a1, a2, a3]).astype(F32)
        g_att, g_up, g_down = final[:, :dn], final[:, dn:2 * dn], final[:, 2 * dn:].reshape(fn, d)
        smalls = smalls.reshape(SMALL, d)
    else:
        norms = butterfly(butterfly(norm_row, "fsdp", n), "rep", rep)[0, :rep * n]
        factor = jnp.minimum(1.0, jnp.mean(norms) / lax.dynamic_index_in_dim(norms, me, 0, keepdims=False)) / (rep * n)
        out = output(scalars, block_input, par, ready, w, wd, act, (ctxa, ctxb))
        scale = lambda v: (v.astype(F32) * factor).astype(BF)
        shards = lambda v: v.reshape(v.shape[0], n, dn, d).swapaxes(0, 1).reshape(n, -1, d)
        pack = jnp.concatenate([scale(shards(dwa[0])), scale(shards(dwf[0])), scale(dwf[1].reshape(n, fn, d))], axis=1)
        mine = lax.psum_scatter(pack, "fsdp", scatter_dimension=0, tiled=True)[0]
        mine = lax.psum(mine, "rep").astype(F32)
        g_att = mine[:4 * dn].reshape(4, dn, d)
        g_up = mine[4 * dn:(4 + chunks) * dn].reshape(chunks, dn, d)
        g_down = mine[(4 + chunks) * dn:]
        smalls = lax.psum(scale(smalls), ("rep", "fsdp")).astype(F32)

    g_triple = jnp.concatenate([g_att[j, :, a * gw:(a + 1) * gw] for a in range(3) for j in range(GROUPS)], axis=1)
    g_upward = jnp.concatenate([g_up[j] for j in range(chunks)], axis=1)
    own = lambda v, width: lax.dynamic_slice_in_dim(v, fi * width, width, 0)
    g1, s1, g2, s2, bd = (own(smalls[i], dn) for i in range(5))
    b_triple = own(jnp.concatenate([smalls[5 + j, a * gw:(a + 1) * gw] for a in range(3) for j in range(GROUPS)]), 3 * dn)
    b_up = own(smalls[8:8 + chunks].reshape(-1), fn)
    return (out, gx, g1, s1, g2, s2, g_triple, b_triple, g_att[GROUPS], bd, g_upward, b_up, g_down, bd, norms)


def solution(mesh):
    rows = P(("rep", "fsdp"), None)
    vec, mat = P("fsdp"), P("fsdp", None)
    sizes = (mesh.shape["rep"], mesh.shape["fsdp"])
    return jax.shard_map(
        lambda *args: per_device(sizes, *args),
        mesh=mesh,
        in_specs=(rows, rows, P(("rep", "fsdp")), vec, vec, vec, vec, mat, vec, mat, vec, mat, vec, mat, vec),
        out_specs=(rows, rows, vec, vec, vec, vec, mat, vec, mat, vec, mat, vec, mat, vec, P()),
        check_vma=False,
    )
```

```python
import math
import numpy as np
import jax
import jax.numpy as jnp
from jax import lax
from jax.experimental import pallas as pl
from jax.experimental.pallas import tpu as pltpu
from jax.sharding import PartitionSpec as P

HEADS = 12
HEAD_DIM = 64
ROT = 16
EPS = 1e-05
MASKED = -1e30
BF = jnp.bfloat16
F32 = jnp.float32
GROUPS = 3
MIB = 1024 * 1024


def mm(a, b):
    return jnp.dot(a, b, preferred_element_type=F32)


def mm_rt(a, b):
    return lax.dot_general(a, b, (((1,), (1,)), ((), ())), preferred_element_type=F32)


def mm_lt(a, b):
    return lax.dot_general(a, b, (((0,), (0,)), ((), ())), preferred_element_type=F32)


def rotary_tables(rows, width):
    half = ROT // 2
    freq = np.exp(np.arange(half, dtype=np.float32) * np.float32(-2.0 * math.log(10000.0) / ROT))
    ang = np.arange(rows, dtype=np.float32)[:, None] * freq.astype(np.float32)[None, :]
    cos, sin = np.cos(ang), np.sin(ang)
    keep = np.ones((rows, HEAD_DIM), np.float32)
    up = np.zeros((rows, HEAD_DIM), np.float32)
    down = np.zeros((rows, HEAD_DIM), np.float32)
    keep[:, :half] = cos
    keep[:, half:ROT] = cos
    up[:, :half] = -sin
    down[:, half:ROT] = sin
    rep = width // HEAD_DIM
    return tuple(np.tile(t, (1, rep)).astype(np.float32) for t in (keep, up, down))


def norm_parts(values):
    centred = values - jnp.mean(values, axis=-1, keepdims=True)
    inverse = lax.rsqrt(jnp.mean(centred * centred, axis=-1, keepdims=True) + EPS)
    return centred * inverse, inverse


def norm_back(e, gain, normed, inverse):
    t = e * gain
    t_mean = jnp.mean(t, axis=-1, keepdims=True)
    cross = jnp.mean(t * normed, axis=-1, keepdims=True)
    return inverse * (t - t_mean - normed * cross)


SMALL = 16
BLOCK = 256
QKV_BIAS = 6
UP_BIAS = QKV_BIAS + GROUPS
VM = pl.BlockSpec(memory_space=pltpu.VMEM)
SM = pl.BlockSpec(memory_space=pltpu.SMEM)
ANY = pl.BlockSpec(memory_space=pl.ANY)


def block(i):
    return pl.ds(pl.multiple_of(i * BLOCK, BLOCK), BLOCK)


def params(mib):
    return pltpu.CompilerParams(vmem_limit_bytes=mib * MIB)


def valid_rows(i, seq):
    return (lax.broadcasted_iota(jnp.int32, (BLOCK, 1), 0) + i * BLOCK < seq).astype(F32)


def unpack_small(small, dn, d, vec_out):
    n = small.shape[0]
    gw = d // GROUPS
    line = lambda row, width: jnp.concatenate([small[s, row:row + 1, :width] for s in range(n)], axis=1)
    vec_out[...] = jnp.zeros_like(vec_out)
    for i in range(6):
        vec_out[i:i + 1, :] = line(i, dn)
    qkv = line(6, 3 * dn)
    for j in range(GROUPS):
        vec_out[QKV_BIAS + j:QKV_BIAS + j + 1, :] = jnp.concatenate([qkv[:, a * d + j * gw:a * d + (j + 1) * gw] for a in range(3)], axis=1)
    up = line(7, small.shape[2])
    for j in range(up.shape[1] // d):
        vec_out[UP_BIAS + j:UP_BIAS + j + 1, :] = up[:, j * d:(j + 1) * d]


def prepare_kernel(plan, waits, sc_ref, x_ref, g_ref, packed, up_ref, down_ref, *rest):
    n1, n1t, n2, n2t, gl, vec_out, token, pick, sems = rest[waits:]
    d = x_ref.shape[1]
    par_ref = vec_out
    if plan["on"]:
        dn, rep = plan["dn"], sc_ref[3]
        cut = [pltpu.make_async_copy(up_ref.at[:, pl.ds(pl.multiple_of(rep * d, 128), d)], pick.at[0], sems.at[0]),
               pltpu.make_async_copy(down_ref.at[pl.ds(pl.multiple_of(rep * dn, 16), dn)], pick.at[1], sems.at[1])]

        @pl.when(pl.program_id(0) == 0)
        def _():
            for c in cut:
                c.start()
            unpack_small(packed[0].astype(F32) + packed[1].astype(F32) + packed[2].astype(F32) + packed[3].astype(F32), dn, d, vec_out)

        @pl.when(pl.program_id(0) == pl.num_programs(0) - 1)
        def _():
            for c in cut:
                c.wait()

    else:
        vec_out[...] = packed[...]
    token[...] = jnp.zeros_like(token)
    normed, _ = norm_parts(x_ref[...].astype(F32))
    one = (normed * par_ref[0:1, :] + par_ref[1:2, :]).astype(BF)
    two = (normed * par_ref[2:3, :] + par_ref[3:4, :]).astype(BF)
    n1[...] = one
    n2[...] = two
    n1t[...] = one.astype(F32).T.astype(BF)
    n2t[...] = two.astype(F32).T.astype(BF)
    gl[...] = (g_ref[...].astype(F32) * valid_rows(pl.program_id(0), sc_ref[0])).astype(BF)


def prepare(plan, scalars, x, g, par, up, down, waits):
    rows, d = x.shape
    flat, turned = jax.ShapeDtypeStruct((rows, d), BF), jax.ShapeDtypeStruct((d, rows), BF)
    vecs = (16, d) if plan["on"] else par.shape
    by_rows, by_cols = pl.BlockSpec((BLOCK, d), lambda i: (i, 0)), pl.BlockSpec((d, BLOCK), lambda i: (0, i))
    return pl.pallas_call(
        lambda *refs: prepare_kernel(plan, len(waits), *refs),
        grid_spec=pl.GridSpec(grid=(rows // BLOCK,), in_specs=[SM, by_rows, by_rows, pl.BlockSpec(par.shape, lambda i: (0,) * par.ndim), ANY, ANY] + [ANY] * len(waits),
                              out_specs=[by_rows, by_cols, by_rows, by_cols, by_rows, pl.BlockSpec(vecs, lambda i: (0, 0)), pl.BlockSpec((1, d), lambda i: (0, 0)), pl.BlockSpec((2, plan["dn"], d), lambda i: (0, 0, 0))],
                              scratch_shapes=[pltpu.SemaphoreType.DMA((2,))]),
        out_shape=[flat, turned, flat, turned, flat, jax.ShapeDtypeStruct(vecs, F32), jax.ShapeDtypeStruct((1, d), BF),
                   jax.ShapeDtypeStruct((2, plan["dn"], d), BF)], compiler_params=params(60), name="prepare",
        cost_estimate=pl.CostEstimate(flops=40 * rows * d, bytes_accessed=14 * rows * d, transcendentals=rows),
    )(scalars, x, g, par, up, down, *waits)


def attn_kernel(plan, first, base, sc_ref, n1, gl, b3_ref, keep_ref, up_ref, down_ref, *rest):
    nw = plan["pieces"] if first else 2
    w_refs, rest = rest[:nw], rest[nw:]
    d3, ctx_low, sm_ref, token, rest = rest[0].at[0], rest[1].at[0], rest[2].at[0], rest[3], rest[4:]
    token[...] = jnp.zeros_like(token)
    rows, d = n1.shape
    gw = d // GROUPS
    qb = BLOCK
    nb = rows // qb
    seq = sc_ref[0]
    if first:
        w_out, rest = rest[0], rest[1:]
    q_s, k_s, v_s, dc_s, ctx, dq, dk, dv, qm, km, vm, dcm, pall, dall = rest[:14]

    if first:
        w, sems = rest[14:]
        if plan["on"]:
            z, core, rep = sc_ref[1], sc_ref[2], sc_ref[3]
            dn, nz, nr = plan["dn"], plan["nz"], plan["nr"]
            own, sib, near, sibs = w_refs[0], w_refs[1], w_refs[2:2 + nr], w_refs[2 + nr]
            place = lambda zz, cc: pl.ds(pl.multiple_of((zz * 2 + cc) * dn, 16), dn)
            pairs = []
            for m in range(nr):
                pairs.append((own.at[m], w.at[m, place(z, core)]))
                pairs.append((sib.at[m], w.at[m, place(z, 1 - core)]))
            for j in range(nr):
                for k in range(1, nz):
                    m, zz = rep ^ j, z ^ k
                    pairs.append((near[j].at[k - 1], w.at[m, place(zz, core)]))
                    pairs.append((sibs.at[j, k - 1], w.at[m, place(zz, 1 - core)]))
        else:
            pairs = [(w_refs[0].at[m], w.at[m]) for m in range(GROUPS + 1)]
        copies = [pltpu.make_async_copy(a, b, sems.at[i]) for i, (a, b) in enumerate(pairs)]
        for c in copies:
            c.start()
        for c in copies:
            c.wait()
        back = pltpu.make_async_copy(w, w_out, sems.at[len(pairs)])
        back.start()
        w3, wo = w.at[0], w.at[GROUPS, 0:gw]
    else:
        w3, wo = w_refs[0].at[0], w_refs[1].at[0]
    half = ROT // 2

    def tables(r):
        return tuple(jnp.concatenate([t[r, :]] * (gw // 128), axis=1) for t in (keep_ref, up_ref, down_ref))

    def project(i, c):
        r = block(i)
        t = mm(n1[r, :], w3[...]) + b3_ref[pl.ds(QKV_BIAS + base + pl.program_id(0), 1), :]
        keep, up, down = tables(r)
        for at, ref, scale in ((0, q_s, HEAD_DIM ** -0.5), (1, k_s, None)):
            v = t[:, at * gw:(at + 1) * gw]
            low = (v * keep + pltpu.roll(v, gw - half, 1) * up + pltpu.roll(v, half, 1) * down).astype(BF)
            ref[r, :] = low if scale is None else (low.astype(F32) * scale).astype(BF)
        v_s[r, :] = t[:, 2 * gw:].astype(BF)
        dc_s[r, :] = mm_rt(gl[r, :], wo[...]).astype(BF)
        return c
    lax.fori_loop(0, nb, project, 0, unroll=True)

    key_bias = jnp.where(lax.broadcasted_iota(jnp.int32, (1, rows), 1) < seq, 0.0, MASKED).astype(F32)
    causal = lax.broadcasted_iota(jnp.int32, (qb, qb), 1) <= lax.broadcasted_iota(jnp.int32, (qb, qb), 0)

    heads = gw // HEAD_DIM

    def head(h, c):
        lane = lax.broadcasted_iota(jnp.int32, (1, gw), 1) // HEAD_DIM
        mask = jnp.where(lane == h, 1.0, 0.0).astype(BF)
        for ref, out in ((q_s, qm), (k_s, km), (v_s, vm), (dc_s, dcm)):
            out[h] = ref[...] * mask
        for i in range(nb):
            lo, kl = i * qb, (i + 1) * qb
            s = mm_rt(qm[h, lo:kl, :], k_s[:kl, :]) + key_bias[:, :kl]
            diag = jnp.where(causal, s[:, lo:], MASKED)
            s = diag if i == 0 else jnp.concatenate([s[:, :lo], diag], axis=1)
            dp = mm_rt(dcm[h, lo:kl, :], v_s[:kl, :])
            e = jnp.exp(s - jnp.max(s, axis=1, keepdims=True))
            p = e * (1.0 / jnp.sum(e, axis=1, keepdims=True))
            pall[h, lo:kl, :kl] = p.astype(BF)
            inner = jnp.sum(p * dp, axis=1, keepdims=True)
            dall[h, lo:kl, :kl] = (p * (dp - inner)).astype(BF)
        return c
    lax.fori_loop(0, heads, head, 0, unroll=2)
    for i in range(nb):
        lo, kl = i * qb, (i + 1) * qb
        ctx[lo:kl, :] = sum(mm(pall[h, lo:kl, :kl], vm[h, :kl, :]) for h in range(heads))
        dq[lo:kl, :] = sum(mm(dall[h, lo:kl, :kl], km[h, :kl, :]) for h in range(heads))
        dv[lo:kl, :] = sum(mm_lt(pall[h, lo:, lo:kl], dcm[h, lo:, :]) for h in range(heads))
        dk[lo:kl, :] = sum(mm_lt(dall[h, lo:, lo:kl], qm[h, lo:, :]) for h in range(heads))

    def finish(i, total):
        r = block(i)
        keep, up, down = tables(r)
        parts = []
        for ref, scale in ((dq, HEAD_DIM ** -0.5), (dk, 1.0)):
            v = ref[r, :] * scale
            parts.append(v * keep - pltpu.roll(v, gw - half, 1) * up - pltpu.roll(v, half, 1) * down)
        low = jnp.concatenate(parts + [dv[r, :]], axis=1).astype(BF)
        d3[r, :] = low
        ctx_low[r, :] = ctx[r, :].astype(BF)
        return total + jnp.sum(low.astype(F32), axis=0, keepdims=True)
    db3 = lax.fori_loop(0, nb, finish, jnp.zeros((1, d), F32), unroll=True)
    sm_ref[...] = jnp.broadcast_to(db3, sm_ref.shape)
    if first:
        back.wait()


def attention(plan, groups, scalars, n1, gl, b3, tables, weights):
    rows, d = n1.shape
    gw = d // GROUPS
    first, count, base = groups[0] == 0, len(groups), groups[0]
    plan = dict(plan, pieces=len(weights))
    whole = lambda *shape: pl.BlockSpec(shape, lambda j: (0,) * len(shape))
    stacked = lambda *shape: pl.BlockSpec((1,) + shape, lambda j: (j,) + (0,) * len(shape))
    out_shape = [jax.ShapeDtypeStruct((count, rows, d), BF), jax.ShapeDtypeStruct((count, rows, gw), BF), jax.ShapeDtypeStruct((count, 8, d), F32), jax.ShapeDtypeStruct((1, d), BF)]
    out_specs = [stacked(rows, d), stacked(rows, gw), stacked(8, d), whole(1, d)]
    heads = gw // HEAD_DIM
    scratch = [pltpu.VMEM((rows, gw), BF)] * 4 + [pltpu.VMEM((rows, gw), F32)] * 4
    scratch += [pltpu.VMEM((heads, rows, gw), BF)] * 4 + [pltpu.VMEM((heads, rows, rows), BF)] * 2
    if first:
        out_shape.append(jax.ShapeDtypeStruct((GROUPS + 1, d, d), BF))
        out_specs.append(ANY)
        scratch += [pltpu.VMEM((GROUPS + 1, d, d), BF), pltpu.SemaphoreType.DMA((64,))]
        w_specs = [ANY] * len(weights)
    else:
        weights = [weights[0], weights[0]]
        w_specs = [pl.BlockSpec((1, d, d), lambda j: (base + j, 0, 0)), pl.BlockSpec((1, gw, d), lambda j: (GROUPS, base + j, 0))]
    flops = count * (2 * rows * d * (d + gw) + 12 * HEADS // GROUPS * rows * rows * HEAD_DIM)
    return pl.pallas_call(
        lambda *refs: attn_kernel(plan, first, base, *refs),
        grid_spec=pl.GridSpec(
            grid=(count,),
            in_specs=[SM, whole(rows, d), whole(rows, d), whole(*b3.shape)] + [whole(rows, 128)] * 3 + w_specs,
            out_specs=out_specs, scratch_shapes=scratch),
        out_shape=out_shape, compiler_params=params(60), name="attend_first" if first else "attend_rest",
        cost_estimate=pl.CostEstimate(flops=4 * flops, bytes_accessed=8_000_000, transcendentals=count * HEADS * rows * rows // GROUPS),
    )(scalars, n1, gl, b3, *tables, *weights)


def write_halves(value, tmp, keep_ref, send_ref, core, dn):
    tmp[...] = value.astype(BF)
    for z in range(keep_ref.shape[0]):
        mine = pl.ds(pl.multiple_of((2 * z + core) * dn, 16), dn)
        other = pl.ds(pl.multiple_of((2 * z + 1 - core) * dn, 16), dn)
        keep_ref[z, 0] = tmp[mine, :]
        send_ref[z, 0] = tmp[other, :]


def closing_kernel(plan, sc_ref, x_ref, gl, n1t, par_ref, w, d3a, d3b, ctxa, ctxb, sma, smb, *rest):
    nd = 2 if plan["on"] else 1
    dw_refs, rest = rest[:nd], rest[nd:]
    sm_ref, ff_ref, gf, tmp = rest
    step = pl.program_id(0)
    rows, d = x_ref.shape
    nb = rows // BLOCK

    def store(dw):
        if plan["on"]:
            write_halves(dw, tmp, dw_refs[0], dw_refs[1], sc_ref[2], plan["dn"])
        else:
            dw_refs[0][0] = dw.astype(BF)
        return jnp.sum(dw * dw, axis=0, keepdims=True)

    def group(first, d3, db3):
        def body(i, c):
            r = block(i)
            part = mm_rt(d3[0, r, :], w[0])
            gf[r, :] = part if first else gf[r, :] + part
            return c
        lax.fori_loop(0, nb, body, 0, unroll=True)
        total = store(mm(n1t[...], d3[0])) + db3 * db3
        sm_ref[pl.ds(2 + step, 1), :] = db3
        sm_ref[5:6, :] = total if first else sm_ref[5:6, :] + total

    @pl.when(step == 0)
    def _():
        group(True, d3a, sma[0, 0:1, :])

    @pl.when(jnp.logical_and(step > 0, step < GROUPS))
    def _():
        group(False, d3b, smb[0, 0:1, :])

    @pl.when(step == GROUPS)
    def _():
        total = store(mm_lt(jnp.concatenate([ctxa[0]] + [ctxb[g] for g in range(GROUPS - 1)], axis=1), gl[...]))

        def back(i, c):
            r = block(i)
            normed, inverse = norm_parts(x_ref[r, :].astype(F32))
            e = gf[r, :]
            ff_ref[r, :] = norm_back(e, par_ref[0:1, :], normed, inverse)
            return (c[0] + jnp.sum(e * normed, axis=0, keepdims=True), c[1] + jnp.sum(e, axis=0, keepdims=True))
        zero = jnp.zeros((1, d), F32)
        dgain, dshift = lax.fori_loop(0, nb, back, (zero, zero), unroll=True)
        sm_ref[0:1, :] = dgain
        sm_ref[1:2, :] = dshift
        sm_ref[5:6, :] += total + dgain * dgain + dshift * dshift


def closing(plan, scalars, x, gl, n1t, par, w, d3a, d3b, ctxa, ctxb, sma, smb):
    rows, d = x.shape
    gw = d // GROUPS
    whole = lambda *shape: pl.BlockSpec(shape, lambda j: (0,) * len(shape))
    later = lambda *shape: pl.BlockSpec((1,) + shape, lambda j: (jnp.clip(j - 1, 0, GROUPS - 2),) + (0,) * len(shape))
    if plan["on"]:
        nz, dn = plan["nz"], plan["dn"]
        dw_specs = [pl.BlockSpec((nz, 1, dn, d), lambda j: (0, j, 0, 0))] * 2
        dw_shapes = [jax.ShapeDtypeStruct((nz, GROUPS + 1, dn, d), BF)] * 2
    else:
        dw_specs = [pl.BlockSpec((1, d, d), lambda j: (j, 0, 0))]
        dw_shapes = [jax.ShapeDtypeStruct((GROUPS + 1, d, d), BF)]
    return pl.pallas_call(
        lambda *refs: closing_kernel(plan, *refs),
        grid_spec=pl.GridSpec(
            grid=(GROUPS + 1,),
            in_specs=[SM, whole(rows, d), whole(rows, d), whole(d, rows), whole(*par.shape),
                      pl.BlockSpec((1, d, d), lambda j: (jnp.minimum(j, GROUPS - 1), 0, 0)),
                      whole(1, rows, d), later(rows, d), whole(1, rows, gw), whole(GROUPS - 1, rows, gw), whole(1, 8, d), later(8, d)],
            out_specs=dw_specs + [whole(8, d), whole(rows, d)],
            scratch_shapes=[pltpu.VMEM((rows, d), F32), pltpu.VMEM((d, d), BF)],
        ),
        out_shape=dw_shapes + [jax.ShapeDtypeStruct((8, d), F32), jax.ShapeDtypeStruct((rows, d), F32)],
        compiler_params=params(60), name="closing",
        cost_estimate=pl.CostEstimate(flops=4 * rows * d * 7 * d, bytes_accessed=8_000_000, transcendentals=rows),
    )(scalars, x, gl, n1t, par, w, d3a, d3b, ctxa, ctxb, sma, smb)


ERF_P = 0.3275911
ERF_A = (0.254829592, -0.284496736, 1.421413741, -1.453152027, 1.061405429)


def gelu_parts(u):
    z = jnp.abs(u) * (2.0 ** -0.5)
    t = 1.0 / (1.0 + ERF_P * z)
    bell = jnp.exp(-0.5 * (u * u))
    a1, a2, a3, a4, a5 = (0.5 * a for a in ERF_A)
    tail = ((((a5 * t + a4) * t + a3) * t + a2) * t + a1) * t * bell
    cdf = jnp.where(u >= 0.0, 1.0 - tail, tail)
    return u * cdf, cdf + u * bell * (1.0 / math.sqrt(2.0 * math.pi))


def ffn_kernel(plan, sc_ref, x_ref, gl, n2, n2t, par_ref, ff_ref, sm1_ref, *rest):
    nw = plan["pieces"]
    w_refs, rest = rest[:nw], rest[nw:]
    nd = 4 if plan["on"] else 2
    dw_refs, rest = rest[:nd], rest[nd:]
    sm_ref, norm_ref, act_ref, wd_ref, gx_ref = rest[:5]
    wu_s, wd_s, gs, gup, sq, tmp, x_s, ff_s, up_sems, down_sems, late_sems = rest[5:]
    late = [pltpu.make_async_copy(x_ref, x_s, late_sems.at[0]), pltpu.make_async_copy(ff_ref, ff_s, late_sems.at[1])]
    step = pl.program_id(0)
    last = pl.num_programs(0) - 1
    rows, d = x_ref.shape
    fc = d
    nb = rows // BLOCK

    @pl.when(step == 0)
    def _():
        if plan["on"]:
            z, core, rep = sc_ref[1], sc_ref[2], sc_ref[3]
            dn, nz, nr = plan["dn"], plan["nz"], plan["nr"]
            own_up, own_down, sib_up, sib_down = w_refs[:4]
            near, sibs = w_refs[4:4 + nr], w_refs[4 + nr]

            def up(src, m, zz, cc):
                dst = wu_s.at[m, pl.ds(pl.multiple_of((zz * 2 + cc) * dn, 16), dn)]
                pltpu.make_async_copy(src, dst, up_sems.at[m]).start()

            def down(src, b, zz, cc):
                dst = wd_s.at[zz, pl.ds(pl.multiple_of((cc * nr + b) * dn, 16), dn)]
                pltpu.make_async_copy(src, dst, down_sems.at[zz]).start()
            for m in range(nr):
                cols, part = pl.ds(m * d, d), pl.ds(m * dn, dn)
                up(own_up.at[:, cols], m, z, core)
                up(sib_up.at[:, cols], m, z, 1 - core)
                down(own_down.at[part], m, z, core)
                down(sib_down.at[part], m, z, 1 - core)
            for j in range(nr):
                for k in range(1, nz):
                    up(near[j].at[k - 1, 0], rep ^ j, z ^ k, core)
                    up(sibs.at[j, k - 1, 0], rep ^ j, z ^ k, 1 - core)
                    down(near[j].at[k - 1, 1], rep ^ j, z ^ k, core)
                    down(sibs.at[j, k - 1, 1], rep ^ j, z ^ k, 1 - core)
        else:
            for m in range(wu_s.shape[0]):
                pltpu.make_async_copy(w_refs[0].at[m], wu_s.at[m], up_sems.at[m]).start()
                pltpu.make_async_copy(w_refs[1].at[m], wd_s.at[m], down_sems.at[m]).start()
        for c in late:
            c.start()
        gs[...] = jnp.zeros_like(gs)
        sq[...] = jnp.zeros_like(sq)
        sm_ref[...] = jnp.zeros_like(sm_ref)

    pltpu.make_async_copy(wu_s.at[step], wu_s.at[step], up_sems.at[step]).wait()
    pltpu.make_async_copy(wd_s.at[step], wd_s.at[step], down_sems.at[step]).wait()
    wu, wd = wu_s.at[step], wd_s.at[step]
    wd_ref[0] = wd[...]

    def rows_step(i, dbu):
        r = block(i)
        u = mm(n2[r, :], wu[...]) + par_ref[pl.ds(UP_BIAS + step, 1), :]
        da = mm_rt(gl[r, :], wd[...])
        a, slope = gelu_parts(u)
        act_ref[0, r, :] = a.astype(BF)
        gu = (da * slope).astype(BF)
        gup[r, :] = gu
        gs[r, :] += mm_rt(gu, wu[...])
        return dbu + jnp.sum(gu.astype(F32), axis=0, keepdims=True)
    dbu = lax.fori_loop(0, nb, rows_step, jnp.zeros((1, fc), F32), unroll=True)
    sm_ref[pl.ds(8 + step, 1), :] = dbu

    dwu = mm(n2t[...], gup[...])
    total = jnp.sum(dwu * dwu, axis=0, keepdims=True) + dbu * dbu
    if plan["on"]:
        write_halves(dwu, tmp, dw_refs[0], dw_refs[1], sc_ref[2], plan["dn"])
    else:
        dw_refs[0][0] = dwu.astype(BF)
    dwd = mm_lt(act_ref[0], gl[...])
    total += jnp.sum(dwd * dwd, axis=0, keepdims=True)
    if plan["on"]:
        tmp[...] = dwd.astype(BF)
        core, dn, nr = sc_ref[2], plan["dn"], plan["nr"]
        for m in range(nr):
            dw_refs[2][0, m] = tmp[pl.ds(pl.multiple_of((core * nr + m) * dn, 16), dn), :]
            dw_refs[3][0, m] = tmp[pl.ds(pl.multiple_of(((1 - core) * nr + m) * dn, 16), dn), :]
    else:
        dw_refs[1][0] = dwd.astype(BF)
    sq[...] += total

    @pl.when(step == last)
    def _():
        for c in late:
            c.wait()

        def back(i, c):
            r = block(i)
            normed, inverse = norm_parts(x_s[r, :].astype(F32))
            e = gs[r, :]
            grad_rows = gl[r, :].astype(F32)
            gx_ref[r, :] = (grad_rows + ff_s[r, :] + norm_back(e, par_ref[2:3, :], normed, inverse)).astype(BF)
            return (c[0] + jnp.sum(e * normed, axis=0, keepdims=True), c[1] + jnp.sum(e, axis=0, keepdims=True),
                    c[2] + jnp.sum(grad_rows, axis=0, keepdims=True))
        zero = jnp.zeros((1, d), F32)
        dgain, dshift, dbd = lax.fori_loop(0, nb, back, (zero, zero, zero), unroll=True)
        sm_ref[0:2, :] = sm1_ref[0:2, :]
        sm_ref[2:3, :] = dgain
        sm_ref[3:4, :] = dshift
        sm_ref[4:5, :] = dbd
        sm_ref[5:8, :] = sm1_ref[2:5, :]
        final = sq[...] + sm1_ref[5:6, :] + dgain * dgain + dshift * dshift + 2.0 * dbd * dbd
        own = jnp.sqrt(jnp.sum(final, axis=1, keepdims=True))
        here = lax.broadcasted_iota(jnp.int32, norm_ref.shape, 1) == sc_ref[4]
        norm_ref[...] = jnp.where(here, own, 0.0)


def ffn(plan, chunks, scalars, x, gl, n2, n2t, par, ff, sm1, weights, norm_width):
    rows, d = x.shape
    plan = dict(plan, pieces=len(weights))
    whole = lambda *shape: pl.BlockSpec(shape, lambda j: (0,) * len(shape))
    if plan["on"]:
        nz, dn, nr = plan["nz"], plan["dn"], plan["nr"]
        dw_specs = [pl.BlockSpec((nz, 1, dn, d), lambda j: (0, j, 0, 0))] * 2 + [pl.BlockSpec((1, nr, dn, d), lambda j: (j, 0, 0, 0))] * 2
        dw_shapes = [jax.ShapeDtypeStruct((nz, chunks, dn, d), BF)] * 2 + [jax.ShapeDtypeStruct((nz, nr, dn, d), BF)] * 2
    else:
        dw_specs = [pl.BlockSpec((1, d, d), lambda j: (j, 0, 0))] * 2
        dw_shapes = [jax.ShapeDtypeStruct((chunks, d, d), BF)] * 2
    return pl.pallas_call(
        lambda *refs: ffn_kernel(plan, *refs),
        grid_spec=pl.GridSpec(
            grid=(chunks,),
            in_specs=[SM, ANY, whole(rows, d), whole(rows, d), whole(d, rows), whole(*par.shape), ANY, whole(8, d)] + [ANY] * len(weights),
            out_specs=dw_specs + [whole(SMALL, d), whole(1, norm_width), pl.BlockSpec((1, rows, d), lambda j: (j, 0, 0)),
                                  pl.BlockSpec((1, d, d), lambda j: (j, 0, 0)), whole(rows, d)],
            scratch_shapes=[
                pltpu.VMEM((chunks, d, d), BF), pltpu.VMEM((chunks, d, d), BF), pltpu.VMEM((rows, d), F32), pltpu.VMEM((rows, d), BF),
                pltpu.VMEM((1, d), F32), pltpu.VMEM((d, d), BF), pltpu.VMEM((rows, d), BF), pltpu.VMEM((rows, d), F32),
                pltpu.SemaphoreType.DMA((chunks,)), pltpu.SemaphoreType.DMA((chunks,)), pltpu.SemaphoreType.DMA((2,)),
            ],
        ),
        out_shape=dw_shapes + [
            jax.ShapeDtypeStruct((SMALL, d), F32), jax.ShapeDtypeStruct((1, norm_width), F32),
            jax.ShapeDtypeStruct((chunks, rows, d), BF), jax.ShapeDtypeStruct((chunks, d, d), BF), jax.ShapeDtypeStruct((rows, d), BF),
        ],
        compiler_params=params(60), name="feedforward",
        cost_estimate=pl.CostEstimate(flops=2 * 5 * rows * d * d * chunks * 2, bytes_accessed=40_000_000, transcendentals=rows * d * chunks),
    )(scalars, x, gl, n2, n2t, par, ff, sm1, *weights)


def output_kernel(sc_ref, x_ref, par_ref, token, wo, wd, act, *rest):
    ctxs, out_ref = rest[:2], rest[2]
    d = x_ref.shape[1]
    gw = d // GROUPS
    total = x_ref[...].astype(F32) + par_ref[4:5, :] + par_ref[5:6, :]
    for g in range(GROUPS):
        ctx = ctxs[0][0] if g == 0 else ctxs[1][g - 1]
        total += mm(ctx, wo[0, g * gw:(g + 1) * gw, :])
    for j in range(wd.shape[0]):
        total += mm(act[j], wd[j])
    out_ref[...] = (total * valid_rows(pl.program_id(0), sc_ref[0])).astype(BF)


def output(scalars, x, par, token, w, wd, act, ctxs):
    rows, d = x.shape
    gw = d // GROUPS
    chunks = wd.shape[0]
    return pl.pallas_call(
        output_kernel,
        grid_spec=pl.GridSpec(
            grid=(rows // BLOCK,),
            in_specs=[SM, pl.BlockSpec((BLOCK, d), lambda i: (i, 0)), pl.BlockSpec(par.shape, lambda i: (0, 0)), pl.BlockSpec(token.shape, lambda i: (0, 0)),
                      pl.BlockSpec((1, d, d), lambda i: (GROUPS, 0, 0)), pl.BlockSpec((chunks, d, d), lambda i: (0, 0, 0)),
                      pl.BlockSpec((chunks, BLOCK, d), lambda i: (0, i, 0))] + [pl.BlockSpec((1, BLOCK, gw), lambda i: (0, i, 0)), pl.BlockSpec((GROUPS - 1, BLOCK, gw), lambda i: (0, i, 0))],
            out_specs=pl.BlockSpec((BLOCK, d), lambda i: (i, 0)),
        ),
        out_shape=jax.ShapeDtypeStruct((rows, d), BF),
        compiler_params=params(28), name="output",
        cost_estimate=pl.CostEstimate(flops=2 * rows * d * d * (chunks + 1), bytes_accessed=18_000_000, transcendentals=0),
    )(scalars, x, par, token, w, wd, act, *ctxs)


def spread(rows_ref, lane):
    norms = rows_ref
    at = lax.broadcasted_iota(jnp.int32, norms.shape, 1)
    own = jnp.sum(jnp.where(at == lane, norms, 0.0), axis=1, keepdims=True)
    return own


def mix_kernel(seqs, sending, sc_ref, r0, r1, sm, smg, dk, dg, uk, ug, ak, ag, token, d_ref, u_ref, a_ref, norm_out, ins, in_sems, *rest):
    flip = 1 if sending else 0
    xb, yb, lob = flip ^ (sc_ref[3] % 2), flip ^ (sc_ref[3] // 2), flip ^ (sc_ref[1] % 2)
    dn = dk.shape[4]
    d_out, u_out, a_out, out_sems = rest if sending else (d_ref, u_ref, a_ref, None)
    jobs = []
    for i in range(4):
        jobs.append(([v.at[i // 2, lob, i % 2] for v in (dk, dg)], i))
    for i in range(4):
        jobs.append(([v.at[i, yb] for v in (uk, ug)], 4 + i))
    for i in range(4):
        jobs.append(([v.at[i, :, xb] for v in (ak, ag)], 8 + i))
    reads = [[pltpu.make_async_copy(src, ins.at[at, t], in_sems.at[2 * at + t]) for t, src in enumerate(srcs)] for srcs, at in jobs]
    for pair in reads:
        for c in pair:
            c.start()
    norms = r0[...] + r1[...]
    norm_out[...] = norms
    mean = jnp.sum(norms, axis=1, keepdims=True) * (1.0 / seqs)
    me = sc_ref[4]
    factor = jnp.minimum(1.0, mean / spread(norms, me)) * (1.0 / seqs)
    other = jnp.minimum(1.0, mean / spread(norms, me ^ 1)) * (1.0 / seqs)
    factor, other = factor[0, 0], other[0, 0]
    mixed = lambda k, g: (k.astype(F32) * factor + g.astype(F32) * other).astype(BF)
    d_out[8 * dn:, :] = mixed(sm[...], smg[...])
    writes = []
    for pair, (_, at) in zip(reads, jobs):
        for c in pair:
            c.wait()
        for t in range(2):
            low = mixed(ins[at, 0, t], ins[at, 1, t])
            if at < 4:
                d_out[(2 * at + t) * dn:(2 * at + t + 1) * dn, :] = low
            elif at < 8:
                u_out[at - 4, 0, t] = low
            else:
                a_out[at - 8, t, 0] = low
        if sending and at % 4 == 3:
            src, dst = ((d_out, d_ref), (u_out, u_ref), (a_out, a_ref))[at // 4]
            writes.append(pltpu.make_async_copy(src, dst, out_sems.at[at // 4]))
            writes[-1].start()
    for c in writes:
        c.wait()


def mix(seqs, sending, scalars, norm_rows, halves, smalls, token):
    dn, d = halves[0].shape[2:]
    ak, ag, uk, ug = (v.reshape(4, 2, 2, dn, d) for v in halves[:4])
    dk, dg = (v.reshape(2, 2, 2, 2, dn, d) for v in halves[4:])
    width = norm_rows[0].shape[1]
    shapes = [(8 * dn + SMALL, d), (4, 1, 2, dn, d), (4, 2, 1, dn, d)]
    scratch = [pltpu.VMEM((12, 2, 2, dn, d), BF), pltpu.SemaphoreType.DMA((24,))]
    if sending:
        scratch += [pltpu.VMEM(s, BF) for s in shapes] + [pltpu.SemaphoreType.DMA((3,))]
    dd, u, a, norms = pl.pallas_call(
        lambda *refs: mix_kernel(seqs, sending, *refs),
        in_specs=[SM] + [VM] * 4 + [ANY] * 7, out_specs=[ANY if sending else VM] * 3 + [VM],
        out_shape=[jax.ShapeDtypeStruct(s, BF) for s in shapes] + [jax.ShapeDtypeStruct((1, width), F32)],
        scratch_shapes=scratch, compiler_params=params(60 if sending else 54), name="mix_send" if sending else "mix_keep",
        cost_estimate=pl.CostEstimate(flops=16_000_000, bytes_accessed=10_600_000, transcendentals=0),
    )(scalars, *norm_rows, *smalls, dk, dg, uk, ug, ak, ag, token)
    return a.reshape(2, 2, 2, 1, dn, d), u.reshape(2, 2, 1, 2, dn, d), dd, norms


def fold_flat_kernel(name, blocks, sc_ref, mine, got, *rest):
    send, keep = rest[-2:]
    dn = send.shape[0] - SMALL
    dn = dn // (blocks // 2)
    add = lambda a, b: (a.astype(F32) + b.astype(F32)).astype(BF)
    bit = side(name, sc_ref, 0)
    for out, which in ((send, 1 ^ bit), (keep, bit)):
        for i in range(blocks // 2):
            rows = pl.ds(pl.multiple_of((2 * i + which) * dn, 16), dn)
            out[i * dn:(i + 1) * dn, :] = add(mine[rows, :], got[rows, :])
        out[blocks // 2 * dn:, :] = add(mine[blocks * dn:, :], got[blocks * dn:, :])


def fold_flat(scalars, name, blocks, mine, got, waits=()):
    total, d = mine.shape
    half = jax.ShapeDtypeStruct(((total - SMALL) // 2 + SMALL, d), BF)
    return pl.pallas_call(
        lambda *refs: fold_flat_kernel(name, blocks, *refs),
        in_specs=[SM, VM, VM] + [ANY] * len(waits), out_specs=[VM, VM], out_shape=[half, half],
        compiler_params=params(16), name="fold_flat_" + name,
        cost_estimate=pl.CostEstimate(flops=mine.size, bytes_accessed=6 * mine.size, transcendentals=0),
    )(scalars, mine, got, *waits)


AXES = dict(hi=0, lo=1, y=2, x=3)


def side(name, sc, flip):
    bit = {"hi": sc[1] // 2, "lo": sc[1] % 2, "y": sc[3] // 2, "x": sc[3] % 2}[name]
    return flip ^ bit


def fold_kernel(sc_ref, ms, gs, mk, gk, *rest):
    send, keep = rest[-2:]
    d = ms.shape[-1]
    add = lambda a, b, out: (a[...].reshape(-1, d).astype(F32) + b[...].reshape(-1, d).astype(F32)).astype(BF).reshape(out.shape)
    send[...] = add(ms, gs, send)
    keep[...] = add(mk, gk, keep)


def fold(scalars, name, mine, got, waits=()):
    axis = AXES[name]
    shape = mine.shape
    blk = (1,) + tuple(1 if i == axis else s for i, s in enumerate(shape) if i > 0)
    spec = lambda flip: pl.BlockSpec(blk, lambda i, sc: (i,) + tuple(side(name, sc, flip) if k == axis else 0 for k in range(1, 6)))
    out = pl.BlockSpec(blk, lambda i, sc: (i, 0, 0, 0, 0, 0))
    half = jax.ShapeDtypeStruct((shape[0],) + blk[1:], BF)
    return pl.pallas_call(
        fold_kernel,
        grid_spec=pltpu.PrefetchScalarGridSpec(num_scalar_prefetch=1, grid=(shape[0],), in_specs=[spec(1), spec(1), spec(0), spec(0)] + [ANY] * len(waits), out_specs=[out, out]),
        out_shape=[half, half], compiler_params=params(16), name="fold_" + name,
        cost_estimate=pl.CostEstimate(flops=mine.size, bytes_accessed=6 * mine.size, transcendentals=0),
    )(scalars, mine, got, mine, got, *waits)


def last_fold_kernel(sc_ref, am, ag, um, ug, dm, dg, send1, send2, keep1, keep2):
    dn = am.shape[4]
    first = send1.shape[0]
    add = lambda a, b: (a.astype(F32) + b.astype(F32)).astype(BF)
    bit = side("hi", sc_ref, 0)
    small = add(dm[2 * dn:, :], dg[2 * dn:, :])
    for out1, out2, which in ((send1, send2, 1 ^ bit), (keep1, keep2, bit)):
        at = 0

        def put(low):
            nonlocal at
            rows = low.shape[0]
            split = min(max(first - at, 0), rows)
            if split > 0:
                out1[at:at + split, :] = low[:split]
            if split < rows:
                out2[at + split - first:at + rows - first, :] = low[split:]
            at += rows
        put(add(am[which, 0, 0, 0], ag[which, 0, 0, 0]))
        put(add(um[which, 0, 0, 0], ug[which, 0, 0, 0]))
        rows = pl.ds(pl.multiple_of(which * dn, 16), dn)
        put(add(dm[rows, :], dg[rows, :]))
        put(small)


def last_fold(scalars, parts, first):
    dn, d = parts[0][0].shape[4:]
    total = 3 * dn + SMALL
    half = [jax.ShapeDtypeStruct((s, d), BF) for s in (first, total - first)]
    return pl.pallas_call(
        last_fold_kernel, in_specs=[SM] + [VM] * 6, out_specs=[VM] * 4, out_shape=half + half,
        compiler_params=params(16), name="last_fold",
        cost_estimate=pl.CostEstimate(flops=2 * total * d, bytes_accessed=12 * total * d, transcendentals=0),
    )(scalars, *[v for pair in parts for v in pair])


def xor_permute(value, axis, size, bit):
    return lax.ppermute(value, axis, [(i, i ^ bit) for i in range(size)])


def butterfly(value, axis, size):
    if size & (size - 1):
        return lax.psum(value, axis)
    bit = 1
    while bit < size:
        value = value + xor_permute(value, axis, size, bit)
        bit *= 2
    return value


def after(value, other):
    return value + other[(slice(0, 1),) * other.ndim].reshape((1,) * value.ndim).astype(value.dtype) * 0


def per_device(sizes, block_input, cotangent, lengths, first_gain, first_shift, second_gain, second_shift, triple_weight, triple_bias,
               output_weight, output_bias, upward_weight, upward_bias, downward_weight, downward_bias):
    rep, n = sizes
    rows, d = block_input.shape
    dn, fn = first_gain.shape[0], upward_bias.shape[0]
    gw = d // GROUPS
    chunks = fn * n // d
    nz = n // 2
    plan = dict(on=rep == 4 and n == 8 and dn % 16 == 0 and chunks == nz == rep, dn=dn, nz=nz, nr=rep)
    ri, fi = lax.axis_index("rep"), lax.axis_index("fsdp")
    z, core = fi // 2, fi % 2
    me = ri * n + fi
    scalars = jnp.stack([lengths[0], z, core, ri, me]).astype(jnp.int32)
    group_cols = lambda v, j: jnp.concatenate([v[:, a * d + j * gw:a * d + (j + 1) * gw] for a in range(3)], axis=1)
    mats = jnp.stack([group_cols(triple_weight, j) for j in range(GROUPS)] + [output_weight])
    small = [first_gain, first_shift, second_gain, second_shift, output_bias, downward_bias, triple_bias, upward_bias]
    wide_row = max(v.shape[0] for v in small)
    low = jnp.asarray(-jnp.inf, BF)
    small = [lax.pad(v.reshape(1, -1), low, ((i, 7 - i, 0), (0, wide_row - v.shape[0], 0))) for i, v in enumerate(small)]
    while len(small) > 1:
        small = [jnp.maximum(a, b) for a, b in zip(small[::2], small[1::2])]
    small = jnp.maximum(small[0], jnp.asarray(-1e4, BF))
    small = jnp.where(jnp.arange(n)[:, None, None] == fi, small[None], 0.0).astype(BF)

    along_z = lambda v: [xor_permute(v, "fsdp", n, 2 * k) for k in range(1, nz)]
    along_rep = lambda v: [xor_permute(v, "rep", rep, j) for j in range(1, rep)]
    to_core = lambda v: xor_permute(v, "fsdp", n, 1)

    def unpack(small):
        small = small.astype(F32)
        par = small[:, :6, :dn].swapaxes(0, 1).reshape(6, d)
        bias_t = small[:, 6, :3 * dn].reshape(1, 3 * d)
        vecs = jnp.concatenate([par] + [group_cols(bias_t, j) for j in range(GROUPS)] + [small[:, 7, :fn].reshape(chunks, d)])
        return jnp.pad(vecs, ((0, -vecs.shape[0] % 8), (0, 0)))

    if plan["on"]:
        quarter = lax.dynamic_index_in_dim(mats, ri, 0, keepdims=False)
        small = small + to_core(small)
        far = along_z(quarter)
        small = jnp.stack([small] + along_z(small))
        sib_own = to_core(mats)
        wide_own = [upward_weight, downward_weight, to_core(upward_weight), to_core(downward_weight)]
        n1, n1t, n2, n2t, gl, par, ready, pick = prepare(plan, scalars, block_input, cotangent, small, upward_weight, downward_weight, [sib_own] + wide_own[2:])
        far = jnp.stack(far) + ready
        near = [far] + along_rep(far)
    else:
        small = butterfly(small, "fsdp", n)
        weights = [lax.all_gather(mats, "fsdp", axis=1, tiled=True)]
        n1, n1t, n2, n2t, gl, par, ready, _ = prepare(plan, scalars, block_input, cotangent, unpack(small), upward_weight, downward_weight, [])
    tables = [jnp.asarray(t) for t in rotary_tables(rows, 128)]

    if plan["on"]:
        wide_far = jnp.stack(along_z(pick))
        weights = [mats, sib_own] + near + [to_core(jnp.stack(near))]
    d3a, ctxa, sma, token_a, w = attention(plan, (0,), scalars, n1, gl, par, tables, weights)
    if plan["on"]:
        wide_far = wide_far + token_a
        wide_near = [wide_far] + along_rep(wide_far)
    d3b, ctxb, smb, token_b = attention(plan, (1, 2), scalars, n1, gl, par, tables, [w])
    if plan["on"]:
        wide_sibs = to_core(jnp.stack(wide_near) + token_b)
        wide_weights = wide_own + wide_near + [wide_sibs]
    else:
        up = lax.all_gather(upward_weight, "fsdp", axis=0, tiled=True)
        down = lax.all_gather(downward_weight, "fsdp", axis=0, tiled=True)
        wide_weights = [jnp.stack([up[:, j * d:(j + 1) * d] for j in range(chunks)]), down.reshape(chunks, d, d)]
    *dwa, sm1, ff = closing(plan, scalars, block_input, gl, n1t, par, w, d3a, d3b, ctxa, ctxb, sma, smb)
    width = -(-rep * n // 128) * 128
    *dwf, smalls, norm_row, act, wd, gx = ffn(plan, chunks, scalars, block_input, gl, n2, n2t, par, ff, sm1, wide_weights, width)

    if plan["on"]:
        a, b, c = along_z(norm_row)
        norm_row = (norm_row + a) + (b + c)
        a, b, c = along_rep(norm_row)
        norm_row = (norm_row + a) + (b + c)
        norm_rows = (norm_row, to_core(norm_row))
        halves = []
        for keep, send in ((dwa[0], dwa[1]), (dwf[0], dwf[1]), (dwf[2], dwf[3])):
            halves += [keep, to_core(send)]
        pair = (smalls, to_core(smalls))
        steps = dict(x=("rep", rep, 1), y=("rep", rep, 2), lo=("fsdp", n, 2), hi=("fsdp", n, 4))
        move = lambda v, name: xor_permute(v, *steps[name])
        *sends, norm_row = mix(rep * n, True, scalars, norm_rows, halves, pair, ready)
        norms = norm_row[0, :rep * n]
        *mines, token = mix(rep * n, False, scalars, norm_rows, halves, pair, norm_row)
        out = output(scalars, block_input, par, token, w, wd, act, (ctxa, ctxb))
        parts = []
        for send, mine, order in zip(sends, mines, (("x", "y", "lo"), ("y", "lo", "x"), ("lo", "x", "y"))):
            got = move(send, order[0])
            for at, name in enumerate(order[1:]):
                waits = () if at else (out,)
                if mine.ndim == 2:
                    send, mine = fold_flat(scalars, name, 8 >> at, mine, got, waits)
                else:
                    send, mine = fold(scalars, name, mine, got, waits)
                got = move(send, name)
            parts.append((mine, got))
        first = 3 * dn // 2
        send_1, send_2, mine_1, mine_2 = last_fold(scalars, parts, first)
        add = lambda mine, send: (mine.astype(F32) + move(send, "hi").astype(F32)).astype(BF)
        mine_1 = add(mine_1, send_1)
        around_1 = [mine_1] + along_rep(mine_1)
        mine_2 = add(mine_2, send_2)
        smalls = mine_2[first:].astype(F32)
        mine_2 = mine_2[:first]
        around_2 = [mine_2] + along_rep(mine_2)
        around = [jnp.concatenate([p, q]) for p, q in zip(around_1, around_2)]
        x, y = ri % 2, ri // 2
        flip = lambda bit, a, b: (jnp.where(bit == 1, b, a), jnp.where(bit == 1, a, b))
        a0, a1 = flip(x, around[0], around[1])
        a2, a3 = flip(x, around[2], around[3])
        a0, a2 = flip(y, a0, a2)
        a1, a3 = flip(y, a1, a3)
        final = jnp.stack([a0, a1, a2, a3]).astype(F32)
        g_att, g_up, g_down = final[:, :dn], final[:, dn:2 * dn], final[:, 2 * dn:].reshape(fn, d)
        smalls = smalls.reshape(SMALL, d)
    else:
        norms = butterfly(butterfly(norm_row, "fsdp", n), "rep", rep)[0, :rep * n]
        factor = jnp.minimum(1.0, jnp.mean(norms) / lax.dynamic_index_in_dim(norms, me, 0, keepdims=False)) / (rep * n)
        out = output(scalars, block_input, par, ready, w, wd, act, (ctxa, ctxb))
        scale = lambda v: (v.astype(F32) * factor).astype(BF)
        shards = lambda v: v.reshape(v.shape[0], n, dn, d).swapaxes(0, 1).reshape(n, -1, d)
        pack = jnp.concatenate([scale(shards(dwa[0])), scale(shards(dwf[0])), scale(dwf[1].reshape(n, fn, d))], axis=1)
        mine = lax.psum_scatter(pack, "fsdp", scatter_dimension=0, tiled=True)[0]
        mine = lax.psum(mine, "rep").astype(F32)
        g_att = mine[:4 * dn].reshape(4, dn, d)
        g_up = mine[4 * dn:(4 + chunks) * dn].reshape(chunks, dn, d)
        g_down = mine[(4 + chunks) * dn:]
        smalls = lax.psum(scale(smalls), ("rep", "fsdp")).astype(F32)

    g_triple = jnp.concatenate([g_att[j, :, a * gw:(a + 1) * gw] for a in range(3) for j in range(GROUPS)], axis=1)
    g_upward = jnp.concatenate([g_up[j] for j in range(chunks)], axis=1)
    own = lambda v, width: lax.dynamic_slice_in_dim(v, fi * width, width, 0)
    g1, s1, g2, s2, bd = (own(smalls[i], dn) for i in range(5))
    b_triple = own(jnp.concatenate([smalls[5 + j, a * gw:(a + 1) * gw] for a in range(3) for j in range(GROUPS)]), 3 * dn)
    b_up = own(smalls[8:8 + chunks].reshape(-1), fn)
    return (out, gx, g1, s1, g2, s2, g_triple, b_triple, g_att[GROUPS], bd, g_upward, b_up, g_down, bd, norms)


def solution(mesh):
    rows = P(("rep", "fsdp"), None)
    vec, mat = P("fsdp"), P("fsdp", None)
    sizes = (mesh.shape["rep"], mesh.shape["fsdp"])
    return jax.shard_map(
        lambda *args: per_device(sizes, *args),
        mesh=mesh,
        in_specs=(rows, rows, P(("rep", "fsdp")), vec, vec, vec, vec, mat, vec, mat, vec, mat, vec, mat, vec),
        out_specs=(rows, rows, vec, vec, vec, vec, mat, vec, mat, vec, mat, vec, mat, vec, P()),
        check_vma=False,
    )
```

```python
import math
import numpy as np
import jax
import jax.numpy as jnp
from jax import lax
from jax.experimental import pallas as pl
from jax.experimental.pallas import tpu as pltpu
from jax.sharding import PartitionSpec as P

HEADS = 12
HEAD_DIM = 64
ROT = 16
EPS = 1e-05
MASKED = -1e30
BF = jnp.bfloat16
F32 = jnp.float32
GROUPS = 3
MIB = 1024 * 1024


def mm(a, b):
    return jnp.dot(a, b, preferred_element_type=F32)


def mm_rt(a, b):
    return lax.dot_general(a, b, (((1,), (1,)), ((), ())), preferred_element_type=F32)


def mm_lt(a, b):
    return lax.dot_general(a, b, (((0,), (0,)), ((), ())), preferred_element_type=F32)


def rotary_tables(rows, width):
    half = ROT // 2
    freq = np.exp(np.arange(half, dtype=np.float32) * np.float32(-2.0 * math.log(10000.0) / ROT))
    ang = np.arange(rows, dtype=np.float32)[:, None] * freq.astype(np.float32)[None, :]
    cos, sin = np.cos(ang), np.sin(ang)
    keep = np.ones((rows, HEAD_DIM), np.float32)
    up = np.zeros((rows, HEAD_DIM), np.float32)
    down = np.zeros((rows, HEAD_DIM), np.float32)
    keep[:, :half] = cos
    keep[:, half:ROT] = cos
    up[:, :half] = -sin
    down[:, half:ROT] = sin
    rep = width // HEAD_DIM
    return tuple(np.tile(t, (1, rep)).astype(np.float32) for t in (keep, up, down))


def norm_parts(values):
    centred = values - jnp.mean(values, axis=-1, keepdims=True)
    inverse = lax.rsqrt(jnp.mean(centred * centred, axis=-1, keepdims=True) + EPS)
    return centred * inverse, inverse


def norm_back(e, gain, normed, inverse):
    t = e * gain
    t_mean = jnp.mean(t, axis=-1, keepdims=True)
    cross = jnp.mean(t * normed, axis=-1, keepdims=True)
    return inverse * (t - t_mean - normed * cross)


SMALL = 16
BLOCK = 256
QKV_BIAS = 6
UP_BIAS = QKV_BIAS + GROUPS
VM = pl.BlockSpec(memory_space=pltpu.VMEM)
SM = pl.BlockSpec(memory_space=pltpu.SMEM)
ANY = pl.BlockSpec(memory_space=pl.ANY)


def block(i):
    return pl.ds(pl.multiple_of(i * BLOCK, BLOCK), BLOCK)


def params(mib):
    return pltpu.CompilerParams(vmem_limit_bytes=mib * MIB)


def valid_rows(i, seq):
    return (lax.broadcasted_iota(jnp.int32, (BLOCK, 1), 0) + i * BLOCK < seq).astype(F32)


def unpack_small(small, dn, d, vec_out):
    n = small.shape[0]
    gw = d // GROUPS
    line = lambda row, width: jnp.concatenate([small[s, row:row + 1, :width] for s in range(n)], axis=1)
    vec_out[...] = jnp.zeros_like(vec_out)
    for i in range(6):
        vec_out[i:i + 1, :] = line(i, dn)
    qkv = line(6, 3 * dn)
    for j in range(GROUPS):
        vec_out[QKV_BIAS + j:QKV_BIAS + j + 1, :] = jnp.concatenate([qkv[:, a * d + j * gw:a * d + (j + 1) * gw] for a in range(3)], axis=1)
    up = line(7, small.shape[2])
    for j in range(up.shape[1] // d):
        vec_out[UP_BIAS + j:UP_BIAS + j + 1, :] = up[:, j * d:(j + 1) * d]


def prepare_kernel(plan, waits, sc_ref, x_ref, g_ref, packed, up_ref, down_ref, *rest):
    n1, n1t, n2, n2t, gl, vec_out, token, pick, sems = rest[waits:]
    d = x_ref.shape[1]
    par_ref = vec_out
    if plan["on"]:
        dn, rep = plan["dn"], sc_ref[3]
        cut = [pltpu.make_async_copy(up_ref.at[:, pl.ds(pl.multiple_of(rep * d, 128), d)], pick.at[0], sems.at[0]),
               pltpu.make_async_copy(down_ref.at[pl.ds(pl.multiple_of(rep * dn, 16), dn)], pick.at[1], sems.at[1])]

        @pl.when(pl.program_id(0) == 0)
        def _():
            for c in cut:
                c.start()
            unpack_small(packed[0].astype(F32) + packed[1].astype(F32) + packed[2].astype(F32) + packed[3].astype(F32), dn, d, vec_out)

        @pl.when(pl.program_id(0) == pl.num_programs(0) - 1)
        def _():
            for c in cut:
                c.wait()

    else:
        vec_out[...] = packed[...]
    token[...] = jnp.zeros_like(token)
    normed, _ = norm_parts(x_ref[...].astype(F32))
    one = (normed * par_ref[0:1, :] + par_ref[1:2, :]).astype(BF)
    two = (normed * par_ref[2:3, :] + par_ref[3:4, :]).astype(BF)
    n1[...] = one
    n2[...] = two
    n1t[...] = one.astype(F32).T.astype(BF)
    n2t[...] = two.astype(F32).T.astype(BF)
    gl[...] = (g_ref[...].astype(F32) * valid_rows(pl.program_id(0), sc_ref[0])).astype(BF)


def prepare(plan, scalars, x, g, par, up, down, waits):
    rows, d = x.shape
    flat, turned = jax.ShapeDtypeStruct((rows, d), BF), jax.ShapeDtypeStruct((d, rows), BF)
    vecs = (16, d) if plan["on"] else par.shape
    by_rows, by_cols = pl.BlockSpec((BLOCK, d), lambda i: (i, 0)), pl.BlockSpec((d, BLOCK), lambda i: (0, i))
    return pl.pallas_call(
        lambda *refs: prepare_kernel(plan, len(waits), *refs),
        grid_spec=pl.GridSpec(grid=(rows // BLOCK,), in_specs=[SM, by_rows, by_rows, pl.BlockSpec(par.shape, lambda i: (0,) * par.ndim), ANY, ANY] + [ANY] * len(waits),
                              out_specs=[by_rows, by_cols, by_rows, by_cols, by_rows, pl.BlockSpec(vecs, lambda i: (0, 0)), pl.BlockSpec((1, 1), lambda i: (0, 0)), pl.BlockSpec((2, plan["dn"], d), lambda i: (0, 0, 0))],
                              scratch_shapes=[pltpu.SemaphoreType.DMA((2,))]),
        out_shape=[flat, turned, flat, turned, flat, jax.ShapeDtypeStruct(vecs, F32), jax.ShapeDtypeStruct((1, 1), F32),
                   jax.ShapeDtypeStruct((2, plan["dn"], d), BF)], compiler_params=params(60), name="prepare",
        cost_estimate=pl.CostEstimate(flops=40 * rows * d, bytes_accessed=14 * rows * d, transcendentals=rows),
    )(scalars, x, g, par, up, down, *waits)


def attn_kernel(plan, first, base, sc_ref, n1, gl, b3_ref, keep_ref, up_ref, down_ref, *rest):
    nw = plan["pieces"] if first else 2
    w_refs, rest = rest[:nw], rest[nw:]
    d3, ctx_low, sm_ref, token, rest = rest[0].at[0], rest[1].at[0], rest[2].at[0], rest[3], rest[4:]
    token[...] = jnp.zeros_like(token)
    rows, d = n1.shape
    gw = d // GROUPS
    qb = BLOCK
    nb = rows // qb
    seq = sc_ref[0]
    if first:
        w_out, rest = rest[0], rest[1:]
    q_s, k_s, v_s, dc_s, ctx, dq, dk, dv, qm, km, vm, dcm, pall, dall = rest[:14]

    if first:
        w, sems = rest[14:]
        if plan["on"]:
            z, core, rep = sc_ref[1], sc_ref[2], sc_ref[3]
            dn, nz, nr = plan["dn"], plan["nz"], plan["nr"]
            own, sib, near, sibs = w_refs[0], w_refs[1], w_refs[2:2 + nr], w_refs[2 + nr]
            place = lambda zz, cc: pl.ds(pl.multiple_of((zz * 2 + cc) * dn, 16), dn)
            pairs = []
            for m in range(nr):
                pairs.append((own.at[m], w.at[m, place(z, core)]))
                pairs.append((sib.at[m], w.at[m, place(z, 1 - core)]))
            for j in range(nr):
                for k in range(1, nz):
                    m, zz = rep ^ j, z ^ k
                    pairs.append((near[j].at[k - 1], w.at[m, place(zz, core)]))
                    pairs.append((sibs.at[j, k - 1], w.at[m, place(zz, 1 - core)]))
        else:
            pairs = [(w_refs[0].at[m], w.at[m]) for m in range(GROUPS + 1)]
        copies = [pltpu.make_async_copy(a, b, sems.at[i]) for i, (a, b) in enumerate(pairs)]
        for c in copies:
            c.start()
        for c in copies:
            c.wait()
        back = pltpu.make_async_copy(w, w_out, sems.at[len(pairs)])
        back.start()
        w3, wo = w.at[0], w.at[GROUPS, 0:gw]
    else:
        w3, wo = w_refs[0].at[0], w_refs[1].at[0]
    half = ROT // 2

    def tables(r):
        return tuple(jnp.concatenate([t[r, :]] * (gw // 128), axis=1) for t in (keep_ref, up_ref, down_ref))

    def project(i, c):
        r = block(i)
        t = mm(n1[r, :], w3[...]) + b3_ref[pl.ds(QKV_BIAS + base + pl.program_id(0), 1), :]
        keep, up, down = tables(r)
        for at, ref, scale in ((0, q_s, HEAD_DIM ** -0.5), (1, k_s, None)):
            v = t[:, at * gw:(at + 1) * gw]
            low = (v * keep + pltpu.roll(v, gw - half, 1) * up + pltpu.roll(v, half, 1) * down).astype(BF)
            ref[r, :] = low if scale is None else (low.astype(F32) * scale).astype(BF)
        v_s[r, :] = t[:, 2 * gw:].astype(BF)
        dc_s[r, :] = mm_rt(gl[r, :], wo[...]).astype(BF)
        return c
    lax.fori_loop(0, nb, project, 0, unroll=True)

    key_bias = jnp.where(lax.broadcasted_iota(jnp.int32, (1, rows), 1) < seq, 0.0, MASKED).astype(F32)
    causal = lax.broadcasted_iota(jnp.int32, (qb, qb), 1) <= lax.broadcasted_iota(jnp.int32, (qb, qb), 0)

    heads = gw // HEAD_DIM

    def head(h, c):
        lane = lax.broadcasted_iota(jnp.int32, (1, gw), 1) // HEAD_DIM
        mask = jnp.where(lane == h, 1.0, 0.0).astype(BF)
        for ref, out in ((q_s, qm), (k_s, km), (v_s, vm), (dc_s, dcm)):
            out[h] = ref[...] * mask
        for i in range(nb):
            lo, kl = i * qb, (i + 1) * qb
            s = mm_rt(qm[h, lo:kl, :], k_s[:kl, :]) + key_bias[:, :kl]
            diag = jnp.where(causal, s[:, lo:], MASKED)
            s = diag if i == 0 else jnp.concatenate([s[:, :lo], diag], axis=1)
            dp = mm_rt(dcm[h, lo:kl, :], v_s[:kl, :])
            e = jnp.exp(s - jnp.max(s, axis=1, keepdims=True))
            p = e * (1.0 / jnp.sum(e, axis=1, keepdims=True))
            pall[h, lo:kl, :kl] = p.astype(BF)
            inner = jnp.sum(p * dp, axis=1, keepdims=True)
            dall[h, lo:kl, :kl] = (p * (dp - inner)).astype(BF)
        return c
    lax.fori_loop(0, heads, head, 0, unroll=2)
    for i in range(nb):
        lo, kl = i * qb, (i + 1) * qb
        ctx[lo:kl, :] = sum(mm(pall[h, lo:kl, :kl], vm[h, :kl, :]) for h in range(heads))
        dq[lo:kl, :] = sum(mm(dall[h, lo:kl, :kl], km[h, :kl, :]) for h in range(heads))
        dv[lo:kl, :] = sum(mm_lt(pall[h, lo:, lo:kl], dcm[h, lo:, :]) for h in range(heads))
        dk[lo:kl, :] = sum(mm_lt(dall[h, lo:, lo:kl], qm[h, lo:, :]) for h in range(heads))

    def finish(i, total):
        r = block(i)
        keep, up, down = tables(r)
        parts = []
        for ref, scale in ((dq, HEAD_DIM ** -0.5), (dk, 1.0)):
            v = ref[r, :] * scale
            parts.append(v * keep - pltpu.roll(v, gw - half, 1) * up - pltpu.roll(v, half, 1) * down)
        low = jnp.concatenate(parts + [dv[r, :]], axis=1).astype(BF)
        d3[r, :] = low
        ctx_low[r, :] = ctx[r, :].astype(BF)
        return total + jnp.sum(low.astype(F32), axis=0, keepdims=True)
    db3 = lax.fori_loop(0, nb, finish, jnp.zeros((1, d), F32), unroll=True)
    sm_ref[...] = jnp.broadcast_to(db3, sm_ref.shape)
    if first:
        back.wait()


def attention(plan, groups, scalars, n1, gl, b3, tables, weights):
    rows, d = n1.shape
    gw = d // GROUPS
    first, count, base = groups[0] == 0, len(groups), groups[0]
    plan = dict(plan, pieces=len(weights))
    whole = lambda *shape: pl.BlockSpec(shape, lambda j: (0,) * len(shape))
    stacked = lambda *shape: pl.BlockSpec((1,) + shape, lambda j: (j,) + (0,) * len(shape))
    out_shape = [jax.ShapeDtypeStruct((count, rows, d), BF), jax.ShapeDtypeStruct((count, rows, gw), BF), jax.ShapeDtypeStruct((count, 8, d), F32), jax.ShapeDtypeStruct((1, 1), F32)]
    out_specs = [stacked(rows, d), stacked(rows, gw), stacked(8, d), whole(1, 1)]
    heads = gw // HEAD_DIM
    scratch = [pltpu.VMEM((rows, gw), BF)] * 4 + [pltpu.VMEM((rows, gw), F32)] * 4
    scratch += [pltpu.VMEM((heads, rows, gw), BF)] * 4 + [pltpu.VMEM((heads, rows, rows), BF)] * 2
    if first:
        out_shape.append(jax.ShapeDtypeStruct((GROUPS + 1, d, d), BF))
        out_specs.append(ANY)
        scratch += [pltpu.VMEM((GROUPS + 1, d, d), BF), pltpu.SemaphoreType.DMA((64,))]
        w_specs = [ANY] * len(weights)
    else:
        weights = [weights[0], weights[0]]
        w_specs = [pl.BlockSpec((1, d, d), lambda j: (base + j, 0, 0)), pl.BlockSpec((1, gw, d), lambda j: (GROUPS, base + j, 0))]
    flops = count * (2 * rows * d * (d + gw) + 12 * HEADS // GROUPS * rows * rows * HEAD_DIM)
    return pl.pallas_call(
        lambda *refs: attn_kernel(plan, first, base, *refs),
        grid_spec=pl.GridSpec(
            grid=(count,),
            in_specs=[SM, whole(rows, d), whole(rows, d), whole(*b3.shape)] + [whole(rows, 128)] * 3 + w_specs,
            out_specs=out_specs, scratch_shapes=scratch),
        out_shape=out_shape, compiler_params=params(56 if first else 60), name="attend_first" if first else "attend_rest",
        cost_estimate=pl.CostEstimate(flops=4 * flops, bytes_accessed=8_000_000, transcendentals=count * HEADS * rows * rows // GROUPS),
    )(scalars, n1, gl, b3, *tables, *weights)


def write_halves(value, tmp, keep_ref, send_ref, core, dn):
    tmp[...] = value.astype(BF)
    for z in range(keep_ref.shape[0]):
        mine = pl.ds(pl.multiple_of((2 * z + core) * dn, 16), dn)
        other = pl.ds(pl.multiple_of((2 * z + 1 - core) * dn, 16), dn)
        keep_ref[z, 0] = tmp[mine, :]
        send_ref[z, 0] = tmp[other, :]


def closing_kernel(plan, sc_ref, x_ref, gl, n1t, par_ref, w, d3a, d3b, ctxa, ctxb, sma, smb, *rest):
    nd = 2 if plan["on"] else 1
    dw_refs, rest = rest[:nd], rest[nd:]
    sm_ref, ff_ref, gf, tmp, x_s, gl_s, ctx_s, sems = rest
    step = pl.program_id(0)
    rows, d = x_ref.shape
    nb = rows // BLOCK
    late = [pltpu.make_async_copy(x_ref, x_s, sems.at[0]), pltpu.make_async_copy(gl, gl_s, sems.at[1]),
            pltpu.make_async_copy(ctxa, ctx_s.at[pl.ds(0, 1)], sems.at[2]), pltpu.make_async_copy(ctxb, ctx_s.at[pl.ds(1, GROUPS - 1)], sems.at[3])]

    @pl.when(step == 0)
    def _():
        for c in late:
            c.start()

    def store(dw):
        if plan["on"]:
            write_halves(dw, tmp, dw_refs[0], dw_refs[1], sc_ref[2], plan["dn"])
        else:
            dw_refs[0][0] = dw.astype(BF)
        return jnp.sum(dw * dw, axis=0, keepdims=True)

    def group(first, d3, db3):
        def body(i, c):
            r = block(i)
            part = mm_rt(d3[0, r, :], w[0])
            gf[r, :] = part if first else gf[r, :] + part
            return c
        lax.fori_loop(0, nb, body, 0, unroll=True)
        total = store(mm(n1t[...], d3[0])) + db3 * db3
        sm_ref[pl.ds(2 + step, 1), :] = db3
        sm_ref[5:6, :] = total if first else sm_ref[5:6, :] + total

    @pl.when(step == 0)
    def _():
        group(True, d3a, sma[0, 0:1, :])

    @pl.when(jnp.logical_and(step > 0, step < GROUPS))
    def _():
        group(False, d3b, smb[0, 0:1, :])

    @pl.when(step == GROUPS)
    def _():
        for c in late:
            c.wait()
        total = store(mm_lt(jnp.concatenate([ctx_s[g] for g in range(GROUPS)], axis=1), gl_s[...]))

        def back(i, c):
            r = block(i)
            normed, inverse = norm_parts(x_s[r, :].astype(F32))
            e = gf[r, :]
            ff_ref[r, :] = norm_back(e, par_ref[0:1, :], normed, inverse)
            return (c[0] + jnp.sum(e * normed, axis=0, keepdims=True), c[1] + jnp.sum(e, axis=0, keepdims=True))
        zero = jnp.zeros((1, d), F32)
        dgain, dshift = lax.fori_loop(0, nb, back, (zero, zero), unroll=True)
        sm_ref[0:1, :] = dgain
        sm_ref[1:2, :] = dshift
        sm_ref[5:6, :] += total + dgain * dgain + dshift * dshift


def closing(plan, scalars, x, gl, n1t, par, w, d3a, d3b, ctxa, ctxb, sma, smb):
    rows, d = x.shape
    gw = d // GROUPS
    whole = lambda *shape: pl.BlockSpec(shape, lambda j: (0,) * len(shape))
    later = lambda *shape: pl.BlockSpec((1,) + shape, lambda j: (jnp.clip(j - 1, 0, GROUPS - 2),) + (0,) * len(shape))
    if plan["on"]:
        nz, dn = plan["nz"], plan["dn"]
        dw_specs = [pl.BlockSpec((nz, 1, dn, d), lambda j: (0, j, 0, 0))] * 2
        dw_shapes = [jax.ShapeDtypeStruct((nz, GROUPS + 1, dn, d), BF)] * 2
    else:
        dw_specs = [pl.BlockSpec((1, d, d), lambda j: (j, 0, 0))]
        dw_shapes = [jax.ShapeDtypeStruct((GROUPS + 1, d, d), BF)]
    return pl.pallas_call(
        lambda *refs: closing_kernel(plan, *refs),
        grid_spec=pl.GridSpec(
            grid=(GROUPS + 1,),
            in_specs=[SM, ANY, ANY, whole(d, rows), whole(*par.shape),
                      pl.BlockSpec((1, d, d), lambda j: (jnp.minimum(j, GROUPS - 1), 0, 0)),
                      whole(1, rows, d), later(rows, d), ANY, ANY, whole(1, 8, d), later(8, d)],
            out_specs=dw_specs + [whole(8, d), whole(rows, d)],
            scratch_shapes=[pltpu.VMEM((rows, d), F32), pltpu.VMEM((d, d), BF), pltpu.VMEM((rows, d), BF), pltpu.VMEM((rows, d), BF),
                            pltpu.VMEM((GROUPS, rows, gw), BF), pltpu.SemaphoreType.DMA((4,))],
        ),
        out_shape=dw_shapes + [jax.ShapeDtypeStruct((8, d), F32), jax.ShapeDtypeStruct((rows, d), F32)],
        compiler_params=params(60), name="closing",
        cost_estimate=pl.CostEstimate(flops=4 * rows * d * 7 * d, bytes_accessed=8_000_000, transcendentals=rows),
    )(scalars, x, gl, n1t, par, w, d3a, d3b, ctxa, ctxb, sma, smb)


ERF_P = 0.3275911
ERF_A = (0.254829592, -0.284496736, 1.421413741, -1.453152027, 1.061405429)


def gelu_parts(u):
    z = jnp.abs(u) * (2.0 ** -0.5)
    t = 1.0 / (1.0 + ERF_P * z)
    bell = jnp.exp(-0.5 * (u * u))
    a1, a2, a3, a4, a5 = (0.5 * a for a in ERF_A)
    tail = ((((a5 * t + a4) * t + a3) * t + a2) * t + a1) * t * bell
    cdf = jnp.where(u >= 0.0, 1.0 - tail, tail)
    return u * cdf, cdf + u * bell * (1.0 / math.sqrt(2.0 * math.pi))


def ffn_kernel(plan, sc_ref, x_ref, gl, n2, n2t, par_ref, ff_ref, sm1_ref, *rest):
    nw = plan["pieces"]
    w_refs, rest = rest[:nw], rest[nw:]
    nd = 4 if plan["on"] else 2
    dw_refs, rest = rest[:nd], rest[nd:]
    sm_ref, norm_ref, act_ref, wd_ref, gx_ref = rest[:5]
    wu_s, wd_s, gs, gup, sq, tmp, x_s, ff_s, up_sems, down_sems, late_sems = rest[5:]
    late = [pltpu.make_async_copy(x_ref, x_s, late_sems.at[0]), pltpu.make_async_copy(ff_ref, ff_s, late_sems.at[1])]
    step = pl.program_id(0)
    last = pl.num_programs(0) - 1
    rows, d = x_ref.shape
    fc = d
    nb = rows // BLOCK

    @pl.when(step == 0)
    def _():
        if plan["on"]:
            z, core, rep = sc_ref[1], sc_ref[2], sc_ref[3]
            dn, nz, nr = plan["dn"], plan["nz"], plan["nr"]
            own_up, own_down, sib_up, sib_down = w_refs[:4]
            near, sibs = w_refs[4:4 + nr], w_refs[4 + nr]

            def up(src, m, zz, cc):
                dst = wu_s.at[m, pl.ds(pl.multiple_of((zz * 2 + cc) * dn, 16), dn)]
                pltpu.make_async_copy(src, dst, up_sems.at[m]).start()

            def down(src, b, zz, cc):
                dst = wd_s.at[zz, pl.ds(pl.multiple_of((cc * nr + b) * dn, 16), dn)]
                pltpu.make_async_copy(src, dst, down_sems.at[zz]).start()
            for m in range(nr):
                cols, part = pl.ds(m * d, d), pl.ds(m * dn, dn)
                up(own_up.at[:, cols], m, z, core)
                up(sib_up.at[:, cols], m, z, 1 - core)
                down(own_down.at[part], m, z, core)
                down(sib_down.at[part], m, z, 1 - core)
            for j in range(nr):
                for k in range(1, nz):
                    up(near[j].at[k - 1, 0], rep ^ j, z ^ k, core)
                    up(sibs.at[j, k - 1, 0], rep ^ j, z ^ k, 1 - core)
                    down(near[j].at[k - 1, 1], rep ^ j, z ^ k, core)
                    down(sibs.at[j, k - 1, 1], rep ^ j, z ^ k, 1 - core)
        else:
            for m in range(wu_s.shape[0]):
                pltpu.make_async_copy(w_refs[0].at[m], wu_s.at[m], up_sems.at[m]).start()
                pltpu.make_async_copy(w_refs[1].at[m], wd_s.at[m], down_sems.at[m]).start()
        for c in late:
            c.start()
        gs[...] = jnp.zeros_like(gs)
        sq[...] = jnp.zeros_like(sq)
        sm_ref[...] = jnp.zeros_like(sm_ref)

    pltpu.make_async_copy(wu_s.at[step], wu_s.at[step], up_sems.at[step]).wait()
    pltpu.make_async_copy(wd_s.at[step], wd_s.at[step], down_sems.at[step]).wait()
    wu, wd = wu_s.at[step], wd_s.at[step]
    wd_ref[0] = wd[...]

    def rows_step(i, dbu):
        r = block(i)
        u = mm(n2[r, :], wu[...]) + par_ref[pl.ds(UP_BIAS + step, 1), :]
        da = mm_rt(gl[r, :], wd[...])
        a, slope = gelu_parts(u)
        act_ref[0, r, :] = a.astype(BF)
        gu = (da * slope).astype(BF)
        gup[r, :] = gu
        gs[r, :] += mm_rt(gu, wu[...])
        return dbu + jnp.sum(gu.astype(F32), axis=0, keepdims=True)
    dbu = lax.fori_loop(0, nb, rows_step, jnp.zeros((1, fc), F32), unroll=True)
    sm_ref[pl.ds(8 + step, 1), :] = dbu

    dwu = mm(n2t[...], gup[...])
    total = jnp.sum(dwu * dwu, axis=0, keepdims=True) + dbu * dbu
    if plan["on"]:
        write_halves(dwu, tmp, dw_refs[0], dw_refs[1], sc_ref[2], plan["dn"])
    else:
        dw_refs[0][0] = dwu.astype(BF)
    dwd = mm_lt(act_ref[0], gl[...])
    total += jnp.sum(dwd * dwd, axis=0, keepdims=True)
    if plan["on"]:
        tmp[...] = dwd.astype(BF)
        core, dn, nr = sc_ref[2], plan["dn"], plan["nr"]
        for m in range(nr):
            dw_refs[2][0, m] = tmp[pl.ds(pl.multiple_of((core * nr + m) * dn, 16), dn), :]
            dw_refs[3][0, m] = tmp[pl.ds(pl.multiple_of(((1 - core) * nr + m) * dn, 16), dn), :]
    else:
        dw_refs[1][0] = dwd.astype(BF)
    sq[...] += total

    @pl.when(step == last)
    def _():
        for c in late:
            c.wait()

        def back(i, c):
            r = block(i)
            normed, inverse = norm_parts(x_s[r, :].astype(F32))
            e = gs[r, :]
            grad_rows = gl[r, :].astype(F32)
            gx_ref[r, :] = (grad_rows + ff_s[r, :] + norm_back(e, par_ref[2:3, :], normed, inverse)).astype(BF)
            return (c[0] + jnp.sum(e * normed, axis=0, keepdims=True), c[1] + jnp.sum(e, axis=0, keepdims=True),
                    c[2] + jnp.sum(grad_rows, axis=0, keepdims=True))
        zero = jnp.zeros((1, d), F32)
        dgain, dshift, dbd = lax.fori_loop(0, nb, back, (zero, zero, zero), unroll=True)
        sm_ref[0:2, :] = sm1_ref[0:2, :]
        sm_ref[2:3, :] = dgain
        sm_ref[3:4, :] = dshift
        sm_ref[4:5, :] = dbd
        sm_ref[5:8, :] = sm1_ref[2:5, :]
        final = sq[...] + sm1_ref[5:6, :] + dgain * dgain + dshift * dshift + 2.0 * dbd * dbd
        own = jnp.sqrt(jnp.sum(final, axis=1, keepdims=True))
        here = lax.broadcasted_iota(jnp.int32, norm_ref.shape, 1) == sc_ref[4]
        norm_ref[...] = jnp.where(here, own, 0.0)


def ffn(plan, chunks, scalars, x, gl, n2, n2t, par, ff, sm1, weights, norm_width):
    rows, d = x.shape
    plan = dict(plan, pieces=len(weights))
    whole = lambda *shape: pl.BlockSpec(shape, lambda j: (0,) * len(shape))
    if plan["on"]:
        nz, dn, nr = plan["nz"], plan["dn"], plan["nr"]
        dw_specs = [pl.BlockSpec((nz, 1, dn, d), lambda j: (0, j, 0, 0))] * 2 + [pl.BlockSpec((1, nr, dn, d), lambda j: (j, 0, 0, 0))] * 2
        dw_shapes = [jax.ShapeDtypeStruct((nz, chunks, dn, d), BF)] * 2 + [jax.ShapeDtypeStruct((nz, nr, dn, d), BF)] * 2
    else:
        dw_specs = [pl.BlockSpec((1, d, d), lambda j: (j, 0, 0))] * 2
        dw_shapes = [jax.ShapeDtypeStruct((chunks, d, d), BF)] * 2
    return pl.pallas_call(
        lambda *refs: ffn_kernel(plan, *refs),
        grid_spec=pl.GridSpec(
            grid=(chunks,),
            in_specs=[SM, ANY, whole(rows, d), whole(rows, d), whole(d, rows), whole(*par.shape), ANY, whole(8, d)] + [ANY] * len(weights),
            out_specs=dw_specs + [whole(SMALL, d), whole(1, norm_width), pl.BlockSpec((1, rows, d), lambda j: (j, 0, 0)),
                                  pl.BlockSpec((1, d, d), lambda j: (j, 0, 0)), whole(rows, d)],
            scratch_shapes=[
                pltpu.VMEM((chunks, d, d), BF), pltpu.VMEM((chunks, d, d), BF), pltpu.VMEM((rows, d), F32), pltpu.VMEM((rows, d), BF),
                pltpu.VMEM((1, d), F32), pltpu.VMEM((d, d), BF), pltpu.VMEM((rows, d), BF), pltpu.VMEM((rows, d), F32),
                pltpu.SemaphoreType.DMA((chunks,)), pltpu.SemaphoreType.DMA((chunks,)), pltpu.SemaphoreType.DMA((2,)),
            ],
        ),
        out_shape=dw_shapes + [
            jax.ShapeDtypeStruct((SMALL, d), F32), jax.ShapeDtypeStruct((1, norm_width), F32),
            jax.ShapeDtypeStruct((chunks, rows, d), BF), jax.ShapeDtypeStruct((chunks, d, d), BF), jax.ShapeDtypeStruct((rows, d), BF),
        ],
        compiler_params=params(60), name="feedforward",
        cost_estimate=pl.CostEstimate(flops=2 * 5 * rows * d * d * chunks * 2, bytes_accessed=40_000_000, transcendentals=rows * d * chunks),
    )(scalars, x, gl, n2, n2t, par, ff, sm1, *weights)


def output_kernel(sc_ref, x_ref, par_ref, token, wo, wd, act, *rest):
    ctxs, out_ref = rest[:2], rest[2]
    d = x_ref.shape[1]
    gw = d // GROUPS
    total = x_ref[...].astype(F32) + par_ref[4:5, :] + par_ref[5:6, :]
    for g in range(GROUPS):
        ctx = ctxs[0][0] if g == 0 else ctxs[1][g - 1]
        total += mm(ctx, wo[0, g * gw:(g + 1) * gw, :])
    for j in range(wd.shape[0]):
        total += mm(act[j], wd[j])
    out_ref[...] = (total * valid_rows(pl.program_id(0), sc_ref[0])).astype(BF)


def output(scalars, x, par, token, w, wd, act, ctxs):
    rows, d = x.shape
    gw = d // GROUPS
    chunks = wd.shape[0]
    return pl.pallas_call(
        output_kernel,
        grid_spec=pl.GridSpec(
            grid=(rows // BLOCK,),
            in_specs=[SM, pl.BlockSpec((BLOCK, d), lambda i: (i, 0)), pl.BlockSpec(par.shape, lambda i: (0, 0)), pl.BlockSpec(token.shape, lambda i: (0, 0)),
                      pl.BlockSpec((1, d, d), lambda i: (GROUPS, 0, 0)), pl.BlockSpec((chunks, d, d), lambda i: (0, 0, 0)),
                      pl.BlockSpec((chunks, BLOCK, d), lambda i: (0, i, 0))] + [pl.BlockSpec((1, BLOCK, gw), lambda i: (0, i, 0)), pl.BlockSpec((GROUPS - 1, BLOCK, gw), lambda i: (0, i, 0))],
            out_specs=pl.BlockSpec((BLOCK, d), lambda i: (i, 0)),
        ),
        out_shape=jax.ShapeDtypeStruct((rows, d), BF),
        compiler_params=params(28), name="output",
        cost_estimate=pl.CostEstimate(flops=2 * rows * d * d * (chunks + 1), bytes_accessed=18_000_000, transcendentals=0),
    )(scalars, x, par, token, w, wd, act, *ctxs)


def spread(rows_ref, lane):
    norms = rows_ref
    at = lax.broadcasted_iota(jnp.int32, norms.shape, 1)
    own = jnp.sum(jnp.where(at == lane, norms, 0.0), axis=1, keepdims=True)
    return own


def mix_kernel(seqs, sending, sc_ref, r0, r1, sm, smg, dk, dg, uk, ug, ak, ag, token, d_ref, u_ref, a_ref, norm_out, ins, in_sems, *rest):
    flip = 1 if sending else 0
    xb, yb, lob = flip ^ (sc_ref[3] % 2), flip ^ (sc_ref[3] // 2), flip ^ (sc_ref[1] % 2)
    dn = dk.shape[4]
    d_out, u_out, a_out, out_sems = rest if sending else (d_ref, u_ref, a_ref, None)
    jobs = []
    for i in range(4):
        jobs.append(([v.at[i // 2, lob, i % 2] for v in (dk, dg)], i))
    for i in range(4):
        jobs.append(([v.at[i, yb] for v in (uk, ug)], 4 + i))
    for i in range(4):
        jobs.append(([v.at[i, :, xb] for v in (ak, ag)], 8 + i))
    reads = [[pltpu.make_async_copy(src, ins.at[at, t], in_sems.at[2 * at + t]) for t, src in enumerate(srcs)] for srcs, at in jobs]
    for pair in reads:
        for c in pair:
            c.start()
    norms = r0[...] + r1[...]
    norm_out[...] = norms
    mean = jnp.sum(norms, axis=1, keepdims=True) * (1.0 / seqs)
    me = sc_ref[4]
    factor = jnp.minimum(1.0, mean / spread(norms, me)) * (1.0 / seqs)
    other = jnp.minimum(1.0, mean / spread(norms, me ^ 1)) * (1.0 / seqs)
    factor, other = factor[0, 0], other[0, 0]
    mixed = lambda k, g: (k.astype(F32) * factor + g.astype(F32) * other).astype(BF)
    d_out[8 * dn:, :] = mixed(sm[...], smg[...])
    writes = []
    for pair, (_, at) in zip(reads, jobs):
        for c in pair:
            c.wait()
        for t in range(2):
            low = mixed(ins[at, 0, t], ins[at, 1, t])
            if at < 4:
                d_out[(2 * at + t) * dn:(2 * at + t + 1) * dn, :] = low
            elif at < 8:
                u_out[at - 4, 0, t] = low
            else:
                a_out[at - 8, t, 0] = low
        if sending and at % 4 == 3:
            src, dst = ((d_out, d_ref), (u_out, u_ref), (a_out, a_ref))[at // 4]
            writes.append(pltpu.make_async_copy(src, dst, out_sems.at[at // 4]))
            writes[-1].start()
    for c in writes:
        c.wait()


def mix(seqs, sending, scalars, norm_rows, halves, smalls, token):
    dn, d = halves[0].shape[2:]
    ak, ag, uk, ug = (v.reshape(4, 2, 2, dn, d) for v in halves[:4])
    dk, dg = (v.reshape(2, 2, 2, 2, dn, d) for v in halves[4:])
    width = norm_rows[0].shape[1]
    shapes = [(8 * dn + SMALL, d), (4, 1, 2, dn, d), (4, 2, 1, dn, d)]
    scratch = [pltpu.VMEM((12, 2, 2, dn, d), BF), pltpu.SemaphoreType.DMA((24,))]
    if sending:
        scratch += [pltpu.VMEM(s, BF) for s in shapes] + [pltpu.SemaphoreType.DMA((3,))]
    dd, u, a, norms = pl.pallas_call(
        lambda *refs: mix_kernel(seqs, sending, *refs),
        in_specs=[SM] + [VM] * 4 + [ANY] * 7, out_specs=[ANY if sending else VM] * 3 + [VM],
        out_shape=[jax.ShapeDtypeStruct(s, BF) for s in shapes] + [jax.ShapeDtypeStruct((1, width), F32)],
        scratch_shapes=scratch, compiler_params=params(60 if sending else 54), name="mix_send" if sending else "mix_keep",
        cost_estimate=pl.CostEstimate(flops=16_000_000, bytes_accessed=10_600_000, transcendentals=0),
    )(scalars, *norm_rows, *smalls, dk, dg, uk, ug, ak, ag, token)
    return a.reshape(2, 2, 2, 1, dn, d), u.reshape(2, 2, 1, 2, dn, d), dd, norms


def fold_flat_kernel(name, blocks, sc_ref, mine, got, *rest):
    send, keep = rest[-2:]
    dn = send.shape[0] - SMALL
    dn = dn // (blocks // 2)
    add = lambda a, b: (a.astype(F32) + b.astype(F32)).astype(BF)
    bit = side(name, sc_ref, 0)
    for out, which in ((send, 1 ^ bit), (keep, bit)):
        for i in range(blocks // 2):
            rows = pl.ds(pl.multiple_of((2 * i + which) * dn, 16), dn)
            out[i * dn:(i + 1) * dn, :] = add(mine[rows, :], got[rows, :])
        out[blocks // 2 * dn:, :] = add(mine[blocks * dn:, :], got[blocks * dn:, :])


def fold_flat(scalars, name, blocks, mine, got, waits=()):
    total, d = mine.shape
    half = jax.ShapeDtypeStruct(((total - SMALL) // 2 + SMALL, d), BF)
    return pl.pallas_call(
        lambda *refs: fold_flat_kernel(name, blocks, *refs),
        in_specs=[SM, VM, VM] + [ANY] * len(waits), out_specs=[VM, VM], out_shape=[half, half],
        compiler_params=params(16), name="fold_flat_" + name,
        cost_estimate=pl.CostEstimate(flops=mine.size, bytes_accessed=6 * mine.size, transcendentals=0),
    )(scalars, mine, got, *waits)


AXES = dict(hi=0, lo=1, y=2, x=3)


def side(name, sc, flip):
    bit = {"hi": sc[1] // 2, "lo": sc[1] % 2, "y": sc[3] // 2, "x": sc[3] % 2}[name]
    return flip ^ bit


def fold_kernel(sc_ref, ms, gs, mk, gk, *rest):
    send, keep = rest[-2:]
    d = ms.shape[-1]
    add = lambda a, b, out: (a[...].reshape(-1, d).astype(F32) + b[...].reshape(-1, d).astype(F32)).astype(BF).reshape(out.shape)
    send[...] = add(ms, gs, send)
    keep[...] = add(mk, gk, keep)


def fold(scalars, name, mine, got, waits=()):
    axis = AXES[name]
    shape = mine.shape
    blk = (1,) + tuple(1 if i == axis else s for i, s in enumerate(shape) if i > 0)
    spec = lambda flip: pl.BlockSpec(blk, lambda i, sc: (i,) + tuple(side(name, sc, flip) if k == axis else 0 for k in range(1, 6)))
    out = pl.BlockSpec(blk, lambda i, sc: (i, 0, 0, 0, 0, 0))
    half = jax.ShapeDtypeStruct((shape[0],) + blk[1:], BF)
    return pl.pallas_call(
        fold_kernel,
        grid_spec=pltpu.PrefetchScalarGridSpec(num_scalar_prefetch=1, grid=(shape[0],), in_specs=[spec(1), spec(1), spec(0), spec(0)] + [ANY] * len(waits), out_specs=[out, out]),
        out_shape=[half, half], compiler_params=params(16), name="fold_" + name,
        cost_estimate=pl.CostEstimate(flops=mine.size, bytes_accessed=6 * mine.size, transcendentals=0),
    )(scalars, mine, got, mine, got, *waits)


def last_fold_kernel(sc_ref, am, ag, um, ug, dm, dg, send1, send2, keep1, keep2):
    dn = am.shape[4]
    first = send1.shape[0]
    add = lambda a, b: (a.astype(F32) + b.astype(F32)).astype(BF)
    bit = side("hi", sc_ref, 0)
    small = add(dm[2 * dn:, :], dg[2 * dn:, :])
    for out1, out2, which in ((send1, send2, 1 ^ bit), (keep1, keep2, bit)):
        at = 0

        def put(low):
            nonlocal at
            rows = low.shape[0]
            split = min(max(first - at, 0), rows)
            if split > 0:
                out1[at:at + split, :] = low[:split]
            if split < rows:
                out2[at + split - first:at + rows - first, :] = low[split:]
            at += rows
        put(add(am[which, 0, 0, 0], ag[which, 0, 0, 0]))
        put(add(um[which, 0, 0, 0], ug[which, 0, 0, 0]))
        rows = pl.ds(pl.multiple_of(which * dn, 16), dn)
        put(add(dm[rows, :], dg[rows, :]))
        put(small)


def last_fold(scalars, parts, first):
    dn, d = parts[0][0].shape[4:]
    total = 3 * dn + SMALL
    half = [jax.ShapeDtypeStruct((s, d), BF) for s in (first, total - first)]
    return pl.pallas_call(
        last_fold_kernel, in_specs=[SM] + [VM] * 6, out_specs=[VM] * 4, out_shape=half + half,
        compiler_params=params(16), name="last_fold",
        cost_estimate=pl.CostEstimate(flops=2 * total * d, bytes_accessed=12 * total * d, transcendentals=0),
    )(scalars, *[v for pair in parts for v in pair])


def xor_permute(value, axis, size, bit):
    return lax.ppermute(value, axis, [(i, i ^ bit) for i in range(size)])


def butterfly(value, axis, size):
    if size & (size - 1):
        return lax.psum(value, axis)
    bit = 1
    while bit < size:
        value = value + xor_permute(value, axis, size, bit)
        bit *= 2
    return value


def after(value, other):
    return value + other[(slice(0, 1),) * other.ndim].reshape((1,) * value.ndim).astype(value.dtype) * 0


def per_device(sizes, block_input, cotangent, lengths, first_gain, first_shift, second_gain, second_shift, triple_weight, triple_bias,
               output_weight, output_bias, upward_weight, upward_bias, downward_weight, downward_bias):
    rep, n = sizes
    rows, d = block_input.shape
    dn, fn = first_gain.shape[0], upward_bias.shape[0]
    gw = d // GROUPS
    chunks = fn * n // d
    nz = n // 2
    plan = dict(on=rep == 4 and n == 8 and dn % 16 == 0 and chunks == nz == rep, dn=dn, nz=nz, nr=rep)
    ri, fi = lax.axis_index("rep"), lax.axis_index("fsdp")
    z, core = fi // 2, fi % 2
    me = ri * n + fi
    scalars = jnp.stack([lengths[0], z, core, ri, me]).astype(jnp.int32)
    group_cols = lambda v, j: jnp.concatenate([v[:, a * d + j * gw:a * d + (j + 1) * gw] for a in range(3)], axis=1)
    mats = jnp.stack([group_cols(triple_weight, j) for j in range(GROUPS)] + [output_weight])
    small = [first_gain, first_shift, second_gain, second_shift, output_bias, downward_bias, triple_bias, upward_bias]
    wide_row = max(v.shape[0] for v in small)
    low = jnp.asarray(-jnp.inf, BF)
    small = [lax.pad(v.reshape(1, -1), low, ((i, 7 - i, 0), (0, wide_row - v.shape[0], 0))) for i, v in enumerate(small)]
    while len(small) > 1:
        small = [jnp.maximum(a, b) for a, b in zip(small[::2], small[1::2])]
    small = jnp.maximum(small[0], jnp.asarray(-1e4, BF))
    small = jnp.where(jnp.arange(n)[:, None, None] == fi, small[None], 0.0).astype(BF)

    along_z = lambda v: [xor_permute(v, "fsdp", n, 2 * k) for k in range(1, nz)]
    along_rep = lambda v: [xor_permute(v, "rep", rep, j) for j in range(1, rep)]
    to_core = lambda v: xor_permute(v, "fsdp", n, 1)

    def unpack(small):
        small = small.astype(F32)
        par = small[:, :6, :dn].swapaxes(0, 1).reshape(6, d)
        bias_t = small[:, 6, :3 * dn].reshape(1, 3 * d)
        vecs = jnp.concatenate([par] + [group_cols(bias_t, j) for j in range(GROUPS)] + [small[:, 7, :fn].reshape(chunks, d)])
        return jnp.pad(vecs, ((0, -vecs.shape[0] % 8), (0, 0)))

    if plan["on"]:
        quarter = lax.dynamic_index_in_dim(mats, ri, 0, keepdims=False)
        small = small + to_core(small)
        far = along_z(quarter)
        small = jnp.stack([small] + along_z(small))
        sib_own = to_core(mats)
        wide_own = [upward_weight, downward_weight, to_core(upward_weight), to_core(downward_weight)]
        n1, n1t, n2, n2t, gl, par, ready, pick = prepare(plan, scalars, block_input, cotangent, small, upward_weight, downward_weight, [sib_own] + wide_own[2:])
        far = jnp.stack(far)
        near = [far] + along_rep(far)
    else:
        small = butterfly(small, "fsdp", n)
        weights = [lax.all_gather(mats, "fsdp", axis=1, tiled=True)]
        n1, n1t, n2, n2t, gl, par, ready, _ = prepare(plan, scalars, block_input, cotangent, unpack(small), upward_weight, downward_weight, [])
    tables = [jnp.asarray(t) for t in rotary_tables(rows, 128)]

    if plan["on"]:
        wide_far = jnp.stack(along_z(pick))
        weights = [mats, sib_own] + near + [to_core(jnp.stack(near) + ready[0, 0].astype(BF))]
    d3a, ctxa, sma, token_a, w = attention(plan, (0,), scalars, n1, gl, par, tables, weights)
    if plan["on"]:
        wide_far = wide_far + token_a[0, 0].astype(BF)
        wide_near = [wide_far] + along_rep(wide_far)
    d3b, ctxb, smb, token_b = attention(plan, (1, 2), scalars, n1, gl, par, tables, [w])
    if plan["on"]:
        wide_sibs = to_core(jnp.stack(wide_near) + token_b[0, 0].astype(BF))
        wide_weights = wide_own + wide_near + [wide_sibs]
    else:
        up = lax.all_gather(upward_weight, "fsdp", axis=0, tiled=True)
        down = lax.all_gather(downward_weight, "fsdp", axis=0, tiled=True)
        wide_weights = [jnp.stack([up[:, j * d:(j + 1) * d] for j in range(chunks)]), down.reshape(chunks, d, d)]
    *dwa, sm1, ff = closing(plan, scalars, block_input, gl, n1t, par, w, d3a, d3b, ctxa, ctxb, sma, smb)
    width = -(-rep * n // 128) * 128
    *dwf, smalls, norm_row, act, wd, gx = ffn(plan, chunks, scalars, block_input, gl, n2, n2t, par, ff, sm1, wide_weights, width)

    if plan["on"]:
        a, b, c = along_z(norm_row)
        norm_row = (norm_row + a) + (b + c)
        a, b, c = along_rep(norm_row)
        norm_row = (norm_row + a) + (b + c)
        norm_rows = (norm_row, to_core(norm_row))
        halves = []
        for keep, send in ((dwa[0], dwa[1]), (dwf[0], dwf[1]), (dwf[2], dwf[3])):
            halves += [keep, to_core(send)]
        pair = (smalls, to_core(smalls))
        steps = dict(x=("rep", rep, 1), y=("rep", rep, 2), lo=("fsdp", n, 2), hi=("fsdp", n, 4))
        move = lambda v, name: xor_permute(v, *steps[name])
        *sends, norm_row = mix(rep * n, True, scalars, norm_rows, halves, pair, ready)
        norms = norm_row[0, :rep * n]
        *mines, token = mix(rep * n, False, scalars, norm_rows, halves, pair, norm_row)
        out = output(scalars, block_input, par, token, w, wd, act, (ctxa, ctxb))
        parts = []
        for send, mine, order in zip(sends, mines, (("x", "y", "lo"), ("y", "lo", "x"), ("lo", "x", "y"))):
            got = move(send, order[0])
            for at, name in enumerate(order[1:]):
                waits = () if at else (out,)
                if mine.ndim == 2:
                    send, mine = fold_flat(scalars, name, 8 >> at, mine, got, waits)
                else:
                    send, mine = fold(scalars, name, mine, got, waits)
                got = move(send, name)
            parts.append((mine, got))
        first = 3 * dn // 2
        send_1, send_2, mine_1, mine_2 = last_fold(scalars, parts, first)
        add = lambda mine, send: (mine.astype(F32) + move(send, "hi").astype(F32)).astype(BF)
        mine_1 = add(mine_1, send_1)
        around_1 = [mine_1] + along_rep(mine_1)
        mine_2 = add(mine_2, send_2)
        smalls = mine_2[first:].astype(F32)
        mine_2 = mine_2[:first]
        around_2 = [mine_2] + along_rep(mine_2)
        around = [jnp.concatenate([p, q]) for p, q in zip(around_1, around_2)]
        x, y = ri % 2, ri // 2
        flip = lambda bit, a, b: (jnp.where(bit == 1, b, a), jnp.where(bit == 1, a, b))
        a0, a1 = flip(x, around[0], around[1])
        a2, a3 = flip(x, around[2], around[3])
        a0, a2 = flip(y, a0, a2)
        a1, a3 = flip(y, a1, a3)
        final = jnp.stack([a0, a1, a2, a3]).astype(F32)
        g_att, g_up, g_down = final[:, :dn], final[:, dn:2 * dn], final[:, 2 * dn:].reshape(fn, d)
        smalls = smalls.reshape(SMALL, d)
    else:
        norms = butterfly(butterfly(norm_row, "fsdp", n), "rep", rep)[0, :rep * n]
        factor = jnp.minimum(1.0, jnp.mean(norms) / lax.dynamic_index_in_dim(norms, me, 0, keepdims=False)) / (rep * n)
        out = output(scalars, block_input, par, ready, w, wd, act, (ctxa, ctxb))
        scale = lambda v: (v.astype(F32) * factor).astype(BF)
        shards = lambda v: v.reshape(v.shape[0], n, dn, d).swapaxes(0, 1).reshape(n, -1, d)
        pack = jnp.concatenate([scale(shards(dwa[0])), scale(shards(dwf[0])), scale(dwf[1].reshape(n, fn, d))], axis=1)
        mine = lax.psum_scatter(pack, "fsdp", scatter_dimension=0, tiled=True)[0]
        mine = lax.psum(mine, "rep").astype(F32)
        g_att = mine[:4 * dn].reshape(4, dn, d)
        g_up = mine[4 * dn:(4 + chunks) * dn].reshape(chunks, dn, d)
        g_down = mine[(4 + chunks) * dn:]
        smalls = lax.psum(scale(smalls), ("rep", "fsdp")).astype(F32)

    g_triple = jnp.concatenate([g_att[j, :, a * gw:(a + 1) * gw] for a in range(3) for j in range(GROUPS)], axis=1)
    g_upward = jnp.concatenate([g_up[j] for j in range(chunks)], axis=1)
    own = lambda v, width: lax.dynamic_slice_in_dim(v, fi * width, width, 0)
    g1, s1, g2, s2, bd = (own(smalls[i], dn) for i in range(5))
    b_triple = own(jnp.concatenate([smalls[5 + j, a * gw:(a + 1) * gw] for a in range(3) for j in range(GROUPS)]), 3 * dn)
    b_up = own(smalls[8:8 + chunks].reshape(-1), fn)
    return (out, gx, g1, s1, g2, s2, g_triple, b_triple, g_att[GROUPS], bd, g_upward, b_up, g_down, bd, norms)


def solution(mesh):
    rows = P(("rep", "fsdp"), None)
    vec, mat = P("fsdp"), P("fsdp", None)
    sizes = (mesh.shape["rep"], mesh.shape["fsdp"])
    return jax.shard_map(
        lambda *args: per_device(sizes, *args),
        mesh=mesh,
        in_specs=(rows, rows, P(("rep", "fsdp")), vec, vec, vec, vec, mat, vec, mat, vec, mat, vec, mat, vec),
        out_specs=(rows, rows, vec, vec, vec, vec, mat, vec, mat, vec, mat, vec, mat, vec, P()),
        check_vma=False,
    )
```

```python
import math
import numpy as np
import jax
import jax.numpy as jnp
from jax import lax
from jax.experimental import pallas as pl
from jax.experimental.pallas import tpu as pltpu
from jax.sharding import PartitionSpec as P

HEADS = 12
HEAD_DIM = 64
ROT = 16
EPS = 1e-05
MASKED = -1e30
BF = jnp.bfloat16
F32 = jnp.float32
GROUPS = 3
MIB = 1024 * 1024


def mm(a, b):
    return jnp.dot(a, b, preferred_element_type=F32)


def mm_rt(a, b):
    return lax.dot_general(a, b, (((1,), (1,)), ((), ())), preferred_element_type=F32)


def mm_lt(a, b):
    return lax.dot_general(a, b, (((0,), (0,)), ((), ())), preferred_element_type=F32)


def rotary_tables(rows, width):
    half = ROT // 2
    freq = np.exp(np.arange(half, dtype=np.float32) * np.float32(-2.0 * math.log(10000.0) / ROT))
    ang = np.arange(rows, dtype=np.float32)[:, None] * freq.astype(np.float32)[None, :]
    cos, sin = np.cos(ang), np.sin(ang)
    keep = np.ones((rows, HEAD_DIM), np.float32)
    up = np.zeros((rows, HEAD_DIM), np.float32)
    down = np.zeros((rows, HEAD_DIM), np.float32)
    keep[:, :half] = cos
    keep[:, half:ROT] = cos
    up[:, :half] = -sin
    down[:, half:ROT] = sin
    rep = width // HEAD_DIM
    return tuple(np.tile(t, (1, rep)).astype(np.float32) for t in (keep, up, down))


def norm_parts(values):
    centred = values - jnp.mean(values, axis=-1, keepdims=True)
    inverse = lax.rsqrt(jnp.mean(centred * centred, axis=-1, keepdims=True) + EPS)
    return centred * inverse, inverse


def norm_back(e, gain, normed, inverse):
    t = e * gain
    t_mean = jnp.mean(t, axis=-1, keepdims=True)
    cross = jnp.mean(t * normed, axis=-1, keepdims=True)
    return inverse * (t - t_mean - normed * cross)


SMALL = 16
BLOCK = 256
QKV_BIAS = 6
UP_BIAS = QKV_BIAS + GROUPS
VM = pl.BlockSpec(memory_space=pltpu.VMEM)
SM = pl.BlockSpec(memory_space=pltpu.SMEM)
ANY = pl.BlockSpec(memory_space=pl.ANY)


def block(i):
    return pl.ds(pl.multiple_of(i * BLOCK, BLOCK), BLOCK)


def params(mib):
    return pltpu.CompilerParams(vmem_limit_bytes=mib * MIB)


def valid_rows(i, seq):
    return (lax.broadcasted_iota(jnp.int32, (BLOCK, 1), 0) + i * BLOCK < seq).astype(F32)


def unpack_small(small, dn, d, vec_out):
    n = small.shape[0]
    gw = d // GROUPS
    line = lambda row, width: jnp.concatenate([small[s, row:row + 1, :width] for s in range(n)], axis=1)
    vec_out[...] = jnp.zeros_like(vec_out)
    for i in range(6):
        vec_out[i:i + 1, :] = line(i, dn)
    qkv = line(6, 3 * dn)
    for j in range(GROUPS):
        vec_out[QKV_BIAS + j:QKV_BIAS + j + 1, :] = jnp.concatenate([qkv[:, a * d + j * gw:a * d + (j + 1) * gw] for a in range(3)], axis=1)
    up = line(7, small.shape[2])
    for j in range(up.shape[1] // d):
        vec_out[UP_BIAS + j:UP_BIAS + j + 1, :] = up[:, j * d:(j + 1) * d]


def prepare_kernel(plan, waits, sc_ref, x_ref, g_ref, packed, up_ref, down_ref, *rest):
    n1, n1t, n2, n2t, gl, vec_out, token, pick, sems = rest[waits:]
    d = x_ref.shape[1]
    par_ref = vec_out
    if plan["on"]:
        dn, rep = plan["dn"], sc_ref[3]
        cut = [pltpu.make_async_copy(up_ref.at[:, pl.ds(pl.multiple_of(rep * d, 128), d)], pick.at[0], sems.at[0]),
               pltpu.make_async_copy(down_ref.at[pl.ds(pl.multiple_of(rep * dn, 16), dn)], pick.at[1], sems.at[1])]

        @pl.when(pl.program_id(0) == 0)
        def _():
            for c in cut:
                c.start()
            unpack_small(packed[0].astype(F32) + packed[1].astype(F32) + packed[2].astype(F32) + packed[3].astype(F32), dn, d, vec_out)

        @pl.when(pl.program_id(0) == pl.num_programs(0) - 1)
        def _():
            for c in cut:
                c.wait()

    else:
        vec_out[...] = packed[...]
    token[...] = jnp.zeros_like(token)
    normed, _ = norm_parts(x_ref[...].astype(F32))
    one = (normed * par_ref[0:1, :] + par_ref[1:2, :]).astype(BF)
    two = (normed * par_ref[2:3, :] + par_ref[3:4, :]).astype(BF)
    n1[...] = one
    n2[...] = two
    n1t[...] = one.astype(F32).T.astype(BF)
    n2t[...] = two.astype(F32).T.astype(BF)
    gl[...] = (g_ref[...].astype(F32) * valid_rows(pl.program_id(0), sc_ref[0])).astype(BF)


def prepare(plan, scalars, x, g, par, up, down, waits):
    rows, d = x.shape
    flat, turned = jax.ShapeDtypeStruct((rows, d), BF), jax.ShapeDtypeStruct((d, rows), BF)
    vecs = (16, d) if plan["on"] else par.shape
    by_rows, by_cols = pl.BlockSpec((BLOCK, d), lambda i: (i, 0)), pl.BlockSpec((d, BLOCK), lambda i: (0, i))
    return pl.pallas_call(
        lambda *refs: prepare_kernel(plan, len(waits), *refs),
        grid_spec=pl.GridSpec(grid=(rows // BLOCK,), in_specs=[SM, by_rows, by_rows, pl.BlockSpec(par.shape, lambda i: (0,) * par.ndim), ANY, ANY] + [ANY] * len(waits),
                              out_specs=[by_rows, by_cols, by_rows, by_cols, by_rows, pl.BlockSpec(vecs, lambda i: (0, 0)), pl.BlockSpec((1, 1), lambda i: (0, 0)), pl.BlockSpec((2, plan["dn"], d), lambda i: (0, 0, 0))],
                              scratch_shapes=[pltpu.SemaphoreType.DMA((2,))]),
        out_shape=[flat, turned, flat, turned, flat, jax.ShapeDtypeStruct(vecs, F32), jax.ShapeDtypeStruct((1, 1), F32),
                   jax.ShapeDtypeStruct((2, plan["dn"], d), BF)], compiler_params=params(60), name="prepare",
        cost_estimate=pl.CostEstimate(flops=40 * rows * d, bytes_accessed=14 * rows * d, transcendentals=rows),
    )(scalars, x, g, par, up, down, *waits)


def attn_kernel(plan, first, base, sc_ref, n1, gl, b3_ref, keep_ref, up_ref, down_ref, *rest):
    nw = plan["pieces"] if first else 2
    w_refs, rest = rest[:nw], rest[nw:]
    d3, ctx_low, sm_ref, token, rest = rest[0].at[0], rest[1].at[0], rest[2].at[0], rest[3], rest[4:]
    token[...] = jnp.zeros_like(token)
    rows, d = n1.shape
    gw = d // GROUPS
    qb = BLOCK
    nb = rows // qb
    seq = sc_ref[0]
    if first:
        w_out, rest = rest[0], rest[1:]
    q_s, k_s, v_s, dc_s, ctx, dq, dk, dv, qm, km, vm, dcm, pall, dall = rest[:14]

    if first:
        w, sems = rest[14:]
        if plan["on"]:
            z, core, rep = sc_ref[1], sc_ref[2], sc_ref[3]
            dn, nz, nr = plan["dn"], plan["nz"], plan["nr"]
            own, sib, near, sibs = w_refs[0], w_refs[1], w_refs[2:2 + nr], w_refs[2 + nr]
            place = lambda zz, cc: pl.ds(pl.multiple_of((zz * 2 + cc) * dn, 16), dn)
            pairs = []
            for m in range(nr):
                pairs.append((own.at[m], w.at[m, place(z, core)]))
                pairs.append((sib.at[m], w.at[m, place(z, 1 - core)]))
            for j in range(nr):
                for k in range(1, nz):
                    m, zz = rep ^ j, z ^ k
                    pairs.append((near[j].at[k - 1], w.at[m, place(zz, core)]))
                    pairs.append((sibs.at[j, k - 1], w.at[m, place(zz, 1 - core)]))
        else:
            pairs = [(w_refs[0].at[m], w.at[m]) for m in range(GROUPS + 1)]
        copies = [pltpu.make_async_copy(a, b, sems.at[i]) for i, (a, b) in enumerate(pairs)]
        for c in copies:
            c.start()
        for c in copies:
            c.wait()
        back = pltpu.make_async_copy(w, w_out, sems.at[len(pairs)])
        back.start()
        w3, wo = w.at[0], w.at[GROUPS, 0:gw]
    else:
        w3, wo = w_refs[0].at[0], w_refs[1].at[0]
    half = ROT // 2

    def tables(r):
        return tuple(jnp.concatenate([t[r, :]] * (gw // 128), axis=1) for t in (keep_ref, up_ref, down_ref))

    def project(i, c):
        r = block(i)
        t = mm(n1[r, :], w3[...]) + b3_ref[pl.ds(QKV_BIAS + base + pl.program_id(0), 1), :]
        keep, up, down = tables(r)
        for at, ref, scale in ((0, q_s, HEAD_DIM ** -0.5), (1, k_s, None)):
            v = t[:, at * gw:(at + 1) * gw]
            low = (v * keep + pltpu.roll(v, gw - half, 1) * up + pltpu.roll(v, half, 1) * down).astype(BF)
            ref[r, :] = low if scale is None else (low.astype(F32) * scale).astype(BF)
        v_s[r, :] = t[:, 2 * gw:].astype(BF)
        dc_s[r, :] = mm_rt(gl[r, :], wo[...]).astype(BF)
        return c
    lax.fori_loop(0, nb, project, 0, unroll=True)

    key_bias = jnp.where(lax.broadcasted_iota(jnp.int32, (1, rows), 1) < seq, 0.0, MASKED).astype(F32)
    causal = lax.broadcasted_iota(jnp.int32, (qb, qb), 1) <= lax.broadcasted_iota(jnp.int32, (qb, qb), 0)

    heads = gw // HEAD_DIM

    def head(h, c):
        lane = lax.broadcasted_iota(jnp.int32, (1, gw), 1) // HEAD_DIM
        mask = jnp.where(lane == h, 1.0, 0.0).astype(BF)
        for ref, out in ((q_s, qm), (k_s, km), (v_s, vm), (dc_s, dcm)):
            out[h] = ref[...] * mask
        for i in range(nb):
            lo, kl = i * qb, (i + 1) * qb
            s = mm_rt(qm[h, lo:kl, :], k_s[:kl, :]) + key_bias[:, :kl]
            diag = jnp.where(causal, s[:, lo:], MASKED)
            s = diag if i == 0 else jnp.concatenate([s[:, :lo], diag], axis=1)
            dp = mm_rt(dcm[h, lo:kl, :], v_s[:kl, :])
            e = jnp.exp(s - jnp.max(s, axis=1, keepdims=True))
            p = e * (1.0 / jnp.sum(e, axis=1, keepdims=True))
            pall[h, lo:kl, :kl] = p.astype(BF)
            inner = jnp.sum(p * dp, axis=1, keepdims=True)
            dall[h, lo:kl, :kl] = (p * (dp - inner)).astype(BF)
        return c
    lax.fori_loop(0, heads, head, 0, unroll=2)
    for i in range(nb):
        lo, kl = i * qb, (i + 1) * qb
        ctx[lo:kl, :] = sum(mm(pall[h, lo:kl, :kl], vm[h, :kl, :]) for h in range(heads))
        dq[lo:kl, :] = sum(mm(dall[h, lo:kl, :kl], km[h, :kl, :]) for h in range(heads))
        dv[lo:kl, :] = sum(mm_lt(pall[h, lo:, lo:kl], dcm[h, lo:, :]) for h in range(heads))
        dk[lo:kl, :] = sum(mm_lt(dall[h, lo:, lo:kl], qm[h, lo:, :]) for h in range(heads))

    def finish(i, total):
        r = block(i)
        keep, up, down = tables(r)
        parts = []
        for ref, scale in ((dq, HEAD_DIM ** -0.5), (dk, 1.0)):
            v = ref[r, :] * scale
            parts.append(v * keep - pltpu.roll(v, gw - half, 1) * up - pltpu.roll(v, half, 1) * down)
        low = jnp.concatenate(parts + [dv[r, :]], axis=1).astype(BF)
        d3[r, :] = low
        ctx_low[r, :] = ctx[r, :].astype(BF)
        return total + jnp.sum(low.astype(F32), axis=0, keepdims=True)
    db3 = lax.fori_loop(0, nb, finish, jnp.zeros((1, d), F32), unroll=True)
    sm_ref[...] = jnp.broadcast_to(db3, sm_ref.shape)
    if first:
        back.wait()


def attention(plan, groups, scalars, n1, gl, b3, tables, weights):
    rows, d = n1.shape
    gw = d // GROUPS
    first, count, base = groups[0] == 0, len(groups), groups[0]
    plan = dict(plan, pieces=len(weights))
    whole = lambda *shape: pl.BlockSpec(shape, lambda j: (0,) * len(shape))
    stacked = lambda *shape: pl.BlockSpec((1,) + shape, lambda j: (j,) + (0,) * len(shape))
    out_shape = [jax.ShapeDtypeStruct((count, rows, d), BF), jax.ShapeDtypeStruct((count, rows, gw), BF), jax.ShapeDtypeStruct((count, 8, d), F32), jax.ShapeDtypeStruct((1, 1), F32)]
    out_specs = [stacked(rows, d), stacked(rows, gw), stacked(8, d), whole(1, 1)]
    heads = gw // HEAD_DIM
    scratch = [pltpu.VMEM((rows, gw), BF)] * 4 + [pltpu.VMEM((rows, gw), F32)] * 4
    scratch += [pltpu.VMEM((heads, rows, gw), BF)] * 4 + [pltpu.VMEM((heads, rows, rows), BF)] * 2
    if first:
        out_shape.append(jax.ShapeDtypeStruct((GROUPS + 1, d, d), BF))
        out_specs.append(ANY)
        scratch += [pltpu.VMEM((GROUPS + 1, d, d), BF), pltpu.SemaphoreType.DMA((64,))]
        w_specs = [ANY] * len(weights)
    else:
        weights = [weights[0], weights[0]]
        w_specs = [pl.BlockSpec((1, d, d), lambda j: (base + j, 0, 0)), pl.BlockSpec((1, gw, d), lambda j: (GROUPS, base + j, 0))]
    flops = count * (2 * rows * d * (d + gw) + 12 * HEADS // GROUPS * rows * rows * HEAD_DIM)
    return pl.pallas_call(
        lambda *refs: attn_kernel(plan, first, base, *refs),
        grid_spec=pl.GridSpec(
            grid=(count,),
            in_specs=[SM, whole(rows, d), whole(rows, d), whole(*b3.shape)] + [whole(rows, 128)] * 3 + w_specs,
            out_specs=out_specs, scratch_shapes=scratch),
        out_shape=out_shape, compiler_params=params(56 if first else 60), name="attend_first" if first else "attend_rest",
        cost_estimate=pl.CostEstimate(flops=4 * flops, bytes_accessed=8_000_000, transcendentals=count * HEADS * rows * rows // GROUPS),
    )(scalars, n1, gl, b3, *tables, *weights)


def write_halves(value, tmp, keep_ref, send_ref, core, dn):
    tmp[...] = value.astype(BF)
    for z in range(keep_ref.shape[0]):
        mine = pl.ds(pl.multiple_of((2 * z + core) * dn, 16), dn)
        other = pl.ds(pl.multiple_of((2 * z + 1 - core) * dn, 16), dn)
        keep_ref[z, 0] = tmp[mine, :]
        send_ref[z, 0] = tmp[other, :]


def closing_kernel(plan, sc_ref, x_ref, gl, n1t, par_ref, w, d3a, d3b, ctxa, ctxb, sma, smb, *rest):
    nd = 2 if plan["on"] else 1
    dw_refs, rest = rest[:nd], rest[nd:]
    sm_ref, ff_ref, gf, tmp, x_s, gl_s, ctx_s, sems = rest
    step = pl.program_id(0)
    rows, d = x_ref.shape
    nb = rows // BLOCK
    late = [pltpu.make_async_copy(x_ref, x_s, sems.at[0]), pltpu.make_async_copy(gl, gl_s, sems.at[1]),
            pltpu.make_async_copy(ctxa, ctx_s.at[pl.ds(0, 1)], sems.at[2]), pltpu.make_async_copy(ctxb, ctx_s.at[pl.ds(1, GROUPS - 1)], sems.at[3])]

    @pl.when(step == 0)
    def _():
        for c in late:
            c.start()

    def store(dw):
        if plan["on"]:
            write_halves(dw, tmp, dw_refs[0], dw_refs[1], sc_ref[2], plan["dn"])
        else:
            dw_refs[0][0] = dw.astype(BF)
        return jnp.sum(dw * dw, axis=0, keepdims=True)

    def group(first, d3, db3):
        def body(i, c):
            r = block(i)
            part = mm_rt(d3[0, r, :], w[0])
            gf[r, :] = part if first else gf[r, :] + part
            return c
        lax.fori_loop(0, nb, body, 0, unroll=True)
        total = store(mm(n1t[...], d3[0])) + db3 * db3
        sm_ref[pl.ds(2 + step, 1), :] = db3
        sm_ref[5:6, :] = total if first else sm_ref[5:6, :] + total

    @pl.when(step == 0)
    def _():
        group(True, d3a, sma[0, 0:1, :])

    @pl.when(jnp.logical_and(step > 0, step < GROUPS))
    def _():
        group(False, d3b, smb[0, 0:1, :])

    @pl.when(step == GROUPS)
    def _():
        for c in late:
            c.wait()
        total = store(mm_lt(jnp.concatenate([ctx_s[g] for g in range(GROUPS)], axis=1), gl_s[...]))

        def back(i, c):
            r = block(i)
            normed, inverse = norm_parts(x_s[r, :].astype(F32))
            e = gf[r, :]
            ff_ref[r, :] = norm_back(e, par_ref[0:1, :], normed, inverse)
            return (c[0] + jnp.sum(e * normed, axis=0, keepdims=True), c[1] + jnp.sum(e, axis=0, keepdims=True))
        zero = jnp.zeros((1, d), F32)
        dgain, dshift = lax.fori_loop(0, nb, back, (zero, zero), unroll=True)
        sm_ref[0:1, :] = dgain
        sm_ref[1:2, :] = dshift
        sm_ref[5:6, :] += total + dgain * dgain + dshift * dshift


def closing(plan, scalars, x, gl, n1t, par, w, d3a, d3b, ctxa, ctxb, sma, smb):
    rows, d = x.shape
    gw = d // GROUPS
    whole = lambda *shape: pl.BlockSpec(shape, lambda j: (0,) * len(shape))
    later = lambda *shape: pl.BlockSpec((1,) + shape, lambda j: (jnp.clip(j - 1, 0, GROUPS - 2),) + (0,) * len(shape))
    if plan["on"]:
        nz, dn = plan["nz"], plan["dn"]
        dw_specs = [pl.BlockSpec((nz, 1, dn, d), lambda j: (0, j, 0, 0))] * 2
        dw_shapes = [jax.ShapeDtypeStruct((nz, GROUPS + 1, dn, d), BF)] * 2
    else:
        dw_specs = [pl.BlockSpec((1, d, d), lambda j: (j, 0, 0))]
        dw_shapes = [jax.ShapeDtypeStruct((GROUPS + 1, d, d), BF)]
    return pl.pallas_call(
        lambda *refs: closing_kernel(plan, *refs),
        grid_spec=pl.GridSpec(
            grid=(GROUPS + 1,),
            in_specs=[SM, ANY, ANY, whole(d, rows), whole(*par.shape),
                      pl.BlockSpec((1, d, d), lambda j: (jnp.minimum(j, GROUPS - 1), 0, 0)),
                      whole(1, rows, d), later(rows, d), ANY, ANY, whole(1, 8, d), later(8, d)],
            out_specs=dw_specs + [whole(8, d), whole(rows, d)],
            scratch_shapes=[pltpu.VMEM((rows, d), F32), pltpu.VMEM((d, d), BF), pltpu.VMEM((rows, d), BF), pltpu.VMEM((rows, d), BF),
                            pltpu.VMEM((GROUPS, rows, gw), BF), pltpu.SemaphoreType.DMA((4,))],
        ),
        out_shape=dw_shapes + [jax.ShapeDtypeStruct((8, d), F32), jax.ShapeDtypeStruct((rows, d), F32)],
        compiler_params=params(60), name="closing",
        cost_estimate=pl.CostEstimate(flops=4 * rows * d * 7 * d, bytes_accessed=8_000_000, transcendentals=rows),
    )(scalars, x, gl, n1t, par, w, d3a, d3b, ctxa, ctxb, sma, smb)


ERF_P = 0.3275911
ERF_A = (0.254829592, -0.284496736, 1.421413741, -1.453152027, 1.061405429)


def gelu_parts(u):
    z = jnp.abs(u) * (2.0 ** -0.5)
    t = 1.0 / (1.0 + ERF_P * z)
    bell = jnp.exp(-0.5 * (u * u))
    a1, a2, a3, a4, a5 = (0.5 * a for a in ERF_A)
    tail = ((((a5 * t + a4) * t + a3) * t + a2) * t + a1) * t * bell
    cdf = jnp.where(u >= 0.0, 1.0 - tail, tail)
    return u * cdf, cdf + u * bell * (1.0 / math.sqrt(2.0 * math.pi))


def ffn_kernel(plan, sc_ref, x_ref, gl, n2, n2t, par_ref, ff_ref, sm1_ref, *rest):
    nw = plan["pieces"]
    w_refs, rest = rest[:nw], rest[nw:]
    nd = 4 if plan["on"] else 2
    dw_refs, rest = rest[:nd], rest[nd:]
    sm_ref, norm_ref, act_ref, wd_ref, gx_ref = rest[:5]
    wu_s, wd_s, gs, gup, sq, tmp, x_s, ff_s, up_sems, down_sems, late_sems = rest[5:]
    late = [pltpu.make_async_copy(x_ref, x_s, late_sems.at[0]), pltpu.make_async_copy(ff_ref, ff_s, late_sems.at[1])]
    step = pl.program_id(0)
    last = pl.num_programs(0) - 1
    rows, d = x_ref.shape
    fc = d
    nb = rows // BLOCK

    @pl.when(step == 0)
    def _():
        if plan["on"]:
            z, core, rep = sc_ref[1], sc_ref[2], sc_ref[3]
            dn, nz, nr = plan["dn"], plan["nz"], plan["nr"]
            own_up, own_down, sib_up, sib_down = w_refs[:4]
            near, sibs = w_refs[4:4 + nr], w_refs[4 + nr]

            def up(src, m, zz, cc):
                dst = wu_s.at[m, pl.ds(pl.multiple_of((zz * 2 + cc) * dn, 16), dn)]
                pltpu.make_async_copy(src, dst, up_sems.at[m]).start()

            def down(src, b, zz, cc):
                dst = wd_s.at[zz, pl.ds(pl.multiple_of((cc * nr + b) * dn, 16), dn)]
                pltpu.make_async_copy(src, dst, down_sems.at[zz]).start()
            for m in range(nr):
                cols, part = pl.ds(m * d, d), pl.ds(m * dn, dn)
                up(own_up.at[:, cols], m, z, core)
                up(sib_up.at[:, cols], m, z, 1 - core)
                down(own_down.at[part], m, z, core)
                down(sib_down.at[part], m, z, 1 - core)
            for j in range(nr):
                for k in range(1, nz):
                    up(near[j].at[k - 1, 0], rep ^ j, z ^ k, core)
                    up(sibs.at[j, k - 1, 0], rep ^ j, z ^ k, 1 - core)
                    down(near[j].at[k - 1, 1], rep ^ j, z ^ k, core)
                    down(sibs.at[j, k - 1, 1], rep ^ j, z ^ k, 1 - core)
        else:
            for m in range(wu_s.shape[0]):
                pltpu.make_async_copy(w_refs[0].at[m], wu_s.at[m], up_sems.at[m]).start()
                pltpu.make_async_copy(w_refs[1].at[m], wd_s.at[m], down_sems.at[m]).start()
        for c in late:
            c.start()
        gs[...] = jnp.zeros_like(gs)
        sq[...] = jnp.zeros_like(sq)
        sm_ref[...] = jnp.zeros_like(sm_ref)

    pltpu.make_async_copy(wu_s.at[step], wu_s.at[step], up_sems.at[step]).wait()
    pltpu.make_async_copy(wd_s.at[step], wd_s.at[step], down_sems.at[step]).wait()
    wu, wd = wu_s.at[step], wd_s.at[step]
    wd_ref[0] = wd[...]

    def rows_step(i, dbu):
        r = block(i)
        u = mm(n2[r, :], wu[...]) + par_ref[pl.ds(UP_BIAS + step, 1), :]
        da = mm_rt(gl[r, :], wd[...])
        a, slope = gelu_parts(u)
        act_ref[0, r, :] = a.astype(BF)
        gu = (da * slope).astype(BF)
        gup[r, :] = gu
        gs[r, :] += mm_rt(gu, wu[...])
        return dbu + jnp.sum(gu.astype(F32), axis=0, keepdims=True)
    dbu = lax.fori_loop(0, nb, rows_step, jnp.zeros((1, fc), F32), unroll=True)
    sm_ref[pl.ds(8 + step, 1), :] = dbu

    dwu = mm(n2t[...], gup[...])
    total = jnp.sum(dwu * dwu, axis=0, keepdims=True) + dbu * dbu
    if plan["on"]:
        write_halves(dwu, tmp, dw_refs[0], dw_refs[1], sc_ref[2], plan["dn"])
    else:
        dw_refs[0][0] = dwu.astype(BF)
    dwd = mm_lt(act_ref[0], gl[...])
    total += jnp.sum(dwd * dwd, axis=0, keepdims=True)
    if plan["on"]:
        tmp[...] = dwd.astype(BF)
        core, dn, nr = sc_ref[2], plan["dn"], plan["nr"]
        for m in range(nr):
            dw_refs[2][0, m] = tmp[pl.ds(pl.multiple_of((core * nr + m) * dn, 16), dn), :]
            dw_refs[3][0, m] = tmp[pl.ds(pl.multiple_of(((1 - core) * nr + m) * dn, 16), dn), :]
    else:
        dw_refs[1][0] = dwd.astype(BF)
    sq[...] += total

    @pl.when(step == last)
    def _():
        for c in late:
            c.wait()

        def back(i, c):
            r = block(i)
            normed, inverse = norm_parts(x_s[r, :].astype(F32))
            e = gs[r, :]
            grad_rows = gl[r, :].astype(F32)
            gx_ref[r, :] = (grad_rows + ff_s[r, :] + norm_back(e, par_ref[2:3, :], normed, inverse)).astype(BF)
            return (c[0] + jnp.sum(e * normed, axis=0, keepdims=True), c[1] + jnp.sum(e, axis=0, keepdims=True),
                    c[2] + jnp.sum(grad_rows, axis=0, keepdims=True))
        zero = jnp.zeros((1, d), F32)
        dgain, dshift, dbd = lax.fori_loop(0, nb, back, (zero, zero, zero), unroll=True)
        sm_ref[0:2, :] = sm1_ref[0:2, :]
        sm_ref[2:3, :] = dgain
        sm_ref[3:4, :] = dshift
        sm_ref[4:5, :] = dbd
        sm_ref[5:8, :] = sm1_ref[2:5, :]
        final = sq[...] + sm1_ref[5:6, :] + dgain * dgain + dshift * dshift + 2.0 * dbd * dbd
        own = jnp.sqrt(jnp.sum(final, axis=1, keepdims=True))
        here = lax.broadcasted_iota(jnp.int32, norm_ref.shape, 1) == sc_ref[4]
        norm_ref[...] = jnp.where(here, own, 0.0)


def ffn(plan, chunks, scalars, x, gl, n2, n2t, par, ff, sm1, weights, norm_width):
    rows, d = x.shape
    plan = dict(plan, pieces=len(weights))
    whole = lambda *shape: pl.BlockSpec(shape, lambda j: (0,) * len(shape))
    if plan["on"]:
        nz, dn, nr = plan["nz"], plan["dn"], plan["nr"]
        dw_specs = [pl.BlockSpec((nz, 1, dn, d), lambda j: (0, j, 0, 0))] * 2 + [pl.BlockSpec((1, nr, dn, d), lambda j: (j, 0, 0, 0))] * 2
        dw_shapes = [jax.ShapeDtypeStruct((nz, chunks, dn, d), BF)] * 2 + [jax.ShapeDtypeStruct((nz, nr, dn, d), BF)] * 2
    else:
        dw_specs = [pl.BlockSpec((1, d, d), lambda j: (j, 0, 0))] * 2
        dw_shapes = [jax.ShapeDtypeStruct((chunks, d, d), BF)] * 2
    return pl.pallas_call(
        lambda *refs: ffn_kernel(plan, *refs),
        grid_spec=pl.GridSpec(
            grid=(chunks,),
            in_specs=[SM, ANY, whole(rows, d), whole(rows, d), whole(d, rows), whole(*par.shape), ANY, whole(8, d)] + [ANY] * len(weights),
            out_specs=dw_specs + [whole(SMALL, d), whole(1, norm_width), pl.BlockSpec((1, rows, d), lambda j: (j, 0, 0)),
                                  pl.BlockSpec((1, d, d), lambda j: (j, 0, 0)), whole(rows, d)],
            scratch_shapes=[
                pltpu.VMEM((chunks, d, d), BF), pltpu.VMEM((chunks, d, d), BF), pltpu.VMEM((rows, d), F32), pltpu.VMEM((rows, d), BF),
                pltpu.VMEM((1, d), F32), pltpu.VMEM((d, d), BF), pltpu.VMEM((rows, d), BF), pltpu.VMEM((rows, d), F32),
                pltpu.SemaphoreType.DMA((chunks,)), pltpu.SemaphoreType.DMA((chunks,)), pltpu.SemaphoreType.DMA((2,)),
            ],
        ),
        out_shape=dw_shapes + [
            jax.ShapeDtypeStruct((SMALL, d), F32), jax.ShapeDtypeStruct((1, norm_width), F32),
            jax.ShapeDtypeStruct((chunks, rows, d), BF), jax.ShapeDtypeStruct((chunks, d, d), BF), jax.ShapeDtypeStruct((rows, d), BF),
        ],
        compiler_params=params(60), name="feedforward",
        cost_estimate=pl.CostEstimate(flops=2 * 5 * rows * d * d * chunks * 2, bytes_accessed=40_000_000, transcendentals=rows * d * chunks),
    )(scalars, x, gl, n2, n2t, par, ff, sm1, *weights)


def output_kernel(sc_ref, x_ref, par_ref, token, wo, wd, act, *rest):
    ctxs, out_ref, done = rest[:2], rest[2], rest[3]
    done[...] = jnp.zeros_like(done)
    d = x_ref.shape[1]
    gw = d // GROUPS
    total = x_ref[...].astype(F32) + par_ref[4:5, :] + par_ref[5:6, :]
    for g in range(GROUPS):
        ctx = ctxs[0][0] if g == 0 else ctxs[1][g - 1]
        total += mm(ctx, wo[0, g * gw:(g + 1) * gw, :])
    for j in range(wd.shape[0]):
        total += mm(act[j], wd[j])
    out_ref[...] = (total * valid_rows(pl.program_id(0), sc_ref[0])).astype(BF)


def output(scalars, x, par, token, w, wd, act, ctxs):
    rows, d = x.shape
    gw = d // GROUPS
    chunks = wd.shape[0]
    return pl.pallas_call(
        output_kernel,
        grid_spec=pl.GridSpec(
            grid=(rows // BLOCK,),
            in_specs=[SM, pl.BlockSpec((BLOCK, d), lambda i: (i, 0)), pl.BlockSpec(par.shape, lambda i: (0, 0)), pl.BlockSpec(token.shape, lambda i: (0, 0)),
                      pl.BlockSpec((1, d, d), lambda i: (GROUPS, 0, 0)), pl.BlockSpec((chunks, d, d), lambda i: (0, 0, 0)),
                      pl.BlockSpec((chunks, BLOCK, d), lambda i: (0, i, 0))] + [pl.BlockSpec((1, BLOCK, gw), lambda i: (0, i, 0)), pl.BlockSpec((GROUPS - 1, BLOCK, gw), lambda i: (0, i, 0))],
            out_specs=[pl.BlockSpec((BLOCK, d), lambda i: (i, 0)), pl.BlockSpec((1, 128), lambda i: (0, 0))],
        ),
        out_shape=[jax.ShapeDtypeStruct((rows, d), BF), jax.ShapeDtypeStruct((1, 128), F32)],
        compiler_params=params(28), name="output",
        cost_estimate=pl.CostEstimate(flops=2 * rows * d * d * (chunks + 1), bytes_accessed=18_000_000, transcendentals=0),
    )(scalars, x, par, token, w, wd, act, *ctxs)


def spread(rows_ref, lane):
    norms = rows_ref
    at = lax.broadcasted_iota(jnp.int32, norms.shape, 1)
    own = jnp.sum(jnp.where(at == lane, norms, 0.0), axis=1, keepdims=True)
    return own


def mix_kernel(seqs, sending, sc_ref, r0, r1, sm, smg, dk, dg, uk, ug, ak, ag, token, d_ref, u_ref, a_ref, norm_out, d_in, u_in, a_in, in_sems, *rest):
    ins = (d_in, u_in, a_in)
    flip = 1 if sending else 0
    xb, yb, lob = flip ^ (sc_ref[3] % 2), flip ^ (sc_ref[3] // 2), flip ^ (sc_ref[1] % 2)
    dn = dk.shape[4]
    d_out, u_out, a_out, out_sems = rest if sending else (d_ref, u_ref, a_ref, None)
    wanted = ([v.at[:, lob] for v in (dk, dg)], [v.at[:, yb] for v in (uk, ug)], [v.at[:, :, xb] for v in (ak, ag)])
    reads = [[pltpu.make_async_copy(src, dst.at[t], in_sems.at[2 * p + t]) for t, src in enumerate(srcs)] for p, (srcs, dst) in enumerate(zip(wanted, ins))]
    for pair in reads:
        for c in pair:
            c.start()
    norms = r0[...] + r1[...]
    norm_out[...] = norms
    mean = jnp.sum(norms, axis=1, keepdims=True) * (1.0 / seqs)
    me = sc_ref[4]
    factor = jnp.minimum(1.0, mean / spread(norms, me)) * (1.0 / seqs)
    other = jnp.minimum(1.0, mean / spread(norms, me ^ 1)) * (1.0 / seqs)
    factor, other = factor[0, 0], other[0, 0]
    mixed = lambda k, g: (k.astype(F32) * factor + g.astype(F32) * other).astype(BF)
    d_out[8 * dn:, :] = mixed(sm[...], smg[...])
    writes = []
    for p, pair in enumerate(reads):
        for c in pair:
            c.wait()
        for i in range(4):
            for t in range(2):
                if p == 0:
                    at = (2 * i + t) * dn
                    d_out[at:at + dn, :] = mixed(d_in[0, i // 2, i % 2, t], d_in[1, i // 2, i % 2, t])
                elif p == 1:
                    u_out[i, 0, t] = mixed(u_in[0, i, t], u_in[1, i, t])
                else:
                    a_out[i, t, 0] = mixed(a_in[0, i, t], a_in[1, i, t])
        if sending:
            src, dst = ((d_out, d_ref), (u_out, u_ref), (a_out, a_ref))[p]
            writes.append(pltpu.make_async_copy(src, dst, out_sems.at[p]))
            writes[-1].start()
    for c in writes:
        c.wait()


def mix(seqs, sending, scalars, norm_rows, halves, smalls, token):
    dn, d = halves[0].shape[2:]
    ak, ag, uk, ug = (v.reshape(4, 2, 2, dn, d) for v in halves[:4])
    dk, dg = (v.reshape(2, 2, 2, 2, dn, d) for v in halves[4:])
    width = norm_rows[0].shape[1]
    shapes = [(8 * dn + SMALL, d), (4, 1, 2, dn, d), (4, 2, 1, dn, d)]
    scratch = [pltpu.VMEM((2, 2, 2, 2, dn, d), BF), pltpu.VMEM((2, 4, 2, dn, d), BF), pltpu.VMEM((2, 4, 2, dn, d), BF), pltpu.SemaphoreType.DMA((6,))]
    if sending:
        scratch += [pltpu.VMEM(s, BF) for s in shapes] + [pltpu.SemaphoreType.DMA((3,))]
    dd, u, a, norms = pl.pallas_call(
        lambda *refs: mix_kernel(seqs, sending, *refs),
        in_specs=[SM] + [VM] * 4 + [ANY] * 7, out_specs=[ANY if sending else VM] * 3 + [VM],
        out_shape=[jax.ShapeDtypeStruct(s, BF) for s in shapes] + [jax.ShapeDtypeStruct((1, width), F32)],
        scratch_shapes=scratch, compiler_params=params(60 if sending else 54), name="mix_send" if sending else "mix_keep",
        cost_estimate=pl.CostEstimate(flops=16_000_000, bytes_accessed=10_600_000, transcendentals=0),
    )(scalars, *norm_rows, *smalls, dk, dg, uk, ug, ak, ag, token)
    return a.reshape(2, 2, 2, 1, dn, d), u.reshape(2, 2, 1, 2, dn, d), dd, norms


def fold_flat_kernel(name, blocks, sc_ref, mine, got, *rest):
    send, keep = rest[-2:]
    dn = send.shape[0] - SMALL
    dn = dn // (blocks // 2)
    add = lambda a, b: (a.astype(F32) + b.astype(F32)).astype(BF)
    bit = side(name, sc_ref, 0)
    for out, which in ((send, 1 ^ bit), (keep, bit)):
        for i in range(blocks // 2):
            rows = pl.ds(pl.multiple_of((2 * i + which) * dn, 16), dn)
            out[i * dn:(i + 1) * dn, :] = add(mine[rows, :], got[rows, :])
        out[blocks // 2 * dn:, :] = add(mine[blocks * dn:, :], got[blocks * dn:, :])


def fold_flat(scalars, name, blocks, mine, got, waits=()):
    total, d = mine.shape
    half = jax.ShapeDtypeStruct(((total - SMALL) // 2 + SMALL, d), BF)
    return pl.pallas_call(
        lambda *refs: fold_flat_kernel(name, blocks, *refs),
        in_specs=[SM, VM, VM] + [ANY] * len(waits), out_specs=[VM, VM], out_shape=[half, half],
        compiler_params=params(16), name="fold_flat_" + name,
        cost_estimate=pl.CostEstimate(flops=mine.size, bytes_accessed=6 * mine.size, transcendentals=0),
    )(scalars, mine, got, *waits)


AXES = dict(hi=0, lo=1, y=2, x=3)


def side(name, sc, flip):
    bit = {"hi": sc[1] // 2, "lo": sc[1] % 2, "y": sc[3] // 2, "x": sc[3] % 2}[name]
    return flip ^ bit


def fold_kernel(sc_ref, ms, gs, mk, gk, *rest):
    send, keep = rest[-2:]
    d = ms.shape[-1]
    add = lambda a, b, out: (a[...].reshape(-1, d).astype(F32) + b[...].reshape(-1, d).astype(F32)).astype(BF).reshape(out.shape)
    send[...] = add(ms, gs, send)
    keep[...] = add(mk, gk, keep)


def fold(scalars, name, mine, got, waits=()):
    axis = AXES[name]
    shape = mine.shape
    blk = (1,) + tuple(1 if i == axis else s for i, s in enumerate(shape) if i > 0)
    spec = lambda flip: pl.BlockSpec(blk, lambda i, sc: (i,) + tuple(side(name, sc, flip) if k == axis else 0 for k in range(1, 6)))
    out = pl.BlockSpec(blk, lambda i, sc: (i, 0, 0, 0, 0, 0))
    half = jax.ShapeDtypeStruct((shape[0],) + blk[1:], BF)
    return pl.pallas_call(
        fold_kernel,
        grid_spec=pltpu.PrefetchScalarGridSpec(num_scalar_prefetch=1, grid=(shape[0],), in_specs=[spec(1), spec(1), spec(0), spec(0)] + [ANY] * len(waits), out_specs=[out, out]),
        out_shape=[half, half], compiler_params=params(16), name="fold_" + name,
        cost_estimate=pl.CostEstimate(flops=mine.size, bytes_accessed=6 * mine.size, transcendentals=0),
    )(scalars, mine, got, mine, got, *waits)


def last_fold_kernel(sc_ref, am, ag, um, ug, dm, dg, send1, send2, keep1, keep2):
    dn = am.shape[4]
    first = send1.shape[0]
    add = lambda a, b: (a.astype(F32) + b.astype(F32)).astype(BF)
    bit = side("hi", sc_ref, 0)
    small = add(dm[2 * dn:, :], dg[2 * dn:, :])
    for out1, out2, which in ((send1, send2, 1 ^ bit), (keep1, keep2, bit)):
        at = 0

        def put(low):
            nonlocal at
            rows = low.shape[0]
            split = min(max(first - at, 0), rows)
            if split > 0:
                out1[at:at + split, :] = low[:split]
            if split < rows:
                out2[at + split - first:at + rows - first, :] = low[split:]
            at += rows
        put(add(am[which, 0, 0, 0], ag[which, 0, 0, 0]))
        put(add(um[which, 0, 0, 0], ug[which, 0, 0, 0]))
        rows = pl.ds(pl.multiple_of(which * dn, 16), dn)
        put(add(dm[rows, :], dg[rows, :]))
        put(small)


def last_fold(scalars, parts, first):
    dn, d = parts[0][0].shape[4:]
    total = 3 * dn + SMALL
    half = [jax.ShapeDtypeStruct((s, d), BF) for s in (first, total - first)]
    return pl.pallas_call(
        last_fold_kernel, in_specs=[SM] + [VM] * 6, out_specs=[VM] * 4, out_shape=half + half,
        compiler_params=params(16), name="last_fold",
        cost_estimate=pl.CostEstimate(flops=2 * total * d, bytes_accessed=12 * total * d, transcendentals=0),
    )(scalars, *[v for pair in parts for v in pair])


def xor_permute(value, axis, size, bit):
    return lax.ppermute(value, axis, [(i, i ^ bit) for i in range(size)])


def butterfly(value, axis, size):
    if size & (size - 1):
        return lax.psum(value, axis)
    bit = 1
    while bit < size:
        value = value + xor_permute(value, axis, size, bit)
        bit *= 2
    return value


def after(value, other):
    return value + other[(slice(0, 1),) * other.ndim].reshape((1,) * value.ndim).astype(value.dtype) * 0


def per_device(sizes, block_input, cotangent, lengths, first_gain, first_shift, second_gain, second_shift, triple_weight, triple_bias,
               output_weight, output_bias, upward_weight, upward_bias, downward_weight, downward_bias):
    rep, n = sizes
    rows, d = block_input.shape
    dn, fn = first_gain.shape[0], upward_bias.shape[0]
    gw = d // GROUPS
    chunks = fn * n // d
    nz = n // 2
    plan = dict(on=rep == 4 and n == 8 and dn % 16 == 0 and chunks == nz == rep, dn=dn, nz=nz, nr=rep)
    ri, fi = lax.axis_index("rep"), lax.axis_index("fsdp")
    z, core = fi // 2, fi % 2
    me = ri * n + fi
    scalars = jnp.stack([lengths[0], z, core, ri, me]).astype(jnp.int32)
    group_cols = lambda v, j: jnp.concatenate([v[:, a * d + j * gw:a * d + (j + 1) * gw] for a in range(3)], axis=1)
    mats = jnp.stack([group_cols(triple_weight, j) for j in range(GROUPS)] + [output_weight])
    small = [first_gain, first_shift, second_gain, second_shift, output_bias, downward_bias, triple_bias, upward_bias]
    wide_row = max(v.shape[0] for v in small)
    low = jnp.asarray(-jnp.inf, BF)
    small = [lax.pad(v.reshape(1, -1), low, ((i, 7 - i, 0), (0, wide_row - v.shape[0], 0))) for i, v in enumerate(small)]
    while len(small) > 1:
        small = [jnp.maximum(a, b) for a, b in zip(small[::2], small[1::2])]
    small = jnp.maximum(small[0], jnp.asarray(-1e4, BF))
    small = jnp.where(jnp.arange(n)[:, None, None] == fi, small[None], 0.0).astype(BF)

    along_z = lambda v: [xor_permute(v, "fsdp", n, 2 * k) for k in range(1, nz)]
    along_rep = lambda v: [xor_permute(v, "rep", rep, j) for j in range(1, rep)]
    to_core = lambda v: xor_permute(v, "fsdp", n, 1)

    def unpack(small):
        small = small.astype(F32)
        par = small[:, :6, :dn].swapaxes(0, 1).reshape(6, d)
        bias_t = small[:, 6, :3 * dn].reshape(1, 3 * d)
        vecs = jnp.concatenate([par] + [group_cols(bias_t, j) for j in range(GROUPS)] + [small[:, 7, :fn].reshape(chunks, d)])
        return jnp.pad(vecs, ((0, -vecs.shape[0] % 8), (0, 0)))

    if plan["on"]:
        quarter = lax.dynamic_index_in_dim(mats, ri, 0, keepdims=False)
        small = small + to_core(small)
        far = along_z(quarter)
        small = jnp.stack([small] + along_z(small))
        sib_own = to_core(mats)
        wide_own = [upward_weight, downward_weight, to_core(upward_weight), to_core(downward_weight)]
        n1, n1t, n2, n2t, gl, par, ready, pick = prepare(plan, scalars, block_input, cotangent, small, upward_weight, downward_weight, [sib_own] + wide_own[2:])
        far = jnp.stack(far)
        near = [far] + along_rep(far)
    else:
        small = butterfly(small, "fsdp", n)
        weights = [lax.all_gather(mats, "fsdp", axis=1, tiled=True)]
        n1, n1t, n2, n2t, gl, par, ready, _ = prepare(plan, scalars, block_input, cotangent, unpack(small), upward_weight, downward_weight, [])
    tables = [jnp.asarray(t) for t in rotary_tables(rows, 128)]

    if plan["on"]:
        wide_far = jnp.stack(along_z(pick))
        weights = [mats, sib_own] + near + [to_core(jnp.stack(near) + ready[0, 0].astype(BF))]
    d3a, ctxa, sma, token_a, w = attention(plan, (0,), scalars, n1, gl, par, tables, weights)
    if plan["on"]:
        wide_far = wide_far + token_a[0, 0].astype(BF)
        wide_near = [wide_far] + along_rep(wide_far)
    d3b, ctxb, smb, token_b = attention(plan, (1, 2), scalars, n1, gl, par, tables, [w])
    if plan["on"]:
        wide_sibs = to_core(jnp.stack(wide_near) + token_b[0, 0].astype(BF))
        wide_weights = wide_own + wide_near + [wide_sibs]
    else:
        up = lax.all_gather(upward_weight, "fsdp", axis=0, tiled=True)
        down = lax.all_gather(downward_weight, "fsdp", axis=0, tiled=True)
        wide_weights = [jnp.stack([up[:, j * d:(j + 1) * d] for j in range(chunks)]), down.reshape(chunks, d, d)]
    *dwa, sm1, ff = closing(plan, scalars, block_input, gl, n1t, par, w, d3a, d3b, ctxa, ctxb, sma, smb)
    width = -(-rep * n // 128) * 128
    *dwf, smalls, norm_row, act, wd, gx = ffn(plan, chunks, scalars, block_input, gl, n2, n2t, par, ff, sm1, wide_weights, width)

    if plan["on"]:
        steps = dict(x=("rep", rep, 1), y=("rep", rep, 2), lo=("fsdp", n, 2), hi=("fsdp", n, 4))
        move = lambda v, name: xor_permute(v, *steps[name])
        a, b, c = along_z(norm_row)
        norm_row = (norm_row + a) + (b + c)
        a, b, c = along_rep(norm_row)
        norm_row = (norm_row + a) + (b + c)
        norm_rows = (norm_row, to_core(norm_row))
        halves = []
        for keep, send in ((dwa[0], dwa[1]), (dwf[0], dwf[1]), (dwf[2], dwf[3])):
            halves += [keep, to_core(send)]
        pair = (smalls, to_core(smalls))
        *sends, norm_row = mix(rep * n, True, scalars, norm_rows, halves, pair, ready)
        norms = norm_row[0, :rep * n]
        *mines, token = mix(rep * n, False, scalars, norm_rows, halves, pair, norm_row)
        out, done = output(scalars, block_input, par, token, w, wd, act, (ctxa, ctxb))
        parts = []
        for send, mine, order in zip(sends, mines, (("x", "y", "lo"), ("y", "lo", "x"), ("lo", "x", "y"))):
            got = move(send, order[0])
            for at, name in enumerate(order[1:]):
                waits = () if at else (done,)
                if mine.ndim == 2:
                    send, mine = fold_flat(scalars, name, 8 >> at, mine, got, waits)
                else:
                    send, mine = fold(scalars, name, mine, got, waits)
                got = move(send, name)
            parts.append((mine, got))
        first = 3 * dn // 2
        send_1, send_2, mine_1, mine_2 = last_fold(scalars, parts, first)
        add = lambda mine, send: (mine.astype(F32) + move(send, "hi").astype(F32)).astype(BF)
        mine_1 = add(mine_1, send_1)
        around_1 = [mine_1] + along_rep(mine_1)
        mine_2 = add(mine_2, send_2)
        smalls = mine_2[first:].astype(F32)
        mine_2 = mine_2[:first]
        around_2 = [mine_2] + along_rep(mine_2)
        around = [jnp.concatenate([p, q]) for p, q in zip(around_1, around_2)]
        x, y = ri % 2, ri // 2
        flip = lambda bit, a, b: (jnp.where(bit == 1, b, a), jnp.where(bit == 1, a, b))
        a0, a1 = flip(x, around[0], around[1])
        a2, a3 = flip(x, around[2], around[3])
        a0, a2 = flip(y, a0, a2)
        a1, a3 = flip(y, a1, a3)
        final = jnp.stack([a0, a1, a2, a3]).astype(F32)
        g_att, g_up, g_down = final[:, :dn], final[:, dn:2 * dn], final[:, 2 * dn:].reshape(fn, d)
        smalls = smalls.reshape(SMALL, d)
    else:
        norms = butterfly(butterfly(norm_row, "fsdp", n), "rep", rep)[0, :rep * n]
        factor = jnp.minimum(1.0, jnp.mean(norms) / lax.dynamic_index_in_dim(norms, me, 0, keepdims=False)) / (rep * n)
        out, _ = output(scalars, block_input, par, ready, w, wd, act, (ctxa, ctxb))
        scale = lambda v: (v.astype(F32) * factor).astype(BF)
        shards = lambda v: v.reshape(v.shape[0], n, dn, d).swapaxes(0, 1).reshape(n, -1, d)
        pack = jnp.concatenate([scale(shards(dwa[0])), scale(shards(dwf[0])), scale(dwf[1].reshape(n, fn, d))], axis=1)
        mine = lax.psum_scatter(pack, "fsdp", scatter_dimension=0, tiled=True)[0]
        mine = lax.psum(mine, "rep").astype(F32)
        g_att = mine[:4 * dn].reshape(4, dn, d)
        g_up = mine[4 * dn:(4 + chunks) * dn].reshape(chunks, dn, d)
        g_down = mine[(4 + chunks) * dn:]
        smalls = lax.psum(scale(smalls), ("rep", "fsdp")).astype(F32)

    g_triple = jnp.concatenate([g_att[j, :, a * gw:(a + 1) * gw] for a in range(3) for j in range(GROUPS)], axis=1)
    g_upward = jnp.concatenate([g_up[j] for j in range(chunks)], axis=1)
    own = lambda v, width: lax.dynamic_slice_in_dim(v, fi * width, width, 0)
    g1, s1, g2, s2, bd = (own(smalls[i], dn) for i in range(5))
    b_triple = own(jnp.concatenate([smalls[5 + j, a * gw:(a + 1) * gw] for a in range(3) for j in range(GROUPS)]), 3 * dn)
    b_up = own(smalls[8:8 + chunks].reshape(-1), fn)
    return (out, gx, g1, s1, g2, s2, g_triple, b_triple, g_att[GROUPS], bd, g_upward, b_up, g_down, bd, norms)


def solution(mesh):
    rows = P(("rep", "fsdp"), None)
    vec, mat = P("fsdp"), P("fsdp", None)
    sizes = (mesh.shape["rep"], mesh.shape["fsdp"])
    return jax.shard_map(
        lambda *args: per_device(sizes, *args),
        mesh=mesh,
        in_specs=(rows, rows, P(("rep", "fsdp")), vec, vec, vec, vec, mat, vec, mat, vec, mat, vec, mat, vec),
        out_specs=(rows, rows, vec, vec, vec, vec, mat, vec, mat, vec, mat, vec, mat, vec, P()),
        check_vma=False,
    )
```

```python
import math
import numpy as np
import jax
import jax.numpy as jnp
from jax import lax
from jax.experimental import pallas as pl
from jax.experimental.pallas import tpu as pltpu
from jax.sharding import PartitionSpec as P

HEADS = 12
HEAD_DIM = 64
ROT = 16
EPS = 1e-05
MASKED = -1e30
BF = jnp.bfloat16
F32 = jnp.float32
GROUPS = 3
MIB = 1024 * 1024


def mm(a, b):
    return jnp.dot(a, b, preferred_element_type=F32)


def mm_rt(a, b):
    return lax.dot_general(a, b, (((1,), (1,)), ((), ())), preferred_element_type=F32)


def mm_lt(a, b):
    return lax.dot_general(a, b, (((0,), (0,)), ((), ())), preferred_element_type=F32)


def rotary_tables(rows, width):
    half = ROT // 2
    freq = np.exp(np.arange(half, dtype=np.float32) * np.float32(-2.0 * math.log(10000.0) / ROT))
    ang = np.arange(rows, dtype=np.float32)[:, None] * freq.astype(np.float32)[None, :]
    cos, sin = np.cos(ang), np.sin(ang)
    keep = np.ones((rows, HEAD_DIM), np.float32)
    up = np.zeros((rows, HEAD_DIM), np.float32)
    down = np.zeros((rows, HEAD_DIM), np.float32)
    keep[:, :half] = cos
    keep[:, half:ROT] = cos
    up[:, :half] = -sin
    down[:, half:ROT] = sin
    rep = width // HEAD_DIM
    return tuple(np.tile(t, (1, rep)).astype(np.float32) for t in (keep, up, down))


def norm_parts(values):
    centred = values - jnp.mean(values, axis=-1, keepdims=True)
    inverse = lax.rsqrt(jnp.mean(centred * centred, axis=-1, keepdims=True) + EPS)
    return centred * inverse, inverse


def norm_back(e, gain, normed, inverse):
    t = e * gain
    t_mean = jnp.mean(t, axis=-1, keepdims=True)
    cross = jnp.mean(t * normed, axis=-1, keepdims=True)
    return inverse * (t - t_mean - normed * cross)


SMALL = 16
BLOCK = 256
QKV_BIAS = 6
UP_BIAS = QKV_BIAS + GROUPS
VM = pl.BlockSpec(memory_space=pltpu.VMEM)
SM = pl.BlockSpec(memory_space=pltpu.SMEM)
ANY = pl.BlockSpec(memory_space=pl.ANY)


def block(i):
    return pl.ds(pl.multiple_of(i * BLOCK, BLOCK), BLOCK)


def params(mib):
    return pltpu.CompilerParams(vmem_limit_bytes=mib * MIB)


def valid_rows(i, seq):
    return (lax.broadcasted_iota(jnp.int32, (BLOCK, 1), 0) + i * BLOCK < seq).astype(F32)


def unpack_small(small, dn, d, vec_out):
    n = small.shape[0]
    gw = d // GROUPS
    line = lambda row, width: jnp.concatenate([small[s, row:row + 1, :width] for s in range(n)], axis=1)
    vec_out[...] = jnp.zeros_like(vec_out)
    for i in range(6):
        vec_out[i:i + 1, :] = line(i, dn)
    qkv = line(6, 3 * dn)
    for j in range(GROUPS):
        vec_out[QKV_BIAS + j:QKV_BIAS + j + 1, :] = jnp.concatenate([qkv[:, a * d + j * gw:a * d + (j + 1) * gw] for a in range(3)], axis=1)
    up = line(7, small.shape[2])
    for j in range(up.shape[1] // d):
        vec_out[UP_BIAS + j:UP_BIAS + j + 1, :] = up[:, j * d:(j + 1) * d]


def prepare_kernel(plan, waits, sc_ref, x_ref, g_ref, packed, up_ref, down_ref, *rest):
    n1, n1t, n2, n2t, gl, vec_out, token, pick, sems = rest[waits:]
    d = x_ref.shape[1]
    par_ref = vec_out
    if plan["on"]:
        dn, rep = plan["dn"], sc_ref[3]
        cut = [pltpu.make_async_copy(up_ref.at[:, pl.ds(pl.multiple_of(rep * d, 128), d)], pick.at[0], sems.at[0]),
               pltpu.make_async_copy(down_ref.at[pl.ds(pl.multiple_of(rep * dn, 16), dn)], pick.at[1], sems.at[1])]

        @pl.when(pl.program_id(0) == 0)
        def _():
            for c in cut:
                c.start()
            unpack_small(packed[0].astype(F32) + packed[1].astype(F32) + packed[2].astype(F32) + packed[3].astype(F32), dn, d, vec_out)

        @pl.when(pl.program_id(0) == pl.num_programs(0) - 1)
        def _():
            for c in cut:
                c.wait()

    else:
        vec_out[...] = packed[...]
    token[...] = jnp.zeros_like(token)
    normed, _ = norm_parts(x_ref[...].astype(F32))
    one = (normed * par_ref[0:1, :] + par_ref[1:2, :]).astype(BF)
    two = (normed * par_ref[2:3, :] + par_ref[3:4, :]).astype(BF)
    n1[...] = one
    n2[...] = two
    n1t[...] = one.astype(F32).T.astype(BF)
    n2t[...] = two.astype(F32).T.astype(BF)
    gl[...] = (g_ref[...].astype(F32) * valid_rows(pl.program_id(0), sc_ref[0])).astype(BF)


def prepare(plan, scalars, x, g, par, up, down, waits):
    rows, d = x.shape
    flat, turned = jax.ShapeDtypeStruct((rows, d), BF), jax.ShapeDtypeStruct((d, rows), BF)
    vecs = (16, d) if plan["on"] else par.shape
    by_rows, by_cols = pl.BlockSpec((BLOCK, d), lambda i: (i, 0)), pl.BlockSpec((d, BLOCK), lambda i: (0, i))
    return pl.pallas_call(
        lambda *refs: prepare_kernel(plan, len(waits), *refs),
        grid_spec=pl.GridSpec(grid=(rows // BLOCK,), in_specs=[SM, by_rows, by_rows, pl.BlockSpec(par.shape, lambda i: (0,) * par.ndim), ANY, ANY] + [ANY] * len(waits),
                              out_specs=[by_rows, by_cols, by_rows, by_cols, by_rows, pl.BlockSpec(vecs, lambda i: (0, 0)), pl.BlockSpec((1, 1), lambda i: (0, 0)), pl.BlockSpec((2, plan["dn"], d), lambda i: (0, 0, 0))],
                              scratch_shapes=[pltpu.SemaphoreType.DMA((2,))]),
        out_shape=[flat, turned, flat, turned, flat, jax.ShapeDtypeStruct(vecs, F32), jax.ShapeDtypeStruct((1, 1), F32),
                   jax.ShapeDtypeStruct((2, plan["dn"], d), BF)], compiler_params=params(60), name="prepare",
        cost_estimate=pl.CostEstimate(flops=40 * rows * d, bytes_accessed=14 * rows * d, transcendentals=rows),
    )(scalars, x, g, par, up, down, *waits)


def attn_kernel(plan, first, base, sc_ref, n1, gl, b3_ref, keep_ref, up_ref, down_ref, *rest):
    nw = plan["pieces"] if first else 2
    w_refs, rest = rest[:nw], rest[nw:]
    d3, ctx_low, sm_ref, token, rest = rest[0].at[0], rest[1].at[0], rest[2].at[0], rest[3], rest[4:]
    token[...] = jnp.zeros_like(token)
    rows, d = n1.shape
    gw = d // GROUPS
    qb = BLOCK
    nb = rows // qb
    seq = sc_ref[0]
    if first:
        w_out, rest = rest[0], rest[1:]
    q_s, k_s, v_s, dc_s, ctx, dq, dk, dv, qm, km, vm, dcm, pall, dall = rest[:14]

    if first:
        w, sems = rest[14:]
        if plan["on"]:
            z, core, rep = sc_ref[1], sc_ref[2], sc_ref[3]
            dn, nz, nr = plan["dn"], plan["nz"], plan["nr"]
            own, sib, near, sibs = w_refs[0], w_refs[1], w_refs[2:2 + nr], w_refs[2 + nr]
            place = lambda zz, cc: pl.ds(pl.multiple_of((zz * 2 + cc) * dn, 16), dn)
            pairs = []
            for m in range(nr):
                pairs.append((own.at[m], w.at[m, place(z, core)]))
                pairs.append((sib.at[m], w.at[m, place(z, 1 - core)]))
            for j in range(nr):
                for k in range(1, nz):
                    m, zz = rep ^ j, z ^ k
                    pairs.append((near[j].at[k - 1], w.at[m, place(zz, core)]))
                    pairs.append((sibs.at[j, k - 1], w.at[m, place(zz, 1 - core)]))
        else:
            pairs = [(w_refs[0].at[m], w.at[m]) for m in range(GROUPS + 1)]
        copies = [pltpu.make_async_copy(a, b, sems.at[i]) for i, (a, b) in enumerate(pairs)]
        for c in copies:
            c.start()
        for c in copies:
            c.wait()
        back = pltpu.make_async_copy(w, w_out, sems.at[len(pairs)])
        back.start()
        w3, wo = w.at[0], w.at[GROUPS, 0:gw]
    else:
        w3, wo = w_refs[0].at[0], w_refs[1].at[0]
    half = ROT // 2

    def tables(r):
        return tuple(jnp.concatenate([t[r, :]] * (gw // 128), axis=1) for t in (keep_ref, up_ref, down_ref))

    def project(i, c):
        r = block(i)
        t = mm(n1[r, :], w3[...]) + b3_ref[pl.ds(QKV_BIAS + base + pl.program_id(0), 1), :]
        keep, up, down = tables(r)
        for at, ref, scale in ((0, q_s, HEAD_DIM ** -0.5), (1, k_s, None)):
            v = t[:, at * gw:(at + 1) * gw]
            low = (v * keep + pltpu.roll(v, gw - half, 1) * up + pltpu.roll(v, half, 1) * down).astype(BF)
            ref[r, :] = low if scale is None else (low.astype(F32) * scale).astype(BF)
        v_s[r, :] = t[:, 2 * gw:].astype(BF)
        dc_s[r, :] = mm_rt(gl[r, :], wo[...]).astype(BF)
        return c
    lax.fori_loop(0, nb, project, 0, unroll=True)

    key_bias = jnp.where(lax.broadcasted_iota(jnp.int32, (1, rows), 1) < seq, 0.0, MASKED).astype(F32)
    causal = lax.broadcasted_iota(jnp.int32, (qb, qb), 1) <= lax.broadcasted_iota(jnp.int32, (qb, qb), 0)

    heads = gw // HEAD_DIM

    def head(h, c):
        lane = lax.broadcasted_iota(jnp.int32, (1, gw), 1) // HEAD_DIM
        mask = jnp.where(lane == h, 1.0, 0.0).astype(BF)
        for ref, out in ((q_s, qm), (k_s, km), (v_s, vm), (dc_s, dcm)):
            out[h] = ref[...] * mask
        for i in range(nb):
            lo, kl = i * qb, (i + 1) * qb
            s = mm_rt(qm[h, lo:kl, :], k_s[:kl, :]) + key_bias[:, :kl]
            diag = jnp.where(causal, s[:, lo:], MASKED)
            s = diag if i == 0 else jnp.concatenate([s[:, :lo], diag], axis=1)
            dp = mm_rt(dcm[h, lo:kl, :], v_s[:kl, :])
            e = jnp.exp(s - jnp.max(s, axis=1, keepdims=True))
            p = e * (1.0 / jnp.sum(e, axis=1, keepdims=True))
            pall[h, lo:kl, :kl] = p.astype(BF)
            inner = jnp.sum(p * dp, axis=1, keepdims=True)
            dall[h, lo:kl, :kl] = (p * (dp - inner)).astype(BF)
        return c
    lax.fori_loop(0, heads, head, 0, unroll=4)
    for i in range(nb):
        lo, kl = i * qb, (i + 1) * qb
        ctx[lo:kl, :] = sum(mm(pall[h, lo:kl, :kl], vm[h, :kl, :]) for h in range(heads))
        dq[lo:kl, :] = sum(mm(dall[h, lo:kl, :kl], km[h, :kl, :]) for h in range(heads))
        dv[lo:kl, :] = sum(mm_lt(pall[h, lo:, lo:kl], dcm[h, lo:, :]) for h in range(heads))
        dk[lo:kl, :] = sum(mm_lt(dall[h, lo:, lo:kl], qm[h, lo:, :]) for h in range(heads))

    def finish(i, total):
        r = block(i)
        keep, up, down = tables(r)
        parts = []
        for ref, scale in ((dq, HEAD_DIM ** -0.5), (dk, 1.0)):
            v = ref[r, :] * scale
            parts.append(v * keep - pltpu.roll(v, gw - half, 1) * up - pltpu.roll(v, half, 1) * down)
        low = jnp.concatenate(parts + [dv[r, :]], axis=1).astype(BF)
        d3[r, :] = low
        ctx_low[r, :] = ctx[r, :].astype(BF)
        return total + jnp.sum(low.astype(F32), axis=0, keepdims=True)
    db3 = lax.fori_loop(0, nb, finish, jnp.zeros((1, d), F32), unroll=True)
    sm_ref[...] = jnp.broadcast_to(db3, sm_ref.shape)
    if first:
        back.wait()


def attention(plan, groups, scalars, n1, gl, b3, tables, weights):
    rows, d = n1.shape
    gw = d // GROUPS
    first, count, base = groups[0] == 0, len(groups), groups[0]
    plan = dict(plan, pieces=len(weights))
    whole = lambda *shape: pl.BlockSpec(shape, lambda j: (0,) * len(shape))
    stacked = lambda *shape: pl.BlockSpec((1,) + shape, lambda j: (j,) + (0,) * len(shape))
    out_shape = [jax.ShapeDtypeStruct((count, rows, d), BF), jax.ShapeDtypeStruct((count, rows, gw), BF), jax.ShapeDtypeStruct((count, 8, d), F32), jax.ShapeDtypeStruct((1, 1), F32)]
    out_specs = [stacked(rows, d), stacked(rows, gw), stacked(8, d), whole(1, 1)]
    heads = gw // HEAD_DIM
    scratch = [pltpu.VMEM((rows, gw), BF)] * 4 + [pltpu.VMEM((rows, gw), F32)] * 4
    scratch += [pltpu.VMEM((heads, rows, gw), BF)] * 4 + [pltpu.VMEM((heads, rows, rows), BF)] * 2
    if first:
        out_shape.append(jax.ShapeDtypeStruct((GROUPS + 1, d, d), BF))
        out_specs.append(ANY)
        scratch += [pltpu.VMEM((GROUPS + 1, d, d), BF), pltpu.SemaphoreType.DMA((64,))]
        w_specs = [ANY] * len(weights)
    else:
        weights = [weights[0], weights[0]]
        w_specs = [pl.BlockSpec((1, d, d), lambda j: (base + j, 0, 0)), pl.BlockSpec((1, gw, d), lambda j: (GROUPS, base + j, 0))]
    flops = count * (2 * rows * d * (d + gw) + 12 * HEADS // GROUPS * rows * rows * HEAD_DIM)
    return pl.pallas_call(
        lambda *refs: attn_kernel(plan, first, base, *refs),
        grid_spec=pl.GridSpec(
            grid=(count,),
            in_specs=[SM, whole(rows, d), whole(rows, d), whole(*b3.shape)] + [whole(rows, 128)] * 3 + w_specs,
            out_specs=out_specs, scratch_shapes=scratch),
        out_shape=out_shape, compiler_params=params(56 if first else 60), name="attend_first" if first else "attend_rest",
        cost_estimate=pl.CostEstimate(flops=4 * flops, bytes_accessed=8_000_000, transcendentals=count * HEADS * rows * rows // GROUPS),
    )(scalars, n1, gl, b3, *tables, *weights)


def write_halves(value, tmp, keep_ref, send_ref, core, dn):
    tmp[...] = value.astype(BF)
    for z in range(keep_ref.shape[0]):
        mine = pl.ds(pl.multiple_of((2 * z + core) * dn, 16), dn)
        other = pl.ds(pl.multiple_of((2 * z + 1 - core) * dn, 16), dn)
        keep_ref[z, 0] = tmp[mine, :]
        send_ref[z, 0] = tmp[other, :]


def closing_kernel(plan, sc_ref, x_ref, gl, n1t, par_ref, w, d3a, d3b, ctxa, ctxb, sma, smb, *rest):
    nd = 2 if plan["on"] else 1
    dw_refs, rest = rest[:nd], rest[nd:]
    sm_ref, ff_ref, gf, tmp, x_s, gl_s, ctx_s, sems = rest
    step = pl.program_id(0)
    rows, d = x_ref.shape
    nb = rows // BLOCK
    late = [pltpu.make_async_copy(x_ref, x_s, sems.at[0]), pltpu.make_async_copy(gl, gl_s, sems.at[1]),
            pltpu.make_async_copy(ctxa, ctx_s.at[pl.ds(0, 1)], sems.at[2]), pltpu.make_async_copy(ctxb, ctx_s.at[pl.ds(1, GROUPS - 1)], sems.at[3])]

    @pl.when(step == 0)
    def _():
        for c in late:
            c.start()

    def store(dw):
        if plan["on"]:
            write_halves(dw, tmp, dw_refs[0], dw_refs[1], sc_ref[2], plan["dn"])
        else:
            dw_refs[0][0] = dw.astype(BF)
        return jnp.sum(dw * dw, axis=0, keepdims=True)

    def group(first, d3, db3):
        def body(i, c):
            r = block(i)
            part = mm_rt(d3[0, r, :], w[0])
            gf[r, :] = part if first else gf[r, :] + part
            return c
        lax.fori_loop(0, nb, body, 0, unroll=True)
        total = store(mm(n1t[...], d3[0])) + db3 * db3
        sm_ref[pl.ds(2 + step, 1), :] = db3
        sm_ref[5:6, :] = total if first else sm_ref[5:6, :] + total

    @pl.when(step == 0)
    def _():
        group(True, d3a, sma[0, 0:1, :])

    @pl.when(jnp.logical_and(step > 0, step < GROUPS))
    def _():
        group(False, d3b, smb[0, 0:1, :])

    @pl.when(step == GROUPS)
    def _():
        for c in late:
            c.wait()
        total = store(mm_lt(jnp.concatenate([ctx_s[g] for g in range(GROUPS)], axis=1), gl_s[...]))

        def back(i, c):
            r = block(i)
            normed, inverse = norm_parts(x_s[r, :].astype(F32))
            e = gf[r, :]
            ff_ref[r, :] = norm_back(e, par_ref[0:1, :], normed, inverse)
            return (c[0] + jnp.sum(e * normed, axis=0, keepdims=True), c[1] + jnp.sum(e, axis=0, keepdims=True))
        zero = jnp.zeros((1, d), F32)
        dgain, dshift = lax.fori_loop(0, nb, back, (zero, zero), unroll=True)
        sm_ref[0:1, :] = dgain
        sm_ref[1:2, :] = dshift
        sm_ref[5:6, :] += total + dgain * dgain + dshift * dshift


def closing(plan, scalars, x, gl, n1t, par, w, d3a, d3b, ctxa, ctxb, sma, smb):
    rows, d = x.shape
    gw = d // GROUPS
    whole = lambda *shape: pl.BlockSpec(shape, lambda j: (0,) * len(shape))
    later = lambda *shape: pl.BlockSpec((1,) + shape, lambda j: (jnp.clip(j - 1, 0, GROUPS - 2),) + (0,) * len(shape))
    if plan["on"]:
        nz, dn = plan["nz"], plan["dn"]
        dw_specs = [pl.BlockSpec((nz, 1, dn, d), lambda j: (0, j, 0, 0))] * 2
        dw_shapes = [jax.ShapeDtypeStruct((nz, GROUPS + 1, dn, d), BF)] * 2
    else:
        dw_specs = [pl.BlockSpec((1, d, d), lambda j: (j, 0, 0))]
        dw_shapes = [jax.ShapeDtypeStruct((GROUPS + 1, d, d), BF)]
    return pl.pallas_call(
        lambda *refs: closing_kernel(plan, *refs),
        grid_spec=pl.GridSpec(
            grid=(GROUPS + 1,),
            in_specs=[SM, ANY, ANY, whole(d, rows), whole(*par.shape),
                      pl.BlockSpec((1, d, d), lambda j: (jnp.minimum(j, GROUPS - 1), 0, 0)),
                      whole(1, rows, d), later(rows, d), ANY, ANY, whole(1, 8, d), later(8, d)],
            out_specs=dw_specs + [whole(8, d), whole(rows, d)],
            scratch_shapes=[pltpu.VMEM((rows, d), F32), pltpu.VMEM((d, d), BF), pltpu.VMEM((rows, d), BF), pltpu.VMEM((rows, d), BF),
                            pltpu.VMEM((GROUPS, rows, gw), BF), pltpu.SemaphoreType.DMA((4,))],
        ),
        out_shape=dw_shapes + [jax.ShapeDtypeStruct((8, d), F32), jax.ShapeDtypeStruct((rows, d), F32)],
        compiler_params=params(60), name="closing",
        cost_estimate=pl.CostEstimate(flops=4 * rows * d * 7 * d, bytes_accessed=8_000_000, transcendentals=rows),
    )(scalars, x, gl, n1t, par, w, d3a, d3b, ctxa, ctxb, sma, smb)


ERF_P = 0.3275911
ERF_A = (0.254829592, -0.284496736, 1.421413741, -1.453152027, 1.061405429)


def gelu_parts(u):
    z = jnp.abs(u) * (2.0 ** -0.5)
    t = 1.0 / (1.0 + ERF_P * z)
    bell = jnp.exp(-0.5 * (u * u))
    a1, a2, a3, a4, a5 = (0.5 * a for a in ERF_A)
    tail = ((((a5 * t + a4) * t + a3) * t + a2) * t + a1) * t * bell
    cdf = jnp.where(u >= 0.0, 1.0 - tail, tail)
    return u * cdf, cdf + u * bell * (1.0 / math.sqrt(2.0 * math.pi))


def ffn_kernel(plan, sc_ref, x_ref, gl, n2, n2t, par_ref, ff_ref, sm1_ref, *rest):
    nw = plan["pieces"]
    w_refs, rest = rest[:nw], rest[nw:]
    nd = 4 if plan["on"] else 2
    dw_refs, rest = rest[:nd], rest[nd:]
    sm_ref, norm_ref, act_ref, wd_ref, gx_ref = rest[:5]
    wu_s, wd_s, gs, gup, sq, tmp, x_s, ff_s, up_sems, down_sems, late_sems = rest[5:]
    late = [pltpu.make_async_copy(x_ref, x_s, late_sems.at[0]), pltpu.make_async_copy(ff_ref, ff_s, late_sems.at[1])]
    step = pl.program_id(0)
    last = pl.num_programs(0) - 1
    rows, d = x_ref.shape
    fc = d
    nb = rows // BLOCK

    @pl.when(step == 0)
    def _():
        if plan["on"]:
            z, core, rep = sc_ref[1], sc_ref[2], sc_ref[3]
            dn, nz, nr = plan["dn"], plan["nz"], plan["nr"]
            own_up, own_down, sib_up, sib_down = w_refs[:4]
            near, sibs = w_refs[4:4 + nr], w_refs[4 + nr]

            def up(src, m, zz, cc):
                dst = wu_s.at[m, pl.ds(pl.multiple_of((zz * 2 + cc) * dn, 16), dn)]
                pltpu.make_async_copy(src, dst, up_sems.at[m]).start()

            def down(src, b, zz, cc):
                dst = wd_s.at[zz, pl.ds(pl.multiple_of((cc * nr + b) * dn, 16), dn)]
                pltpu.make_async_copy(src, dst, down_sems.at[zz]).start()
            for m in range(nr):
                cols, part = pl.ds(m * d, d), pl.ds(m * dn, dn)
                up(own_up.at[:, cols], m, z, core)
                up(sib_up.at[:, cols], m, z, 1 - core)
                down(own_down.at[part], m, z, core)
                down(sib_down.at[part], m, z, 1 - core)
            for j in range(nr):
                for k in range(1, nz):
                    up(near[j].at[k - 1, 0], rep ^ j, z ^ k, core)
                    up(sibs.at[j, k - 1, 0], rep ^ j, z ^ k, 1 - core)
                    down(near[j].at[k - 1, 1], rep ^ j, z ^ k, core)
                    down(sibs.at[j, k - 1, 1], rep ^ j, z ^ k, 1 - core)
        else:
            for m in range(wu_s.shape[0]):
                pltpu.make_async_copy(w_refs[0].at[m], wu_s.at[m], up_sems.at[m]).start()
                pltpu.make_async_copy(w_refs[1].at[m], wd_s.at[m], down_sems.at[m]).start()
        for c in late:
            c.start()
        gs[...] = jnp.zeros_like(gs)
        sq[...] = jnp.zeros_like(sq)
        sm_ref[...] = jnp.zeros_like(sm_ref)

    pltpu.make_async_copy(wu_s.at[step], wu_s.at[step], up_sems.at[step]).wait()
    pltpu.make_async_copy(wd_s.at[step], wd_s.at[step], down_sems.at[step]).wait()
    wu, wd = wu_s.at[step], wd_s.at[step]
    wd_ref[0] = wd[...]

    def rows_step(i, dbu):
        r = block(i)
        u = mm(n2[r, :], wu[...]) + par_ref[pl.ds(UP_BIAS + step, 1), :]
        da = mm_rt(gl[r, :], wd[...])
        a, slope = gelu_parts(u)
        act_ref[0, r, :] = a.astype(BF)
        gu = (da * slope).astype(BF)
        gup[r, :] = gu
        gs[r, :] += mm_rt(gu, wu[...])
        return dbu + jnp.sum(gu.astype(F32), axis=0, keepdims=True)
    dbu = lax.fori_loop(0, nb, rows_step, jnp.zeros((1, fc), F32), unroll=True)
    sm_ref[pl.ds(8 + step, 1), :] = dbu

    dwu = mm(n2t[...], gup[...])
    total = jnp.sum(dwu * dwu, axis=0, keepdims=True) + dbu * dbu
    if plan["on"]:
        write_halves(dwu, tmp, dw_refs[0], dw_refs[1], sc_ref[2], plan["dn"])
    else:
        dw_refs[0][0] = dwu.astype(BF)
    dwd = mm_lt(act_ref[0], gl[...])
    total += jnp.sum(dwd * dwd, axis=0, keepdims=True)
    if plan["on"]:
        tmp[...] = dwd.astype(BF)
        core, dn, nr = sc_ref[2], plan["dn"], plan["nr"]
        for m in range(nr):
            dw_refs[2][0, m] = tmp[pl.ds(pl.multiple_of((core * nr + m) * dn, 16), dn), :]
            dw_refs[3][0, m] = tmp[pl.ds(pl.multiple_of(((1 - core) * nr + m) * dn, 16), dn), :]
    else:
        dw_refs[1][0] = dwd.astype(BF)
    sq[...] += total

    @pl.when(step == last)
    def _():
        for c in late:
            c.wait()

        def back(i, c):
            r = block(i)
            normed, inverse = norm_parts(x_s[r, :].astype(F32))
            e = gs[r, :]
            grad_rows = gl[r, :].astype(F32)
            gx_ref[r, :] = (grad_rows + ff_s[r, :] + norm_back(e, par_ref[2:3, :], normed, inverse)).astype(BF)
            return (c[0] + jnp.sum(e * normed, axis=0, keepdims=True), c[1] + jnp.sum(e, axis=0, keepdims=True),
                    c[2] + jnp.sum(grad_rows, axis=0, keepdims=True))
        zero = jnp.zeros((1, d), F32)
        dgain, dshift, dbd = lax.fori_loop(0, nb, back, (zero, zero, zero), unroll=True)
        sm_ref[0:2, :] = sm1_ref[0:2, :]
        sm_ref[2:3, :] = dgain
        sm_ref[3:4, :] = dshift
        sm_ref[4:5, :] = dbd
        sm_ref[5:8, :] = sm1_ref[2:5, :]
        final = sq[...] + sm1_ref[5:6, :] + dgain * dgain + dshift * dshift + 2.0 * dbd * dbd
        own = jnp.sqrt(jnp.sum(final, axis=1, keepdims=True))
        here = lax.broadcasted_iota(jnp.int32, norm_ref.shape, 1) == sc_ref[4]
        norm_ref[...] = jnp.where(here, own, 0.0)


def ffn(plan, chunks, scalars, x, gl, n2, n2t, par, ff, sm1, weights, norm_width):
    rows, d = x.shape
    plan = dict(plan, pieces=len(weights))
    whole = lambda *shape: pl.BlockSpec(shape, lambda j: (0,) * len(shape))
    if plan["on"]:
        nz, dn, nr = plan["nz"], plan["dn"], plan["nr"]
        dw_specs = [pl.BlockSpec((nz, 1, dn, d), lambda j: (0, j, 0, 0))] * 2 + [pl.BlockSpec((1, nr, dn, d), lambda j: (j, 0, 0, 0))] * 2
        dw_shapes = [jax.ShapeDtypeStruct((nz, chunks, dn, d), BF)] * 2 + [jax.ShapeDtypeStruct((nz, nr, dn, d), BF)] * 2
    else:
        dw_specs = [pl.BlockSpec((1, d, d), lambda j: (j, 0, 0))] * 2
        dw_shapes = [jax.ShapeDtypeStruct((chunks, d, d), BF)] * 2
    return pl.pallas_call(
        lambda *refs: ffn_kernel(plan, *refs),
        grid_spec=pl.GridSpec(
            grid=(chunks,),
            in_specs=[SM, ANY, whole(rows, d), whole(rows, d), whole(d, rows), whole(*par.shape), ANY, whole(8, d)] + [ANY] * len(weights),
            out_specs=dw_specs + [whole(SMALL, d), whole(1, norm_width), pl.BlockSpec((1, rows, d), lambda j: (j, 0, 0)),
                                  pl.BlockSpec((1, d, d), lambda j: (j, 0, 0)), whole(rows, d)],
            scratch_shapes=[
                pltpu.VMEM((chunks, d, d), BF), pltpu.VMEM((chunks, d, d), BF), pltpu.VMEM((rows, d), F32), pltpu.VMEM((rows, d), BF),
                pltpu.VMEM((1, d), F32), pltpu.VMEM((d, d), BF), pltpu.VMEM((rows, d), BF), pltpu.VMEM((rows, d), F32),
                pltpu.SemaphoreType.DMA((chunks,)), pltpu.SemaphoreType.DMA((chunks,)), pltpu.SemaphoreType.DMA((2,)),
            ],
        ),
        out_shape=dw_shapes + [
            jax.ShapeDtypeStruct((SMALL, d), F32), jax.ShapeDtypeStruct((1, norm_width), F32),
            jax.ShapeDtypeStruct((chunks, rows, d), BF), jax.ShapeDtypeStruct((chunks, d, d), BF), jax.ShapeDtypeStruct((rows, d), BF),
        ],
        compiler_params=params(60), name="feedforward",
        cost_estimate=pl.CostEstimate(flops=2 * 5 * rows * d * d * chunks * 2, bytes_accessed=40_000_000, transcendentals=rows * d * chunks),
    )(scalars, x, gl, n2, n2t, par, ff, sm1, *weights)


def output_kernel(sc_ref, x_ref, par_ref, token, wo, wd, act, *rest):
    ctxs, out_ref, done = rest[:2], rest[2], rest[3]
    done[...] = jnp.zeros_like(done)
    d = x_ref.shape[1]
    gw = d // GROUPS
    total = x_ref[...].astype(F32) + par_ref[4:5, :] + par_ref[5:6, :]
    for g in range(GROUPS):
        ctx = ctxs[0][0] if g == 0 else ctxs[1][g - 1]
        total += mm(ctx, wo[0, g * gw:(g + 1) * gw, :])
    for j in range(wd.shape[0]):
        total += mm(act[j], wd[j])
    out_ref[...] = (total * valid_rows(pl.program_id(0), sc_ref[0])).astype(BF)


def output(scalars, x, par, token, w, wd, act, ctxs):
    rows, d = x.shape
    gw = d // GROUPS
    chunks = wd.shape[0]
    return pl.pallas_call(
        output_kernel,
        grid_spec=pl.GridSpec(
            grid=(rows // BLOCK,),
            in_specs=[SM, pl.BlockSpec((BLOCK, d), lambda i: (i, 0)), pl.BlockSpec(par.shape, lambda i: (0, 0)), pl.BlockSpec(token.shape, lambda i: (0, 0)),
                      pl.BlockSpec((1, d, d), lambda i: (GROUPS, 0, 0)), pl.BlockSpec((chunks, d, d), lambda i: (0, 0, 0)),
                      pl.BlockSpec((chunks, BLOCK, d), lambda i: (0, i, 0))] + [pl.BlockSpec((1, BLOCK, gw), lambda i: (0, i, 0)), pl.BlockSpec((GROUPS - 1, BLOCK, gw), lambda i: (0, i, 0))],
            out_specs=[pl.BlockSpec((BLOCK, d), lambda i: (i, 0)), pl.BlockSpec((1, 128), lambda i: (0, 0))],
        ),
        out_shape=[jax.ShapeDtypeStruct((rows, d), BF), jax.ShapeDtypeStruct((1, 128), F32)],
        compiler_params=params(28), name="output",
        cost_estimate=pl.CostEstimate(flops=2 * rows * d * d * (chunks + 1), bytes_accessed=18_000_000, transcendentals=0),
    )(scalars, x, par, token, w, wd, act, *ctxs)


def spread(rows_ref, lane):
    norms = rows_ref
    at = lax.broadcasted_iota(jnp.int32, norms.shape, 1)
    own = jnp.sum(jnp.where(at == lane, norms, 0.0), axis=1, keepdims=True)
    return own


def mix_kernel(seqs, sending, sc_ref, r0, r1, sm, smg, dk, dg, uk, ug, ak, ag, token, d_ref, u_ref, a_ref, norm_out, d_in, u_in, a_in, in_sems, *rest):
    ins = (d_in, u_in, a_in)
    flip = 1 if sending else 0
    xb, yb, lob = flip ^ (sc_ref[3] % 2), flip ^ (sc_ref[3] // 2), flip ^ (sc_ref[1] % 2)
    dn = dk.shape[4]
    d_out, u_out, a_out, out_sems = rest if sending else (d_ref, u_ref, a_ref, None)
    wanted = ([v.at[:, lob] for v in (dk, dg)], [v.at[:, yb] for v in (uk, ug)], [v.at[:, :, xb] for v in (ak, ag)])
    reads = [[pltpu.make_async_copy(src, dst.at[t], in_sems.at[2 * p + t]) for t, src in enumerate(srcs)] for p, (srcs, dst) in enumerate(zip(wanted, ins))]
    for pair in reads:
        for c in pair:
            c.start()
    norms = r0[...] + r1[...]
    norm_out[...] = norms
    mean = jnp.sum(norms, axis=1, keepdims=True) * (1.0 / seqs)
    me = sc_ref[4]
    factor = jnp.minimum(1.0, mean / spread(norms, me)) * (1.0 / seqs)
    other = jnp.minimum(1.0, mean / spread(norms, me ^ 1)) * (1.0 / seqs)
    factor, other = factor[0, 0], other[0, 0]
    mixed = lambda k, g: (k.astype(F32) * factor + g.astype(F32) * other).astype(BF)
    d_out[8 * dn:, :] = mixed(sm[...], smg[...])
    writes = []
    for p, pair in enumerate(reads):
        for c in pair:
            c.wait()
        for i in range(4):
            for t in range(2):
                if p == 0:
                    at = (2 * i + t) * dn
                    d_out[at:at + dn, :] = mixed(d_in[0, i // 2, i % 2, t], d_in[1, i // 2, i % 2, t])
                elif p == 1:
                    u_out[i, 0, t] = mixed(u_in[0, i, t], u_in[1, i, t])
                else:
                    a_out[i, t, 0] = mixed(a_in[0, i, t], a_in[1, i, t])
        if sending:
            src, dst = ((d_out, d_ref), (u_out, u_ref), (a_out, a_ref))[p]
            writes.append(pltpu.make_async_copy(src, dst, out_sems.at[p]))
            writes[-1].start()
    for c in writes:
        c.wait()


def mix(seqs, sending, scalars, norm_rows, halves, smalls, token):
    dn, d = halves[0].shape[2:]
    ak, ag, uk, ug = (v.reshape(4, 2, 2, dn, d) for v in halves[:4])
    dk, dg = (v.reshape(2, 2, 2, 2, dn, d) for v in halves[4:])
    width = norm_rows[0].shape[1]
    shapes = [(8 * dn + SMALL, d), (4, 1, 2, dn, d), (4, 2, 1, dn, d)]
    scratch = [pltpu.VMEM((2, 2, 2, 2, dn, d), BF), pltpu.VMEM((2, 4, 2, dn, d), BF), pltpu.VMEM((2, 4, 2, dn, d), BF), pltpu.SemaphoreType.DMA((6,))]
    if sending:
        scratch += [pltpu.VMEM(s, BF) for s in shapes] + [pltpu.SemaphoreType.DMA((3,))]
    dd, u, a, norms = pl.pallas_call(
        lambda *refs: mix_kernel(seqs, sending, *refs),
        in_specs=[SM] + [VM] * 4 + [ANY] * 7, out_specs=[ANY if sending else VM] * 3 + [VM],
        out_shape=[jax.ShapeDtypeStruct(s, BF) for s in shapes] + [jax.ShapeDtypeStruct((1, width), F32)],
        scratch_shapes=scratch, compiler_params=params(60 if sending else 54), name="mix_send" if sending else "mix_keep",
        cost_estimate=pl.CostEstimate(flops=16_000_000, bytes_accessed=10_600_000, transcendentals=0),
    )(scalars, *norm_rows, *smalls, dk, dg, uk, ug, ak, ag, token)
    return a.reshape(2, 2, 2, 1, dn, d), u.reshape(2, 2, 1, 2, dn, d), dd, norms


def fold_flat_kernel(name, blocks, sc_ref, mine, got, *rest):
    send, keep = rest[-2:]
    dn = send.shape[0] - SMALL
    dn = dn // (blocks // 2)
    add = lambda a, b: (a.astype(F32) + b.astype(F32)).astype(BF)
    bit = side(name, sc_ref, 0)
    for out, which in ((send, 1 ^ bit), (keep, bit)):
        for i in range(blocks // 2):
            rows = pl.ds(pl.multiple_of((2 * i + which) * dn, 16), dn)
            out[i * dn:(i + 1) * dn, :] = add(mine[rows, :], got[rows, :])
        out[blocks // 2 * dn:, :] = add(mine[blocks * dn:, :], got[blocks * dn:, :])


def fold_flat(scalars, name, blocks, mine, got, waits=()):
    total, d = mine.shape
    half = jax.ShapeDtypeStruct(((total - SMALL) // 2 + SMALL, d), BF)
    return pl.pallas_call(
        lambda *refs: fold_flat_kernel(name, blocks, *refs),
        in_specs=[SM, VM, VM] + [ANY] * len(waits), out_specs=[VM, VM], out_shape=[half, half],
        compiler_params=params(16), name="fold_flat_" + name,
        cost_estimate=pl.CostEstimate(flops=mine.size, bytes_accessed=6 * mine.size, transcendentals=0),
    )(scalars, mine, got, *waits)


AXES = dict(hi=0, lo=1, y=2, x=3)


def side(name, sc, flip):
    bit = {"hi": sc[1] // 2, "lo": sc[1] % 2, "y": sc[3] // 2, "x": sc[3] % 2}[name]
    return flip ^ bit


def fold_kernel(sc_ref, ms, gs, mk, gk, *rest):
    send, keep = rest[-2:]
    d = ms.shape[-1]
    add = lambda a, b, out: (a[...].reshape(-1, d).astype(F32) + b[...].reshape(-1, d).astype(F32)).astype(BF).reshape(out.shape)
    send[...] = add(ms, gs, send)
    keep[...] = add(mk, gk, keep)


def fold(scalars, name, mine, got, waits=()):
    axis = AXES[name]
    shape = mine.shape
    blk = (1,) + tuple(1 if i == axis else s for i, s in enumerate(shape) if i > 0)
    spec = lambda flip: pl.BlockSpec(blk, lambda i, sc: (i,) + tuple(side(name, sc, flip) if k == axis else 0 for k in range(1, 6)))
    out = pl.BlockSpec(blk, lambda i, sc: (i, 0, 0, 0, 0, 0))
    half = jax.ShapeDtypeStruct((shape[0],) + blk[1:], BF)
    return pl.pallas_call(
        fold_kernel,
        grid_spec=pltpu.PrefetchScalarGridSpec(num_scalar_prefetch=1, grid=(shape[0],), in_specs=[spec(1), spec(1), spec(0), spec(0)] + [ANY] * len(waits), out_specs=[out, out]),
        out_shape=[half, half], compiler_params=params(16), name="fold_" + name,
        cost_estimate=pl.CostEstimate(flops=mine.size, bytes_accessed=6 * mine.size, transcendentals=0),
    )(scalars, mine, got, mine, got, *waits)


def last_fold_kernel(sc_ref, am, ag, um, ug, dm, dg, send1, send2, keep1, keep2):
    dn = am.shape[4]
    first = send1.shape[0]
    add = lambda a, b: (a.astype(F32) + b.astype(F32)).astype(BF)
    bit = side("hi", sc_ref, 0)
    small = add(dm[2 * dn:, :], dg[2 * dn:, :])
    for out1, out2, which in ((send1, send2, 1 ^ bit), (keep1, keep2, bit)):
        at = 0

        def put(low):
            nonlocal at
            rows = low.shape[0]
            split = min(max(first - at, 0), rows)
            if split > 0:
                out1[at:at + split, :] = low[:split]
            if split < rows:
                out2[at + split - first:at + rows - first, :] = low[split:]
            at += rows
        put(add(am[which, 0, 0, 0], ag[which, 0, 0, 0]))
        put(add(um[which, 0, 0, 0], ug[which, 0, 0, 0]))
        rows = pl.ds(pl.multiple_of(which * dn, 16), dn)
        put(add(dm[rows, :], dg[rows, :]))
        put(small)


def last_fold(scalars, parts, first):
    dn, d = parts[0][0].shape[4:]
    total = 3 * dn + SMALL
    half = [jax.ShapeDtypeStruct((s, d), BF) for s in (first, total - first)]
    return pl.pallas_call(
        last_fold_kernel, in_specs=[SM] + [VM] * 6, out_specs=[VM] * 4, out_shape=half + half,
        compiler_params=params(16), name="last_fold",
        cost_estimate=pl.CostEstimate(flops=2 * total * d, bytes_accessed=12 * total * d, transcendentals=0),
    )(scalars, *[v for pair in parts for v in pair])


def xor_permute(value, axis, size, bit):
    return lax.ppermute(value, axis, [(i, i ^ bit) for i in range(size)])


def butterfly(value, axis, size):
    if size & (size - 1):
        return lax.psum(value, axis)
    bit = 1
    while bit < size:
        value = value + xor_permute(value, axis, size, bit)
        bit *= 2
    return value


def after(value, other):
    return value + other[(slice(0, 1),) * other.ndim].reshape((1,) * value.ndim).astype(value.dtype) * 0


def per_device(sizes, block_input, cotangent, lengths, first_gain, first_shift, second_gain, second_shift, triple_weight, triple_bias,
               output_weight, output_bias, upward_weight, upward_bias, downward_weight, downward_bias):
    rep, n = sizes
    rows, d = block_input.shape
    dn, fn = first_gain.shape[0], upward_bias.shape[0]
    gw = d // GROUPS
    chunks = fn * n // d
    nz = n // 2
    plan = dict(on=rep == 4 and n == 8 and dn % 16 == 0 and chunks == nz == rep, dn=dn, nz=nz, nr=rep)
    ri, fi = lax.axis_index("rep"), lax.axis_index("fsdp")
    z, core = fi // 2, fi % 2
    me = ri * n + fi
    scalars = jnp.stack([lengths[0], z, core, ri, me]).astype(jnp.int32)
    group_cols = lambda v, j: jnp.concatenate([v[:, a * d + j * gw:a * d + (j + 1) * gw] for a in range(3)], axis=1)
    mats = jnp.stack([group_cols(triple_weight, j) for j in range(GROUPS)] + [output_weight])
    small = [first_gain, first_shift, second_gain, second_shift, output_bias, downward_bias, triple_bias, upward_bias]
    wide_row = max(v.shape[0] for v in small)
    low = jnp.asarray(-jnp.inf, BF)
    small = [lax.pad(v.reshape(1, -1), low, ((i, 7 - i, 0), (0, wide_row - v.shape[0], 0))) for i, v in enumerate(small)]
    while len(small) > 1:
        small = [jnp.maximum(a, b) for a, b in zip(small[::2], small[1::2])]
    small = jnp.maximum(small[0], jnp.asarray(-1e4, BF))
    small = jnp.where(jnp.arange(n)[:, None, None] == fi, small[None], 0.0).astype(BF)

    along_z = lambda v: [xor_permute(v, "fsdp", n, 2 * k) for k in range(1, nz)]
    along_rep = lambda v: [xor_permute(v, "rep", rep, j) for j in range(1, rep)]
    to_core = lambda v: xor_permute(v, "fsdp", n, 1)

    def unpack(small):
        small = small.astype(F32)
        par = small[:, :6, :dn].swapaxes(0, 1).reshape(6, d)
        bias_t = small[:, 6, :3 * dn].reshape(1, 3 * d)
        vecs = jnp.concatenate([par] + [group_cols(bias_t, j) for j in range(GROUPS)] + [small[:, 7, :fn].reshape(chunks, d)])
        return jnp.pad(vecs, ((0, -vecs.shape[0] % 8), (0, 0)))

    if plan["on"]:
        quarter = lax.dynamic_index_in_dim(mats, ri, 0, keepdims=False)
        small = small + to_core(small)
        far = along_z(quarter)
        small = jnp.stack([small] + along_z(small))
        sib_own = to_core(mats)
        wide_own = [upward_weight, downward_weight, to_core(upward_weight), to_core(downward_weight)]
        n1, n1t, n2, n2t, gl, par, ready, pick = prepare(plan, scalars, block_input, cotangent, small, upward_weight, downward_weight, [sib_own] + wide_own[2:])
        far = jnp.stack(far)
        near = [far] + along_rep(far)
    else:
        small = butterfly(small, "fsdp", n)
        weights = [lax.all_gather(mats, "fsdp", axis=1, tiled=True)]
        n1, n1t, n2, n2t, gl, par, ready, _ = prepare(plan, scalars, block_input, cotangent, unpack(small), upward_weight, downward_weight, [])
    tables = [jnp.asarray(t) for t in rotary_tables(rows, 128)]

    if plan["on"]:
        wide_far = jnp.stack(along_z(pick))
        weights = [mats, sib_own] + near + [to_core(jnp.stack(near) + ready[0, 0].astype(BF))]
    d3a, ctxa, sma, token_a, w = attention(plan, (0,), scalars, n1, gl, par, tables, weights)
    if plan["on"]:
        wide_far = wide_far + token_a[0, 0].astype(BF)
        wide_near = [wide_far] + along_rep(wide_far)
    d3b, ctxb, smb, token_b = attention(plan, (1, 2), scalars, n1, gl, par, tables, [w])
    if plan["on"]:
        wide_sibs = to_core(jnp.stack(wide_near) + token_b[0, 0].astype(BF))
        wide_weights = wide_own + wide_near + [wide_sibs]
    else:
        up = lax.all_gather(upward_weight, "fsdp", axis=0, tiled=True)
        down = lax.all_gather(downward_weight, "fsdp", axis=0, tiled=True)
        wide_weights = [jnp.stack([up[:, j * d:(j + 1) * d] for j in range(chunks)]), down.reshape(chunks, d, d)]
    *dwa, sm1, ff = closing(plan, scalars, block_input, gl, n1t, par, w, d3a, d3b, ctxa, ctxb, sma, smb)
    width = -(-rep * n // 128) * 128
    *dwf, smalls, norm_row, act, wd, gx = ffn(plan, chunks, scalars, block_input, gl, n2, n2t, par, ff, sm1, wide_weights, width)

    if plan["on"]:
        steps = dict(x=("rep", rep, 1), y=("rep", rep, 2), lo=("fsdp", n, 2), hi=("fsdp", n, 4))
        move = lambda v, name: xor_permute(v, *steps[name])
        a, b, c = along_z(norm_row)
        norm_row = (norm_row + a) + (b + c)
        a, b, c = along_rep(norm_row)
        norm_row = (norm_row + a) + (b + c)
        norm_rows = (norm_row, to_core(norm_row))
        halves = []
        for keep, send in ((dwa[0], dwa[1]), (dwf[0], dwf[1]), (dwf[2], dwf[3])):
            halves += [keep, to_core(send)]
        pair = (smalls, to_core(smalls))
        *sends, norm_row = mix(rep * n, True, scalars, norm_rows, halves, pair, ready)
        norms = norm_row[0, :rep * n]
        *mines, token = mix(rep * n, False, scalars, norm_rows, halves, pair, norm_row)
        out, done = output(scalars, block_input, par, token, w, wd, act, (ctxa, ctxb))
        parts = []
        for send, mine, order in zip(sends, mines, (("x", "y", "lo"), ("y", "lo", "x"), ("lo", "x", "y"))):
            got = move(send, order[0])
            for at, name in enumerate(order[1:]):
                waits = () if at else (done,)
                if mine.ndim == 2:
                    send, mine = fold_flat(scalars, name, 8 >> at, mine, got, waits)
                else:
                    send, mine = fold(scalars, name, mine, got, waits)
                got = move(send, name)
            parts.append((mine, got))
        first = 3 * dn // 2
        send_1, send_2, mine_1, mine_2 = last_fold(scalars, parts, first)
        add = lambda mine, send: (mine.astype(F32) + move(send, "hi").astype(F32)).astype(BF)
        mine_1 = add(mine_1, send_1)
        around_1 = [mine_1] + along_rep(mine_1)
        mine_2 = add(mine_2, send_2)
        smalls = mine_2[first:].astype(F32)
        mine_2 = mine_2[:first]
        around_2 = [mine_2] + along_rep(mine_2)
        around = [jnp.concatenate([p, q]) for p, q in zip(around_1, around_2)]
        x, y = ri % 2, ri // 2
        flip = lambda bit, a, b: (jnp.where(bit == 1, b, a), jnp.where(bit == 1, a, b))
        a0, a1 = flip(x, around[0], around[1])
        a2, a3 = flip(x, around[2], around[3])
        a0, a2 = flip(y, a0, a2)
        a1, a3 = flip(y, a1, a3)
        final = jnp.stack([a0, a1, a2, a3]).astype(F32)
        g_att, g_up, g_down = final[:, :dn], final[:, dn:2 * dn], final[:, 2 * dn:].reshape(fn, d)
        smalls = smalls.reshape(SMALL, d)
    else:
        norms = butterfly(butterfly(norm_row, "fsdp", n), "rep", rep)[0, :rep * n]
        factor = jnp.minimum(1.0, jnp.mean(norms) / lax.dynamic_index_in_dim(norms, me, 0, keepdims=False)) / (rep * n)
        out, _ = output(scalars, block_input, par, ready, w, wd, act, (ctxa, ctxb))
        scale = lambda v: (v.astype(F32) * factor).astype(BF)
        shards = lambda v: v.reshape(v.shape[0], n, dn, d).swapaxes(0, 1).reshape(n, -1, d)
        pack = jnp.concatenate([scale(shards(dwa[0])), scale(shards(dwf[0])), scale(dwf[1].reshape(n, fn, d))], axis=1)
        mine = lax.psum_scatter(pack, "fsdp", scatter_dimension=0, tiled=True)[0]
        mine = lax.psum(mine, "rep").astype(F32)
        g_att = mine[:4 * dn].reshape(4, dn, d)
        g_up = mine[4 * dn:(4 + chunks) * dn].reshape(chunks, dn, d)
        g_down = mine[(4 + chunks) * dn:]
        smalls = lax.psum(scale(smalls), ("rep", "fsdp")).astype(F32)

    g_triple = jnp.concatenate([g_att[j, :, a * gw:(a + 1) * gw] for a in range(3) for j in range(GROUPS)], axis=1)
    g_upward = jnp.concatenate([g_up[j] for j in range(chunks)], axis=1)
    own = lambda v, width: lax.dynamic_slice_in_dim(v, fi * width, width, 0)
    g1, s1, g2, s2, bd = (own(smalls[i], dn) for i in range(5))
    b_triple = own(jnp.concatenate([smalls[5 + j, a * gw:(a + 1) * gw] for a in range(3) for j in range(GROUPS)]), 3 * dn)
    b_up = own(smalls[8:8 + chunks].reshape(-1), fn)
    return (out, gx, g1, s1, g2, s2, g_triple, b_triple, g_att[GROUPS], bd, g_upward, b_up, g_down, bd, norms)


def solution(mesh):
    rows = P(("rep", "fsdp"), None)
    vec, mat = P("fsdp"), P("fsdp", None)
    sizes = (mesh.shape["rep"], mesh.shape["fsdp"])
    return jax.shard_map(
        lambda *args: per_device(sizes, *args),
        mesh=mesh,
        in_specs=(rows, rows, P(("rep", "fsdp")), vec, vec, vec, vec, mat, vec, mat, vec, mat, vec, mat, vec),
        out_specs=(rows, rows, vec, vec, vec, vec, mat, vec, mat, vec, mat, vec, mat, vec, P()),
        check_vma=False,
    )
```
